128 devices in a mesh: batch: 8 (over z, core), seq: 16 (over x, y).
Axes of the slice: x: 4, y: 4, z: 4, core: 2. Of those that a mesh axis runs over, the one named last changes fastest.
Arguments:
- tokens: bfloat16 [16384, 2048], P(('batch', 'seq')), may hold values from -6 to 6
- lengths: int32 [8, 3], P('batch'), may hold values from 1 to 2046, as said below
- attn_gain: bfloat16 [2048], P(('batch', 'seq')), may hold values from 0.5 to 1.5
- w_query: bfloat16 [2048, 2048], P(('batch', 'seq')), may hold values from -0.125 to 0.125
- w_key: bfloat16 [2048, 256], P(('batch', 'seq')), may hold values from -0.125 to 0.125
- w_value: bfloat16 [2048, 256], P(('batch', 'seq')), may hold values from -0.125 to 0.125
- w_out: bfloat16 [2048, 2048], P(('batch', 'seq')), may hold values from -2 to 2
- mlp_gain: bfloat16 [2048], P(('batch', 'seq')), may hold values from 0.5 to 1.5
- w_gate: bfloat16 [2048, 5632], P(('batch', 'seq')), may hold values from -0.125 to 0.125
- w_up: bfloat16 [2048, 5632], P(('batch', 'seq')), may hold values from -0.125 to 0.125
- w_down: bfloat16 [5632, 2048], P(('batch', 'seq')), may hold values from -0.078125 to 0.078125
- cotangent: bfloat16 [16384, 2048], P(('batch', 'seq')), may hold values from -6 to 6
Outputs:
- output: bfloat16 [16384, 2048], P(('batch', 'seq'))
- grad_tokens: float32 [16384, 2048], P(('batch', 'seq'))
- grad_attn_gain: float32 [2048], P(('batch', 'seq'))
- grad_query: float32 [2048, 2048], P(('batch', 'seq'))
- grad_key: float32 [2048, 256], P(('batch', 'seq'))
- grad_value: float32 [2048, 256], P(('batch', 'seq'))
- grad_out: float32 [2048, 2048], P(('batch', 'seq'))
- grad_mlp_gain: float32 [2048], P(('batch', 'seq'))
- grad_gate: float32 [2048, 5632], P(('batch', 'seq'))
- grad_up: float32 [2048, 5632], P(('batch', 'seq'))
- grad_down: float32 [5632, 2048], P(('batch', 'seq'))
The draws below stay inside these ranges and needn't reach their ends.
Inputs may be any that keep to these rules, and one draw needn't show every extreme that they name: Row g lists in order the lengths of the three documents packed into the 2048 tokens of group g; they sum to 2048; the first and the last are shorter than 128.
All inputs are finite; a program needn't handle non-finite values.
Results may differ from the reference program's by a relative error of at most 0.015.
Values may be sent and summed in bfloat16 or wider, within the bound.
A program may use at most 448 MiB of HBM per device.

```python
import math
import jax
import jax.numpy as jnp
from jax import lax

D = 2048
FF = 5632
HEADS = 32
KV_HEADS = 4
HEAD_DIM = 64
TOK_DEV = 128
SEQ = 2048
GROUPS = 8
TOKENS = 16384


def draw_lengths(key, part):
    key = jax.random.fold_in(key, 7)
    head_key, tail_key = jax.random.split(key)
    leading = jax.random.randint(head_key, (GROUPS,), 1, TOK_DEV)
    trailing = jax.random.randint(tail_key, (GROUPS,), 1, TOK_DEV)
    first_group = jnp.arange(GROUPS) == 0
    leading = jnp.where(first_group, 1, leading)
    trailing = jnp.where(first_group, 1, trailing)
    middle = SEQ - leading - trailing
    return jnp.stack([leading, middle, trailing], axis=1).astype(jnp.int32)


def block_levels(own_key, extent, cuts, least, top_value):
    def one(axis_at, blocks):
        steps = jax.random.uniform(jax.random.fold_in(jax.random.fold_in(own_key, 6), axis_at), (blocks,), jnp.float32, least / len(cuts), top_value / len(cuts))
        return jnp.repeat(jnp.exp(steps), extent[axis_at] // blocks).reshape((-1,) + (1,) * (len(extent) - axis_at - 1))

    loudness = one(*cuts[0])
    for cut in cuts[1:]:
        loudness = loudness * one(*cut)
    return loudness


def centred(rng, shape, spread, bound, cuts=(), kind=jnp.bfloat16):
    drawn = jax.random.normal(rng, shape, jnp.float32) * spread
    if len(cuts) > 0:
        drawn = block_levels(rng, shape, cuts, -0.22, 0.18) * drawn
    return jnp.clip(drawn, min=-bound, max=bound).astype(kind)


def setup_inputs(seed: int = 0) -> dict:
    key_of = jax.random.split(jax.random.key(seed), 13)
    tokens = centred(key_of[0], (TOKENS, D), 1.0, 6.0, ((0, 128),))
    lengths = draw_lengths(jax.random.fold_in(key_of[12], 71), 0)
    attn_gain = jnp.clip(1.0 + 0.1 * jax.random.normal(key_of[2], (D,), jnp.float32), 0.5, 1.5).astype(jnp.bfloat16)
    w_query = centred(key_of[3], (D, HEADS * HEAD_DIM), D ** -0.5, 0.125, ((0, 128),))
    w_key = centred(key_of[4], (D, KV_HEADS * HEAD_DIM), D ** -0.5, 0.125, ((0, 128),))
    w_value = centred(key_of[5], (D, KV_HEADS * HEAD_DIM), D ** -0.5, 0.125, ((0, 128),))
    w_out = centred(key_of[6], (HEADS * HEAD_DIM, D), (max(HEADS * HEAD_DIM // 256, 2)) ** -0.5, 2.0, ((0, 128),))
    mlp_gain = jnp.clip(1.0 + 0.1 * jax.random.normal(key_of[7], (D,), jnp.float32), 0.5, 1.5).astype(jnp.bfloat16)
    w_gate = centred(key_of[8], (D, FF), D ** -0.5, 0.125, ((0, 128),))
    w_up = centred(key_of[9], (D, FF), D ** -0.5, 0.125, ((0, 128),))
    w_down = centred(key_of[10], (FF, D), FF ** -0.5, 0.078125, ((0, 128),))
    cotangent = centred(key_of[11], (TOKENS, D), 1.0, 6.0, ((0, 128),))
    return {"tokens": tokens, "lengths": lengths, "attn_gain": attn_gain, "w_query": w_query, "w_key": w_key, "w_value": w_value, "w_out": w_out, "mlp_gain": mlp_gain, "w_gate": w_gate, "w_up": w_up, "w_down": w_down, "cotangent": cotangent}


EPS = 1e-05
THETA = 10000.0

@jax.custom_vjp
def low(v):
    return lax.optimization_barrier(v.astype(jnp.bfloat16)).astype(jnp.float32)

@jax.custom_vjp
def low_back(v):
    return v

def low_keep(v):
    return (low(v), None)

def low_pass(kept, grad):
    return (grad,)

def back_keep(v):
    return (v, None)

def back_low(kept, grad):
    return (low(grad),)
low.defvjp(low_keep, low_pass)
low_back.defvjp(back_keep, back_low)

def high_dot(left_arg, right_arg):
    return jnp.dot(left_arg, right_arg, precision=lax.Precision.HIGHEST)

def doc_layout(lengths_row, positions):
    first_end = lengths_row[0]
    second_end = lengths_row[0] + lengths_row[1]
    segment = (positions >= first_end).astype(jnp.int32) + (positions >= second_end).astype(jnp.int32)
    doc_start = jnp.where(segment == 0, 0, jnp.where(segment == 1, first_end, second_end)).astype(jnp.int32)
    return (segment, positions - doc_start)

def rotary_tables(offsets):
    half_dim = HEAD_DIM // 2
    frequency = jnp.exp(jnp.arange(half_dim, dtype=jnp.float32) * (-2.0 * math.log(THETA) / HEAD_DIM))
    angles = offsets.astype(jnp.float32)[:, None] * frequency[None, :]
    angles = jnp.concatenate([angles, angles], axis=1)
    return (jnp.cos(angles), jnp.sin(angles))

def rotate(values, cosine_table, sine_table, head_count):
    row_count = values.shape[0]
    shaped = values.reshape(row_count, head_count, HEAD_DIM)
    half_dim = HEAD_DIM // 2
    turned = jnp.concatenate([-shaped[..., half_dim:], shaped[..., :half_dim]], axis=-1)
    result = shaped * cosine_table[:, None, :] + turned * sine_table[:, None, :]
    return result.reshape(row_count, head_count * HEAD_DIM)

def attention(query_rot, key_rot, value_low, segment):
    query_three = query_rot.reshape(SEQ, HEADS, HEAD_DIM)
    key_wide = jnp.repeat(key_rot.reshape(SEQ, KV_HEADS, HEAD_DIM), HEADS // KV_HEADS, axis=1)
    value_wide = jnp.repeat(value_low.reshape(SEQ, KV_HEADS, HEAD_DIM), HEADS // KV_HEADS, axis=1)
    block_rows = min(512, SEQ)
    positions = jnp.arange(SEQ, dtype=jnp.int32)

    def one_block(block_index):
        row_start = block_index * block_rows
        query_block = lax.dynamic_slice_in_dim(query_three, row_start, block_rows, 0)
        scores = jnp.einsum('qhd,khd->hqk', query_block, key_wide, precision=lax.Precision.HIGHEST) * HEAD_DIM ** (-0.5)
        scores = low_back(scores)
        rows_seg = lax.dynamic_slice_in_dim(segment, row_start, block_rows, 0)
        rows_pos = row_start + jnp.arange(block_rows, dtype=jnp.int32)
        allowed = (rows_seg[:, None] == segment[None, :]) & (positions[None, :] <= rows_pos[:, None])
        scores = jnp.where(allowed[None], scores, -1e+30)
        soft_weights = jnp.exp(scores - jax.nn.logsumexp(scores, axis=-1, keepdims=True))
        attended = jnp.einsum('hqk,khd->qhd', low(soft_weights), value_wide, precision=lax.Precision.HIGHEST)
        return attended.reshape(block_rows, HEADS * HEAD_DIM)
    pieces = lax.map(jax.checkpoint(one_block), jnp.arange(SEQ // block_rows, dtype=jnp.int32))
    return pieces.reshape(SEQ, HEADS * HEAD_DIM)

def layer(inputs, attn_gain, w_query, w_key, w_value, w_out, mlp_gain, w_gate, w_up, w_down, segment, cosine_table, sine_table):
    recip_one = lax.rsqrt(lax.optimization_barrier(jnp.mean(inputs * inputs, axis=1, keepdims=True)) + EPS)
    normed_one = low(inputs * recip_one * attn_gain)
    query_rot = low(rotate(low_back(high_dot(normed_one, w_query)), cosine_table, sine_table, HEADS))
    key_rot = low(rotate(low_back(high_dot(normed_one, w_key)), cosine_table, sine_table, KV_HEADS))
    value_low = low(low_back(high_dot(normed_one, w_value)))
    attended = low(low_back(attention(query_rot, key_rot, value_low, segment)))
    hidden = inputs + low_back(high_dot(attended, w_out))
    recip_two = lax.rsqrt(lax.optimization_barrier(jnp.mean(hidden * hidden, axis=1, keepdims=True)) + EPS)
    normed_two = low(hidden * recip_two * mlp_gain)
    gate_pre = low_back(high_dot(normed_two, w_gate))
    upward = low_back(high_dot(normed_two, w_up))
    activated = low(jax.nn.silu(gate_pre) * upward)
    return hidden + low_back(high_dot(activated, w_down))

def reference(tokens, lengths, attn_gain, w_query, w_key, w_value, w_out, mlp_gain, w_gate, w_up, w_down, cotangent):
    params_f32 = tuple((matrix.astype(jnp.float32) for matrix in (attn_gain, w_query, w_key, w_value, w_out, mlp_gain, w_gate, w_up, w_down)))
    inputs_all = tokens.astype(jnp.float32).reshape(GROUPS, SEQ, D)
    cot_all = cotangent.astype(jnp.float32).reshape(GROUPS, SEQ, D)
    positions = jnp.arange(SEQ, dtype=jnp.int32)

    def one_group(totals, group_data):
        inputs, grad_output, lengths_row = group_data
        segment, offsets = doc_layout(lengths_row, positions)
        cosine_table, sine_table = rotary_tables(offsets)

        def apply_layer(inputs_in, *params):
            return layer(inputs_in, *params, segment, cosine_table, sine_table)
        result, pullback = jax.vjp(apply_layer, inputs, *params_f32)
        gradients = pullback(grad_output)
        totals = tuple((running + piece_grad for running, piece_grad in zip(totals, gradients[1:])))
        return (totals, (result.astype(jnp.bfloat16), gradients[0]))
    zero_sums = tuple((jnp.zeros(matrix.shape, jnp.float32) for matrix in params_f32))
    totals, (outputs, grad_inputs) = lax.scan(one_group, zero_sums, (inputs_all, cot_all, lengths))
    return (outputs.reshape(TOKENS, D), grad_inputs.reshape(TOKENS, D), totals[0], totals[1], totals[2], totals[3], totals[4], totals[5], totals[6], totals[7], totals[8])
```

```python
import functools
import math

import jax
import jax.numpy as jnp
from jax import lax
from jax.experimental import pallas as pl
from jax.experimental.pallas import tpu as pltpu
from jax.sharding import Mesh
from jax.sharding import PartitionSpec as P

HEADS = 32
KV_HEADS = 4
HD = 64
EPS = 1e-05
THETA = 10000.0
NEG = -1e30
BF = jnp.bfloat16
F32 = jnp.float32
ANY = pl.ANY
VMEM = pltpu.VMEM
TP = ("x", "core")
DP = ("z", "y")
ALL = ("z", "core", "x", "y")


def tdot(a, b):
    return lax.dot_general(a, b, (((0,), (0,)), ((), ())), preferred_element_type=F32)


def dott(a, b):
    return lax.dot_general(a, b, (((1,), (1,)), ((), ())), preferred_element_type=F32)


def dot(a, b):
    return jnp.dot(a, b, preferred_element_type=F32)


class Wire:
    def __init__(self, ssem, rsem):
        self.ssem, self.rsem, self.sent = ssem, rsem, []

    def put(self, src, dst, k, to):
        cp = pltpu.make_async_remote_copy(
            src_ref=src, dst_ref=dst, send_sem=self.ssem.at[k], recv_sem=self.rsem.at[k],
            device_id=to, device_id_type=pl.DeviceIdType.MESH)
        cp.start()
        self.sent.append(cp)

    def got(self, dst, k, to):
        pltpu.make_async_remote_copy(
            src_ref=dst, dst_ref=dst, send_sem=self.ssem.at[k], recv_sem=self.rsem.at[k],
            device_id=to, device_id_type=pl.DeviceIdType.MESH).wait_recv()

    def drain(self):
        for cp in self.sent:
            cp.wait_send()


def greet(peers):
    barrier = pltpu.get_barrier_semaphore()
    for to in peers:
        pl.semaphore_signal(barrier, inc=1, device_id=to, device_id_type=pl.DeviceIdType.MESH)
    pl.semaphore_wait(barrier, len(peers))


def cx_ring():
    c, x = lax.axis_index("core"), lax.axis_index("x")
    right, left, opp = lax.rem(x + 1, 4), lax.rem(x + 3, 4), lax.rem(x + 2, 4)
    return c, x, right, left, opp, {"x": right}, {"x": left}, {"core": 1 - c}


def comm_params(cid, mb=None):
    kw = {} if mb is None else {"vmem_limit_bytes": mb << 20}
    return pltpu.CompilerParams(collective_id=cid, has_side_effects=True, **kw)


class Mail(Wire):
    def __init__(self, ssem, rsem):
        super().__init__(ssem, rsem)
        self.used = 0

    def new(self):
        self.used += 1
        return self.used - 1


def around(q):
    return lax.rem(q + 1, 4), lax.rem(q + 3, 4), lax.rem(q + 2, 4)


def ring(w, s, axis, q):
    right, left, opp = around(q)
    to_r, to_l = {axis: right}, {axis: left}
    k = [w.new() for _ in range(4)]
    w.put(s(q, None), s(q, None), k[0], to_r)
    w.put(s(q, None), s(q, None), k[1], to_l)
    yield
    w.got(s(left, None), k[0], to_l)
    w.put(s(left, 0), s(left, 0), k[2], to_r)
    w.got(s(right, None), k[1], to_r)
    w.put(s(right, 1), s(right, 1), k[3], to_l)
    yield
    w.got(s(opp, 0), k[2], to_l)
    w.got(s(opp, 1), k[3], to_r)


def col_flows(w, W, z, y):
    cut = lambda h: slice(None) if h is None else pl.ds(2 * h, 2)

    def first():
        yield from ring(w, lambda p, h: W.at[z, 0, cut(h), p], "y", y)
        yield from ring(w, lambda p, h: W.at[p, 0, cut(h)], "z", z)

    def second():
        yield from ring(w, lambda p, h: W.at[p, 1, cut(h), y], "z", z)
        yield from ring(w, lambda p, h: W.at[:, 1, cut(h), p], "y", y)

    return [first(), second()]


def row_flows(w, W, z, y):
    n = W.shape[-1] // 4
    cut = lambda b, h: pl.ds(2 * n * b, 2 * n) if h is None else pl.ds(2 * n * b + n * h, n)

    def first():
        yield from ring(w, lambda p, h: W.at[z, p, :, cut(0, h)], "y", y)
        yield from ring(w, lambda p, h: W.at[p, :, :, cut(0, h)], "z", z)

    def second():
        yield from ring(w, lambda p, h: W.at[p, y, :, cut(1, h)], "z", z)
        yield from ring(w, lambda p, h: W.at[:, p, :, cut(1, h)], "y", y)

    return [first(), second()]


def pump(flows):
    for f in flows:
        next(f, None)


def gather8(w, src, dst):
    c, x, right, left, opp, to_r, to_l, to_c = cx_ring()
    rows = dst.shape[2]
    lo, hi = pl.ds(0, rows // 2), pl.ds(rows // 2, rows // 2)
    k = [w.new() for _ in range(9)]
    w.put(src, dst.at[c, x], k[0], to_r)
    w.put(src, dst.at[c, x], k[1], to_l)
    w.put(src, dst.at[c, x], k[4], to_c)
    yield
    w.got(dst.at[c, left], k[0], to_l)
    w.put(dst.at[c, left, lo], dst.at[c, left, lo], k[2], to_r)
    w.put(dst.at[c, left], dst.at[c, left], k[5], to_c)
    w.got(dst.at[c, right], k[1], to_r)
    w.put(dst.at[c, right, hi], dst.at[c, right, hi], k[3], to_l)
    w.put(dst.at[c, right], dst.at[c, right], k[6], to_c)
    yield
    w.got(dst.at[c, opp, lo], k[2], to_l)
    w.put(dst.at[c, opp, lo], dst.at[c, opp, lo], k[7], to_c)
    w.got(dst.at[c, opp, hi], k[3], to_r)
    w.put(dst.at[c, opp, hi], dst.at[c, opp, hi], k[8], to_c)
    yield
    w.got(dst.at[1 - c, x], k[4], to_c)
    w.got(dst.at[1 - c, left], k[5], to_c)
    w.got(dst.at[1 - c, right], k[6], to_c)
    w.got(dst.at[1 - c, opp, lo], k[7], to_c)
    w.got(dst.at[1 - c, opp, hi], k[8], to_c)


def add_to(dst, other, r0, rows, step=16):
    @pl.loop(0, rows // step)
    def _(i):
        a = pl.ds(pl.multiple_of(r0 + i * step, step), step)
        b = pl.ds(pl.multiple_of(i * step, step), step)
        dst[a, :] = (dst[a, :].astype(F32) + other[b, :].astype(F32)).astype(dst.dtype)


def scatter8_core(w, p, core_r, state):
    c, x, right, left, opp, to_r, to_l, to_c = cx_ring()
    state["k"] = [w.new() for _ in range(4)]
    for i, xx in enumerate((opp, right, left, x)):
        w.put(p.at[1 - c, xx], core_r.at[i], state["k"][i], to_c)


def scatter8_ring(w, p, core_r, hop, fin, state):
    c, x, right, left, opp, to_r, to_l, to_c = cx_ring()
    rows = p.shape[2]
    half = rows // 2
    lo, hi = pl.ds(0, half), pl.ds(half, half)
    kc = state["k"]
    k = [w.new() for _ in range(6)]
    w.got(core_r.at[0], kc[0], to_c)
    add_to(p.at[c, opp], core_r.at[0], 0, rows)
    w.put(p.at[c, opp, lo], hop.at[0], k[0], to_r)
    w.put(p.at[c, opp, hi], hop.at[1], k[1], to_l)
    w.got(core_r.at[1], kc[1], to_c)
    add_to(p.at[c, right], core_r.at[1], 0, rows)
    w.put(p.at[c, right, hi], fin.at[0, hi], k[2], to_r)
    w.got(core_r.at[2], kc[2], to_c)
    add_to(p.at[c, left], core_r.at[2], 0, rows)
    w.put(p.at[c, left, lo], fin.at[1, lo], k[3], to_l)
    yield
    w.got(hop.at[0], k[0], to_l)
    add_to(p.at[c, right], hop.at[0], 0, half)
    w.put(p.at[c, right, lo], fin.at[0, lo], k[4], to_r)
    w.got(hop.at[1], k[1], to_r)
    add_to(p.at[c, left], hop.at[1], half, half)
    w.put(p.at[c, left, hi], fin.at[1, hi], k[5], to_l)
    yield
    w.got(core_r.at[3], kc[3], to_c)
    w.got(fin.at[0, hi], k[2], to_l)
    w.got(fin.at[1, lo], k[3], to_r)
    w.got(fin.at[0, lo], k[4], to_l)
    w.got(fin.at[1, hi], k[5], to_r)


def lanes(shape):
    return lax.broadcasted_iota(jnp.int32, shape, len(shape) - 1)


def swap_halves(u):
    first = lax.rem(lanes(u.shape), 64) < 32
    return jnp.where(first, pltpu.roll(u, 96, u.ndim - 1), pltpu.roll(u, 32, u.ndim - 1))


def entry(peers, extra=None):
    barrier = pltpu.get_barrier_semaphore()
    for to in peers:
        pl.semaphore_signal(barrier, inc=1, device_id=to, device_id_type=pl.DeviceIdType.MESH)
    if extra is None:
        pl.semaphore_wait(barrier, len(peers))
        return
    more, to = extra

    @pl.when(more)
    def _():
        pl.semaphore_signal(barrier, inc=1, device_id=to, device_id_type=pl.DeviceIdType.MESH)
        pl.semaphore_wait(barrier, len(peers) + 1)

    @pl.when(jnp.logical_not(more))
    def _():
        pl.semaphore_wait(barrier, len(peers))


def tp_peers(c, x):
    r = 2 * x + c
    out = []
    for k in range(1, 8):
        rr = lax.rem(r + k, 8)
        out.append((rr, {"x": rr // 2, "core": lax.rem(rr, 2)}))
    return out


def spread(w, src, W, z, c, x, y, local_sem):
    ks = [w.new() for _ in range(7)]
    for k, (rr, to) in zip(ks, tp_peers(c, x)):
        w.put(src.at[rr], W.at[z, c, x, y], k, to)
    own = pltpu.make_async_copy(src.at[2 * x + c], W.at[z, c, x, y], local_sem)
    own.start()
    yield
    r = 2 * x + c
    for i, k in enumerate(ks):
        rr = lax.rem(r + 7 - i, 8)
        w.got(W.at[z, lax.rem(rr, 2), rr // 2, y], k, {"x": rr // 2, "core": lax.rem(rr, 2)})
    own.wait()


def transpose_zx(w, src, dst_of, z, x, local_sem):
    k = w.new()
    to = {"z": x, "x": z}

    def far():
        return pltpu.make_async_remote_copy(
            src_ref=src, dst_ref=dst_of(x), send_sem=w.ssem.at[k], recv_sem=w.rsem.at[k],
            device_id=to, device_id_type=pl.DeviceIdType.MESH)

    def near():
        return pltpu.make_async_copy(src, dst_of(x), local_sem)

    @pl.when(z != x)
    def _():
        far().start()

    @pl.when(z == x)
    def _():
        near().start()

    yield

    @pl.when(z != x)
    def _():
        far().wait_send()
        w.got(dst_of(z), k, to)

    @pl.when(z == x)
    def _():
        near().wait()


def attend(q, keys, j, y, c1, c2):
    n = keys.shape[0]
    s = dott(q, keys)
    row = lax.broadcasted_iota(jnp.int32, (512, 1), 0)
    place = (4 * j + y) * 128 + lax.rem(row, 128)
    start = jnp.where(place >= c2, c2, jnp.where(place >= c1, c1, 0))
    at = lax.broadcasted_iota(jnp.int32, (512, n), 1)
    s = jnp.where((at >= start) & (at <= place), s, NEG)
    top = jnp.max(s, axis=1, keepdims=True)
    e = jnp.exp(s - top)
    total = jnp.sum(e, axis=1, keepdims=True)
    return dot(e.astype(BF), keys) / total, top + jnp.log(total)


def pair_heads(first, second, lower):
    low = lanes(first.shape) < 64
    if lower:
        return jnp.where(low, first, pltpu.roll(second, 64, 1))
    return jnp.where(low, pltpu.roll(first, 64, 1), second)


def m1_kernel(lens, x_ref, cos, sin, cot, qkv_s, out_s, gate_s, up_s, down_s,
              h, n2, n1_out, cg, qp, kv, o, lse, wqkv, wout, wgate, wup, wdown,
              n1, p, core_r, hop, fin, ssem, rsem, lsem):
    z, c, x, y = (lax.axis_index(a) for a in ALL)
    peers = [to for _, to in tp_peers(c, x)]
    for axis, q in (("y", y), ("z", z)):
        peers += [{axis: lax.rem(q + 1, 4)}, {axis: lax.rem(q + 3, 4)}]
    entry(peers, (z != x, {"z": x, "x": z}))
    w = Mail(ssem, rsem)

    sp_qkv = spread(w, qkv_s, wqkv, z, c, x, y, lsem.at[0])
    pump([sp_qkv])

    @pl.loop(0, 8)
    def _(i):
        rows = pl.ds(pl.multiple_of(i * 16, 16), 16)
        v = x_ref[rows, :].astype(F32)
        n1[c, x, rows, :] = (v * lax.rsqrt(jnp.mean(v * v, axis=1, keepdims=True) + EPS)).astype(BF)

    ag_n1 = gather8(w, n1.at[c, x], n1)
    pump([ag_n1])
    tr_out = transpose_zx(w, out_s, lambda zz: wout.at[zz, y], z, x, lsem.at[1])
    sp_gate = spread(w, gate_s, wgate, z, c, x, y, lsem.at[2])
    sp_up = spread(w, up_s, wup, z, c, x, y, lsem.at[3])
    tr_down = transpose_zx(w, down_s, lambda zz: wdown.at[zz, y], z, x, lsem.at[4])
    early = [tr_out, sp_gate, sp_up, tr_down]
    pump(early)
    pump([sp_qkv])
    fl_qkv = col_flows(w, wqkv, z, y)
    pump(fl_qkv)
    pump(early)
    fl_qkv_out = fl_qkv + row_flows(w, wout, z, y)
    pump(fl_qkv_out[2:])
    pump(fl_qkv_out)
    pump(fl_qkv_out)
    pump([ag_n1])
    fl_mlp = col_flows(w, wgate, z, y) + col_flows(w, wup, z, y) + row_flows(w, wdown, z, y)
    pump(fl_mlp)
    pump(fl_qkv_out)
    pump([ag_n1])
    pump(fl_qkv_out)
    pump([ag_n1])
    pump(fl_mlp)

    save_n1 = pltpu.make_async_copy(n1, n1_out, lsem.at[5])
    save_n1.start()
    own_cot = pltpu.make_async_copy(cot, cg.at[c, x], lsem.at[6])
    own_cot.start()
    ag_cot = gather8(w, cot, cg)
    pump([ag_cot])

    weights = wqkv[...].reshape(2048, 384)

    def project(g, keys_too):
        u = dot(n1[g].reshape(512, 2048), weights)
        cs, sn = cos[g], sin[g]
        for t in range(2):
            v = u[:, 128 * t: 128 * t + 128]
            v = (v * cs + swap_halves(v) * sn) * (HD ** -0.5)
            low = lanes(v.shape) < 64
            for b, head in enumerate((v, pltpu.roll(v, 64, 1))):
                rows = pl.ds(128 * (2 * t + b), 128)
                qp[g, :, rows, :] = jnp.where(low, head, 0.0).astype(BF).reshape(4, 128, 128)
        if keys_too:
            v = u[:, 256:384]
            turned = jnp.where(lanes(v.shape) < 64, v * cs + swap_halves(v) * sn, v)
            kv[g, :, y] = turned.astype(BF).reshape(4, 128, 128)

    g0, g1 = 1 - c, c
    to_c = {"core": 1 - c}
    project(g0, True)
    halves = lambda h: slice(None) if h is None else pl.ds(2 * h, 2)
    fl_kv = [ring(w, lambda pp, hh: kv.at[g0, halves(hh), pp], "y", y)]
    pump(fl_kv)
    project(g1, False)
    pump(fl_mlp)
    pump(fl_kv)
    pump(fl_kv)
    k_kv = w.new()
    w.put(kv.at[g0], kv.at[g0], k_kv, to_c)

    state = {}
    out_w = wout[...].reshape(256, 2048)
    for turn_no, g in enumerate((g0, g1)):
        if turn_no == 1:
            w.got(kv.at[g], k_kv, to_c)
        for j in range(4):
            n = 512 * (j + 1)
            keys = kv[g, 0:j + 1].reshape(n, 128)
            res, total = attend(qp[g, j], keys, j, y, lens[g, 0], lens[g, 1])
            heads = [res[128 * a: 128 * a + 128] for a in range(4)]
            rows = pl.ds(128 * j, 128)
            o[g, rows, 0:128] = pair_heads(heads[0], heads[1], False).astype(BF)
            o[g, rows, 128:256] = pair_heads(heads[2], heads[3], False).astype(BF)
            lse[g, pl.ds(j, 1), :] = jnp.broadcast_to(total, (512, 128)).T[0:1, :]
            if j == 1:
                pump([ag_cot])
        ov = o[g]

        @pl.loop(0, 4)
        def _(i):
            p[g, i] = dot(o[g, pl.ds(pl.multiple_of(128 * i, 128), 128), :], out_w).astype(BF)

        if turn_no == 0:
            scatter8_core(w, p, core_r, state)
            pump(fl_mlp)
    rs = scatter8_ring(w, p, core_r, hop, fin, state)
    pump([rs])
    pump([rs])
    pump([ag_cot])
    pump(fl_mlp)
    pump([rs])

    @pl.loop(0, 8)
    def _(i):
        rows = pl.ds(pl.multiple_of(i * 16, 16), 16)
        v = x_ref[rows, :].astype(F32) + p[c, x, rows, :].astype(F32) + core_r[3, rows, :].astype(F32)
        v = v + fin[0, rows, :].astype(F32) + fin[1, rows, :].astype(F32)
        h[rows, :] = v
        n2[rows, :] = (v * lax.rsqrt(jnp.mean(v * v, axis=1, keepdims=True) + EPS)).astype(BF)

    w.drain()
    save_n1.wait()
    own_cot.wait()


def forward_attention(lens, tokens, cos, sin, cot, qkv_s, out_s, gate_s, up_s, down_s, cid):
    sds = jax.ShapeDtypeStruct
    vm, hb = pl.BlockSpec(memory_space=VMEM), pl.BlockSpec(memory_space=ANY)
    outs = [
        (sds((128, 2048), F32), vm), (sds((128, 2048), BF), vm), (sds((2, 4, 128, 2048), BF), hb),
        (sds((2, 4, 128, 2048), BF), hb), (sds((2, 4, 512, 128), BF), vm), (sds((2, 4, 4, 128, 128), BF), vm),
        (sds((2, 512, 256), BF), vm), (sds((2, 4, 512), F32), vm), (sds((4, 2, 4, 4, 16, 384), BF), vm),
        (sds((4, 4, 16, 2048), BF), vm), (sds((4, 2, 4, 4, 16, 768), BF), hb), (sds((4, 2, 4, 4, 16, 768), BF), hb),
        (sds((4, 4, 48, 2048), BF), hb),
    ]
    return pl.pallas_call(
        m1_kernel,
        out_shape=[a for a, _ in outs],
        in_specs=[pl.BlockSpec(memory_space=pltpu.SMEM)] + [vm] * 3 + [hb] * 6,
        out_specs=[b for _, b in outs],
        scratch_shapes=[
            VMEM((2, 4, 128, 2048), BF), VMEM((2, 4, 128, 2048), BF), VMEM((4, 128, 2048), BF),
            VMEM((2, 64, 2048), BF), VMEM((2, 128, 2048), BF),
            pltpu.SemaphoreType.DMA((140,)), pltpu.SemaphoreType.DMA((140,)), pltpu.SemaphoreType.DMA((7,)),
        ],
        compiler_params=comm_params(cid, 60),
        name="forward_attention",
    )(lens, tokens, cos, sin, cot, qkv_s, out_s, gate_s, up_s, down_s)


def m2_kernel(n2, h, cot, cg, wgate, wup, wdown,
              dh, da, s2, g_gate, g_up, g_down,
              n2v, cv, wg, wu, wd, dact, a_all, dg_all, du_all, p3, p2, core3, core2, hop, fin, st_w, st_d,
              ssem, rsem, lsem):
    c, x = lax.axis_index("core"), lax.axis_index("x")
    entry([{"x": lax.rem(x + 1, 4)}, {"x": lax.rem(x + 3, 4)}, {"core": 1 - c}])
    w = Mail(ssem, rsem)
    ag = gather8(w, n2, n2v)
    pump([ag])
    loads = [pltpu.make_async_copy(a, b, lsem.at[i]) for i, (a, b) in enumerate(
        ((n2, n2v.at[c, x]), (cg, cv), (wdown, wd), (wgate, wg), (wup, wu)))]
    for cp in loads:
        cp.start()
    loads[1].wait()
    loads[2].wait()
    down = wd[...].reshape(768, 2048)

    @pl.loop(0, 2)
    def _(g):
        for t in range(2):
            dact[g, pl.ds(256 * t, 256), :] = dott(cv[g, 2 * t: 2 * t + 2].reshape(256, 2048), down)

    pump([ag])
    loads[0].wait()
    pump([ag])
    loads[3].wait()
    loads[4].wait()
    gate, up = wg[...].reshape(2048, 768), wu[...].reshape(2048, 768)
    pump([ag])

    def half(g):
        @pl.loop(0, 2)
        def _(t):
            rows = pl.ds(pl.multiple_of(256 * t, 256), 256)
            xv = n2v[g, pl.ds(2 * t, 2)].reshape(256, 2048)
            gp, u = dot(xv, gate), dot(xv, up)
            sig = jax.nn.sigmoid(gp)
            act = gp * sig
            d = dact[g, rows, :]
            a_all[g, rows, :] = (act * u).astype(BF)
            dg_all[g, rows, :] = (d * u * sig * (1.0 + gp * (1.0 - sig))).astype(BF)
            du_all[g, rows, :] = (d * act).astype(BF)

        @pl.loop(0, 8)
        def _(i):
            part = dott(dg_all[g], wg[i // 2, i % 2].reshape(256, 768))
            part += dott(du_all[g], wu[i // 2, i % 2].reshape(256, 768))
            p3[g, :, :, pl.ds(pl.multiple_of(256 * i, 256), 256)] = part.astype(BF).reshape(4, 128, 256)

    g0, g1 = 1 - c, c
    st3, st2 = {}, {}
    half(g0)
    scatter8_core(w, p3, core3, st3)
    half(g1)
    rs3 = scatter8_ring(w, p3, core3, hop, fin, st3)
    pump([rs3])

    def out_part(g):
        @pl.loop(0, 8)
        def _(i):
            cols = pl.ds(pl.multiple_of(256 * i, 256), 256)
            p2[g, :, :, cols] = dot(a_all[g], wd[:, :, :, cols].reshape(768, 256)).astype(BF).reshape(4, 128, 256)

    out_part(g0)
    scatter8_core(w, p2, core2, st2)
    out_part(g1)
    pump([rs3])

    dg, du, av = dg_all[...].reshape(1024, 768), du_all[...].reshape(1024, 768), a_all[...].reshape(1024, 768)

    def stage(i, k):
        return pltpu.make_async_copy(st_w.at[i % 2, k], (g_gate, g_up)[k].at[i // 2, i % 2], lsem.at[5 + 2 * (i % 2) + k])

    for i in range(8):
        t = n2v[:, :, :, 256 * i: 256 * i + 256].reshape(1024, 256).T
        if i >= 2:
            stage(i - 2, 0).wait()
            stage(i - 2, 1).wait()
        st_w[i % 2, 0] = dot(t, dg).astype(BF).reshape(4, 4, 16, 768)
        st_w[i % 2, 1] = dot(t, du).astype(BF).reshape(4, 4, 16, 768)
        stage(i, 0).start()
        stage(i, 1).start()

    cc, xx, right, left, opp, to_r, to_l, to_c = cx_ring()
    for i, b in enumerate((opp, right, left, x)):
        w.got(core2.at[i], st2["k"][i], to_c)
        add_to(p2.at[c, b], core2.at[i], 0, 128)
    save = pltpu.make_async_copy(p2.at[c], s2, lsem.at[9])
    save.start()
    ct = cv[...].reshape(1024, 2048)

    def keep(i):
        return pltpu.make_async_copy(st_d.at[i], g_down.at[pl.ds(i, 1)], lsem.at[10 + i])

    for i in range(4):
        t = av[:, 192 * i: 192 * i + 192].T
        st_d[i] = dot(t, ct).astype(BF).reshape(1, 4, 48, 2048)
        keep(i).start()
    pump([rs3])

    @pl.loop(0, 8)
    def _(i):
        rows = pl.ds(pl.multiple_of(i * 16, 16), 16)
        e = p3[c, x, rows, :].astype(F32) + core3[3, rows, :].astype(F32)
        e = e + fin[0, rows, :].astype(F32) + fin[1, rows, :].astype(F32)
        v = h[rows, :]
        r = lax.rsqrt(jnp.mean(v * v, axis=1, keepdims=True) + EPS)
        out = cot[rows, :].astype(F32) + r * e - v * (r * r * r * jnp.mean(e * v, axis=1, keepdims=True))
        dh[rows, :] = out
        da[rows, :] = out.astype(BF)

    w.drain()
    save.wait()
    for i in (6, 7):
        stage(i, 0).wait()
        stage(i, 1).wait()
    for i in range(4):
        keep(i).wait()


def feed_forward(n2, h, cot, cg, wgate, wup, wdown, cid):
    sds = jax.ShapeDtypeStruct
    vm, hb = pl.BlockSpec(memory_space=VMEM), pl.BlockSpec(memory_space=ANY)
    col = (4, 2, 4, 4, 16, 768)
    outs = [(sds((128, 2048), F32), vm), (sds((128, 2048), BF), vm), (sds((4, 128, 2048), BF), hb),
            (sds(col, BF), hb), (sds(col, BF), hb), (sds((4, 4, 48, 2048), BF), hb)]
    return pl.pallas_call(
        m2_kernel,
        out_shape=[a for a, _ in outs],
        in_specs=[hb, vm, vm, hb, hb, hb, hb],
        out_specs=[b for _, b in outs],
        scratch_shapes=[
            VMEM((2, 4, 128, 2048), BF), VMEM((2, 4, 128, 2048), BF), VMEM(col, BF), VMEM(col, BF),
            VMEM((4, 4, 48, 2048), BF), VMEM((2, 512, 768), F32), VMEM((2, 512, 768), BF), VMEM((2, 512, 768), BF),
            VMEM((2, 512, 768), BF), VMEM((2, 4, 128, 2048), BF), VMEM((2, 4, 128, 2048), BF),
            VMEM((4, 128, 2048), BF), VMEM((4, 128, 2048), BF), VMEM((2, 64, 2048), BF), VMEM((2, 128, 2048), BF),
            VMEM((2, 2, 4, 4, 16, 768), BF), VMEM((4, 1, 4, 48, 2048), BF),
            pltpu.SemaphoreType.DMA((30,)), pltpu.SemaphoreType.DMA((30,)), pltpu.SemaphoreType.DMA((14,)),
        ],
        compiler_params=comm_params(cid, 63),
        name="feed_forward",
    )(n2, h, cot, cg, wgate, wup, wdown)


def ring_tail(w, s, hop, fin):
    c, x, right, left, opp, to_r, to_l, to_c = cx_ring()
    half = s.shape[1] // 2
    lo, hi = pl.ds(0, half), pl.ds(half, half)
    k = [w.new() for _ in range(6)]
    w.put(s.at[opp, lo], hop.at[0], k[0], to_r)
    w.put(s.at[opp, hi], hop.at[1], k[1], to_l)
    w.put(s.at[right, hi], fin.at[0, hi], k[2], to_r)
    w.put(s.at[left, lo], fin.at[1, lo], k[3], to_l)
    yield
    w.got(hop.at[0], k[0], to_l)
    add_to(s.at[right], hop.at[0], 0, half)
    w.put(s.at[right, lo], fin.at[0, lo], k[4], to_r)
    w.got(hop.at[1], k[1], to_r)
    add_to(s.at[left], hop.at[1], half, half)
    w.put(s.at[left, hi], fin.at[1, hi], k[5], to_l)
    yield
    w.got(fin.at[0, hi], k[2], to_l)
    w.got(fin.at[1, lo], k[3], to_r)
    w.got(fin.at[0, lo], k[4], to_l)
    w.got(fin.at[1, hi], k[5], to_r)


def others(w, q, axis, piece, recv):
    ks = {}
    for k in (1, 3, 2):
        to = lax.rem(q + k, 4)
        ks[k] = w.new()
        w.put(piece(to), recv.at[k - 1], ks[k], {axis: to})
    return [(recv.at[k - 1], ks[k], {axis: lax.rem(q + 4 - k, 4)}) for k in (1, 3, 2)]


def sum_four(dst, own, recv, lead):
    total = math.prod(lead)

    @pl.loop(0, total)
    def _(i):
        at = (i,) if len(lead) == 1 else (i // lead[1], lax.rem(i, lead[1]))
        acc = own[at].astype(F32)
        for k in range(3):
            acc += recv[(k,) + at].astype(F32)
        dst[at] = acc.astype(dst.dtype)


def col_job(w, src, r1, t, r2, s, e, z, y, lsem):
    if e == 0:
        own, piece1, ax1, q1 = src.at[:, 0, :, y], lambda p: src.at[:, 0, :, p], "y", y
        piece2, ax2, q2 = lambda p: t.at[p], "z", z
    else:
        own, piece1, ax1, q1 = src.at[z, 1], lambda p: src.at[p, 1], "z", z
        piece2, ax2, q2 = lambda p: t.at[:, p], "y", y
    first = pltpu.make_async_copy(own, t, lsem)
    first.start()
    waits = others(w, q1, ax1, piece1, r1)
    yield
    first.wait()
    for a in waits:
        w.got(*a)
    sum_four(t, t, r1, (4, 4))
    waits = others(w, q2, ax2, piece2, r2)
    yield
    for a in waits:
        w.got(*a)
    sum_four(s.at[e], piece2(q2), r2, (4,))


def row_job(w, src, r1, t, r2, s, e, z, y, lsem):
    n = src.shape[-1] // 2
    rows = src.shape[2]
    cols = pl.ds(e * n, n)
    if e == 0:
        own, piece1, ax1, q1 = src.at[:, y, :, cols], lambda p: src.at[:, p, :, cols], "y", y
        ax2, q2 = "z", z
    else:
        own, piece1, ax1, q1 = src.at[z, :, :, cols], lambda p: src.at[p, :, :, cols], "z", z
        ax2, q2 = "y", y
    first = pltpu.make_async_copy(own, t, lsem)
    first.start()
    waits = others(w, q1, ax1, piece1, r1)
    yield
    first.wait()
    for a in waits:
        w.got(*a)
    sum_four(t, t, r1, (4,))
    waits = others(w, q2, ax2, lambda p: t.at[p], r2)
    yield
    for a in waits:
        w.got(*a)

    @pl.loop(0, rows // 16)
    def _(i):
        at = pl.ds(pl.multiple_of(i * 16, 16), 16)
        acc = t[q2, at].astype(F32)
        for k in range(3):
            acc += r2[k, at].astype(F32)
        s[at, cols] = acc.astype(BF)


def hand_out(w, s, f, c, x):
    r = 2 * x + c
    ks = [w.new() for _ in range(7)]
    for k, (rr, to) in zip(ks, tp_peers(c, x)):
        w.put(s.at[lax.rem(rr, 2), rr // 2], f.at[r], k, to)
    f[r] = s[c, x]
    yield
    for i, k in enumerate(ks):
        rr = lax.rem(r + 7 - i, 8)
        w.got(f.at[rr], k, {"x": rr // 2, "core": lax.rem(rr, 2)})


def m3_kernel(lens, da, dh, x_ref, h, cos, sin, n1g, wqkv, wout, qp, kv, o, lse, s2, g_gate, g_up, g_down,
              out, gt, f_gate, f_up, f_qkv, f_down, f_out,
              dav, n1v, s2v, do4, delta, acc, kvt, dqt, dkv_s, dkv_r, dqkv, p4, core_r, hop, fin, hop2, fin2,
              d_qkv, d_out,
              ra0, ra1, rb0, rb1, rc0, rc1, rd0, rd1, re0, re1,
              ta0, ta1, tb0, tb1, tc0, tc1, td0, td1, te0, te1,
              qa0, qa1, qb0, qb1, qc0, qc1, qd0, qd1, qe0, qe1,
              s_gate, s_up, s_qkv, s_down, s_out, ssem, rsem, lsem):
    z, c, x, y = (lax.axis_index(a) for a in ALL)
    peers = [to for _, to in tp_peers(c, x)]
    for axis, q in (("y", y), ("z", z)):
        peers += [{axis: lax.rem(q + k, 4)} for k in (1, 2, 3)]
    entry(peers, (z != x, {"z": x, "x": z}))
    w = Mail(ssem, rsem)
    ag = gather8(w, da, dav)
    pump([ag])
    loads = [pltpu.make_async_copy(a, b, lsem.at[i]) for i, (a, b) in enumerate(
        ((da, dav.at[c, x]), (s2, s2v), (n1g, n1v)))]
    for cp in loads:
        cp.start()
    jobs = [
        col_job(w, g_gate, ra0, ta0, qa0, s_gate, 0, z, y, lsem.at[3]),
        col_job(w, g_gate, ra1, ta1, qa1, s_gate, 1, z, y, lsem.at[4]),
        col_job(w, g_up, rb0, tb0, qb0, s_up, 0, z, y, lsem.at[5]),
        col_job(w, g_up, rb1, tb1, qb1, s_up, 1, z, y, lsem.at[6]),
        row_job(w, g_down, rc0, tc0, qc0, s_down, 0, z, y, lsem.at[7]),
        row_job(w, g_down, rc1, tc1, qc1, s_down, 1, z, y, lsem.at[8]),
    ]
    pump(jobs)
    pump([ag])
    loads[0].wait()
    pump([ag])
    loads[1].wait()
    tail2 = ring_tail(w, s2v, hop2, fin2)
    pump([tail2])
    pump([ag])

    ow = wout[...].reshape(256, 2048)
    for g in range(2):
        dv = dott(dav[g].reshape(512, 2048), ow).astype(BF).astype(F32)
        ov = o[g].astype(F32)
        for t in range(2):
            v = dv[:, 128 * t: 128 * t + 128]
            pr = v * ov[:, 128 * t: 128 * t + 128]
            low = lanes(v.shape) < 64
            for b, head in enumerate((pltpu.roll(v, 64, 1), v)):
                rows = pl.ds(128 * (2 * t + b), 128)
                do4[g, :, rows, :] = jnp.where(low, 0.0, head).astype(BF).reshape(4, 128, 128)
                total = jnp.sum(jnp.where(low == (b == 0), pr, 0.0), axis=1, keepdims=True)
                total = jnp.broadcast_to(total, (512, 128)).T
                for j in range(4):
                    delta[g, pl.ds(j, 1), rows] = total[0:1, 128 * j: 128 * j + 128]

    ot = o[...].reshape(1024, 256).T

    @pl.loop(0, 8)
    def _(i):
        cols = pl.ds(pl.multiple_of(256 * i, 256), 256)
        d_out[:, :, :, cols] = dot(ot, dav[:, :, :, cols].reshape(1024, 256)).astype(BF).reshape(4, 4, 16, 256)

    jobs_out = [
        row_job(w, d_out, rd0, td0, qd0, s_out, 0, z, y, lsem.at[9]),
        row_job(w, d_out, rd1, td1, qd1, s_out, 1, z, y, lsem.at[10]),
    ]
    pump(jobs_out)

    g0, g1 = 1 - c, c
    waits = {}
    for no, g in enumerate((g0, g1)):
        kvt[...] = kv[g].reshape(2048, 128).T
        acc[...] = jnp.zeros_like(acc)
        for j in range(4):
            qj, doj = qp[g, j], do4[g, j]
            lse_row, delta_row = lse[g, pl.ds(j, 1), :], delta[g, pl.ds(j, 1), :]
            col = lanes((1, 512))
            place = (4 * j + y) * 128 + lax.rem(col, 128)
            start = jnp.where(place >= lens[g, 1], lens[g, 1], jnp.where(place >= lens[g, 0], lens[g, 0], 0))
            dqt[...] = jnp.zeros_like(dqt)

            @pl.loop(0, j + 1)
            def _(b):
                keys = kv[g, b].reshape(512, 128)
                at = 512 * b + lax.broadcasted_iota(jnp.int32, (512, 512), 0)
                ok = (at >= start) & (at <= place)
                pt = jnp.where(ok, jnp.exp(dott(keys, qj) - lse_row), 0.0)
                ds = (pt * (dott(keys, doj) - delta_row)).astype(BF)
                acc[b] += dot(ds, qj) + dot(pt.astype(BF), doj)
                dqt[...] += dot(kvt[:, pl.ds(pl.multiple_of(512 * b, 512), 512)], ds)

            dq = dqt[...].T
            rows = pl.ds(128 * j, 128)
            cs, sn = cos[g, rows, :], sin[g, rows, :]
            for t in range(2):
                v = pair_heads(dq[256 * t: 256 * t + 128], dq[256 * t + 128: 256 * t + 256], True) * (HD ** -0.5)
                dqkv[g, rows, 128 * t: 128 * t + 128] = (v * cs - swap_halves(v) * sn).astype(BF)
            if j == 1:
                if no == 0:
                    pump(jobs[:2])
                    pump([tail2])
                    pump(jobs[2:])
                else:
                    pump(jobs + jobs_out)
                    ends = [hand_out(w, s_gate, f_gate, c, x), hand_out(w, s_up, f_up, c, x),
                            transpose_zx(w, s_down, lambda zz: f_down, z, x, lsem.at[11])]
                    pump(ends)
        dkv_s[no] = acc[...].astype(BF).reshape(4, 4, 128, 128)
        waits[no] = others(w, y, "y", lambda p, no=no: dkv_s.at[no, :, p], dkv_r.at[no])
        if no == 0:
            pump(jobs_out)
    pump([tail2])

    @pl.loop(0, 8)
    def _(i):
        rows = pl.ds(pl.multiple_of(i * 16, 16), 16)
        v = h[rows, :] + s2v[x, rows, :].astype(F32) + fin2[0, rows, :].astype(F32) + fin2[1, rows, :].astype(F32)
        out[rows, :] = v.astype(BF)

    pump(jobs_out)
    tr_out = transpose_zx(w, s_out, lambda zz: f_out, z, x, lsem.at[12])
    pump([tr_out])

    state = {}
    for no, g in enumerate((g0, g1)):
        for a in waits[no]:
            w.got(*a)
        for j in range(4):
            rows = pl.ds(128 * j, 128)
            v = dkv_s[no, j, y].astype(F32)
            for k in range(3):
                v += dkv_r[no, k, j].astype(F32)
            turned = v * cos[g, rows, :] - swap_halves(v) * sin[g, rows, :]
            dqkv[g, rows, 256:384] = jnp.where(lanes(v.shape) < 64, turned, v).astype(BF)

        @pl.loop(0, 8)
        def _(i):
            wt = wqkv[i // 2, i % 2].reshape(256, 384)
            p4[g, :, :, pl.ds(pl.multiple_of(256 * i, 256), 256)] = dott(dqkv[g], wt).astype(BF).reshape(4, 128, 256)

        if no == 0:
            scatter8_core(w, p4, core_r, state)
    rs = scatter8_ring(w, p4, core_r, hop, fin, state)
    pump([rs])
    loads[2].wait()
    dv = dqkv[...].reshape(1024, 384)

    @pl.loop(0, 8)
    def _(i):
        cols = pl.ds(pl.multiple_of(256 * i, 256), 256)
        d_qkv[i // 2, i % 2] = dot(n1v[:, :, :, cols].reshape(1024, 256).T, dv).astype(BF).reshape(4, 4, 16, 384)

    jobs_qkv = [
        col_job(w, d_qkv, re0, te0, qe0, s_qkv, 0, z, y, lsem.at[13]),
        col_job(w, d_qkv, re1, te1, qe1, s_qkv, 1, z, y, lsem.at[14]),
    ]
    pump(jobs_qkv)
    pump([rs])
    pump(jobs_qkv)
    pump(jobs_qkv)
    end_qkv = hand_out(w, s_qkv, f_qkv, c, x)
    pump([end_qkv])
    pump([rs])

    @pl.loop(0, 8)
    def _(i):
        rows = pl.ds(pl.multiple_of(i * 16, 16), 16)
        e = p4[c, x, rows, :].astype(F32) + core_r[3, rows, :].astype(F32)
        e = e + fin[0, rows, :].astype(F32) + fin[1, rows, :].astype(F32)
        v = x_ref[rows, :].astype(F32)
        r = lax.rsqrt(jnp.mean(v * v, axis=1, keepdims=True) + EPS)
        gt[rows, :] = dh[rows, :] + r * e - v * (r * r * r * jnp.mean(e * v, axis=1, keepdims=True))

    pump(ends)
    pump([tr_out, end_qkv])
    w.drain()


def backward_attention(lens, da, dh, x, h, cos, sin, n1g, wqkv, wout, qp, kv, o, lse, s2, g_gate, g_up, g_down, cid):
    sds = jax.ShapeDtypeStruct
    vm, hb = pl.BlockSpec(memory_space=VMEM), pl.BlockSpec(memory_space=ANY)
    outs = [sds((128, 2048), BF), sds((128, 2048), F32), sds((8, 16, 768), BF), sds((8, 16, 768), BF),
            sds((8, 16, 384), BF), sds((48, 2048), BF), sds((16, 2048), BF)]
    b = lambda *s: VMEM(s, BF)
    r1 = [b(3, 4, 4, 16, 768)] * 4 + [b(3, 4, 48, 1024)] * 2 + [b(3, 4, 16, 1024)] * 2 + [b(3, 4, 4, 16, 384)] * 2
    t1 = [b(4, 4, 16, 768)] * 4 + [b(4, 48, 1024)] * 2 + [b(4, 16, 1024)] * 2 + [b(4, 4, 16, 384)] * 2
    r2 = [b(3, 4, 16, 768)] * 4 + [b(3, 48, 1024)] * 2 + [b(3, 16, 1024)] * 2 + [b(3, 4, 16, 384)] * 2
    return pl.pallas_call(
        m3_kernel,
        out_shape=outs,
        in_specs=[pl.BlockSpec(memory_space=pltpu.SMEM), hb] + [vm] * 5 + [hb] + [vm] * 6 + [hb] * 4,
        out_specs=[vm] * 7,
        scratch_shapes=[
            b(2, 4, 128, 2048), b(2, 4, 128, 2048), b(4, 128, 2048), b(2, 4, 512, 128), VMEM((2, 4, 512), F32),
            VMEM((4, 512, 128), F32), b(128, 2048), VMEM((128, 512), F32), b(2, 4, 4, 128, 128),
            b(2, 3, 4, 128, 128), b(2, 512, 384), b(2, 4, 128, 2048), b(4, 128, 2048), b(2, 64, 2048),
            b(2, 128, 2048), b(2, 64, 2048), b(2, 128, 2048), b(4, 2, 4, 4, 16, 384), b(4, 4, 16, 2048),
        ] + r1 + t1 + r2 + [
            b(2, 4, 16, 768), b(2, 4, 16, 768), b(2, 4, 16, 384), b(48, 2048), b(16, 2048),
            pltpu.SemaphoreType.DMA((130,)), pltpu.SemaphoreType.DMA((130,)), pltpu.SemaphoreType.DMA((15,)),
        ],
        compiler_params=comm_params(cid, 63),
        name="backward_attention",
    )(lens, da, dh, x, h, cos, sin, n1g, wqkv, wout, qp, kv, o, lse, s2, g_gate, g_up, g_down)


def local(tokens, lengths, attn_gain, w_query, w_key, w_value, w_out, mlp_gain, w_gate, w_up, w_down, cotangent):
    y = lax.axis_index("y")
    gain1 = attn_gain.astype(F32)[:, None]
    gain2 = mlp_gain.astype(F32)[:, None]
    fold = lambda w, g: (w.astype(F32) * g).astype(BF)
    ranks_first = lambda w: w.transpose(1, 0, 2)
    pad_ff = lambda w: jnp.pad(w.reshape(16, 8, 16, 44), ((0, 0), (0, 0), (0, 0), (0, 4))).reshape(16, 8, 768)
    twice = lambda w: jnp.repeat(w.reshape(16, 4, HD), 2, axis=1)
    qkv_s = ranks_first(jnp.concatenate(
        [fold(w_query, gain1).reshape(16, 8, 256), twice(fold(w_key, gain1)), twice(fold(w_value, gain1))], axis=2))
    gate_s, up_s = ranks_first(pad_ff(fold(w_gate, gain2))), ranks_first(pad_ff(fold(w_up, gain2)))
    down_s = jnp.pad(w_down, ((0, 4), (0, 0)))

    both = lax.all_gather(lengths, "core", axis=0, tiled=True)
    place = ((4 * jnp.arange(4)[:, None] + y) * 128 + jnp.arange(128)[None, :]).reshape(1, 512).astype(jnp.int32)
    c1, c2 = both[:, 0:1], both[:, 0:1] + both[:, 1:2]
    lens = jnp.concatenate([c1, c2], axis=1)
    start = jnp.where(place >= c2, c2, jnp.where(place >= c1, c1, 0))
    lane = jnp.arange(128) % 32
    frequency = jnp.exp(lane.astype(F32) * (-2.0 * math.log(THETA) / HD))
    sign = jnp.where(jnp.arange(128) % 64 < 32, -1.0, 1.0)
    angle = (place - start)[:, :, None].astype(F32) * frequency
    cos, sin = jnp.cos(angle), jnp.sin(angle) * sign

    h, n2, n1g, cg, qp, kv, o, lse, wqkv, wout, wgate, wup, wdown = forward_attention(
        lens, tokens, cos, sin, cotangent, qkv_s, w_out, gate_s, up_s, down_s, 1)
    dh, da, s2, g_gate, g_up, g_down = feed_forward(n2, h, cotangent, cg, wgate, wup, wdown, 2)
    output, grad_tokens, gate_s, up_s, qkv_s, down_s, out_s = backward_attention(
        lens, da, dh, tokens, h, cos, sin, n1g, wqkv, wout, qp, kv, o, lse, s2, g_gate, g_up, g_down, 3)

    wide = lambda v: v.astype(F32).transpose(1, 0, 2).reshape(16, -1)
    unpad = lambda v: v.reshape(16, 128, 48)[:, :, :44].reshape(16, 5632)
    g_gate, g_up = unpad(wide(gate_s)), unpad(wide(up_s))
    pair = lambda v: v.astype(F32).reshape(4, 2, 16, HD).sum(axis=1).transpose(1, 0, 2).reshape(16, -1)
    g_query, g_key, g_value = wide(qkv_s[..., :256]), pair(qkv_s[..., 256:320]), pair(qkv_s[..., 320:])
    rowdot = lambda w, gr: jnp.sum(w.astype(F32) * gr, axis=1)
    grad_attn_gain = rowdot(w_query, g_query) + rowdot(w_key, g_key) + rowdot(w_value, g_value)
    grad_mlp_gain = rowdot(w_gate, g_gate) + rowdot(w_up, g_up)
    return (output, grad_tokens, grad_attn_gain, gain1 * g_query, gain1 * g_key, gain1 * g_value,
            out_s.astype(F32), grad_mlp_gain, gain2 * g_gate, gain2 * g_up, down_s[:44].astype(F32))


def solution(mesh):
    fine = Mesh(mesh.devices.reshape(4, 2, 4, 4), ALL)
    rows, flat = P(ALL, None), P(ALL)
    in_specs = (rows, P(("z", "core"), None), flat, rows, rows, rows, rows, flat, rows, rows, rows, rows)
    out_specs = (rows, rows, flat, rows, rows, rows, rows, flat, rows, rows, rows)
    return jax.shard_map(local, mesh=fine, in_specs=in_specs, out_specs=out_specs, check_vma=False)
```

```python
import functools
import math

import jax
import jax.numpy as jnp
from jax import lax
from jax.experimental import pallas as pl
from jax.experimental.pallas import tpu as pltpu
from jax.sharding import Mesh
from jax.sharding import PartitionSpec as P

HEADS = 32
KV_HEADS = 4
HD = 64
EPS = 1e-05
THETA = 10000.0
NEG = -1e30
BF = jnp.bfloat16
F32 = jnp.float32
ANY = pl.ANY
VMEM = pltpu.VMEM
TP = ("x", "core")
DP = ("z", "y")
ALL = ("z", "core", "x", "y")


def tdot(a, b):
    return lax.dot_general(a, b, (((0,), (0,)), ((), ())), preferred_element_type=F32)


def dott(a, b):
    return lax.dot_general(a, b, (((1,), (1,)), ((), ())), preferred_element_type=F32)


def dot(a, b):
    return jnp.dot(a, b, preferred_element_type=F32)


class Wire:
    def __init__(self, ssem, rsem):
        self.ssem, self.rsem, self.sent = ssem, rsem, []

    def put(self, src, dst, k, to):
        cp = pltpu.make_async_remote_copy(
            src_ref=src, dst_ref=dst, send_sem=self.ssem.at[k], recv_sem=self.rsem.at[k],
            device_id=to, device_id_type=pl.DeviceIdType.MESH)
        cp.start()
        self.sent.append(cp)
        return cp

    def settle(self, copies):
        for cp in copies:
            cp.wait_send()
        done = {id(cp) for cp in copies}
        self.sent = [cp for cp in self.sent if id(cp) not in done]

    def got(self, dst, k, to):
        pltpu.make_async_remote_copy(
            src_ref=dst, dst_ref=dst, send_sem=self.ssem.at[k], recv_sem=self.rsem.at[k],
            device_id=to, device_id_type=pl.DeviceIdType.MESH).wait_recv()

    def drain(self):
        for cp in self.sent:
            cp.wait_send()


def greet(peers):
    barrier = pltpu.get_barrier_semaphore()
    for to in peers:
        pl.semaphore_signal(barrier, inc=1, device_id=to, device_id_type=pl.DeviceIdType.MESH)
    pl.semaphore_wait(barrier, len(peers))


def cx_ring():
    c, x = lax.axis_index("core"), lax.axis_index("x")
    right, left, opp = lax.rem(x + 1, 4), lax.rem(x + 3, 4), lax.rem(x + 2, 4)
    return c, x, right, left, opp, {"x": right}, {"x": left}, {"core": 1 - c}


def comm_params(cid, mb=None):
    kw = {} if mb is None else {"vmem_limit_bytes": mb << 20}
    return pltpu.CompilerParams(collective_id=cid, has_side_effects=True, **kw)


class Mail(Wire):
    def __init__(self, ssem, rsem):
        super().__init__(ssem, rsem)
        self.used = 0

    def new(self):
        self.used += 1
        return self.used - 1


def around(q):
    return lax.rem(q + 1, 4), lax.rem(q + 3, 4), lax.rem(q + 2, 4)


def ring(w, s, axis, q):
    right, left, opp = around(q)
    to_r, to_l = {axis: right}, {axis: left}
    k = [w.new() for _ in range(4)]
    w.put(s(q, None), s(q, None), k[0], to_r)
    w.put(s(q, None), s(q, None), k[1], to_l)
    yield
    w.got(s(left, None), k[0], to_l)
    w.put(s(left, 0), s(left, 0), k[2], to_r)
    w.got(s(right, None), k[1], to_r)
    w.put(s(right, 1), s(right, 1), k[3], to_l)
    yield
    w.got(s(opp, 0), k[2], to_l)
    w.got(s(opp, 1), k[3], to_r)


def col_flows(w, W, z, y):
    cut = lambda h: slice(None) if h is None else pl.ds(2 * h, 2)

    def first():
        yield from ring(w, lambda p, h: W.at[z, 0, cut(h), p], "y", y)
        yield from ring(w, lambda p, h: W.at[p, 0, cut(h)], "z", z)

    def second():
        yield from ring(w, lambda p, h: W.at[p, 1, cut(h), y], "z", z)
        yield from ring(w, lambda p, h: W.at[:, 1, cut(h), p], "y", y)

    return [first(), second()]


def row_flows(w, W, z, y):
    n = W.shape[-1] // 4
    cut = lambda b, h: pl.ds(2 * n * b, 2 * n) if h is None else pl.ds(2 * n * b + n * h, n)

    def first():
        yield from ring(w, lambda p, h: W.at[z, p, :, cut(0, h)], "y", y)
        yield from ring(w, lambda p, h: W.at[p, :, :, cut(0, h)], "z", z)

    def second():
        yield from ring(w, lambda p, h: W.at[p, y, :, cut(1, h)], "z", z)
        yield from ring(w, lambda p, h: W.at[:, p, :, cut(1, h)], "y", y)

    return [first(), second()]


def straight(w, stages):
    for s, axis, q in stages:
        ks = {}
        for k in (1, 3, 2):
            ks[k] = w.new()
            w.put(s(q), s(q), ks[k], {axis: lax.rem(q + k, 4)})
        yield
        for k in (1, 3, 2):
            frm = lax.rem(q + 4 - k, 4)
            w.got(s(frm), ks[k], {axis: frm})


def col_straight(w, W, z, y):
    return [straight(w, [(lambda p: W.at[z, 0, :, p], "y", y), (lambda p: W.at[p, 0], "z", z)]),
            straight(w, [(lambda p: W.at[p, 1, :, y], "z", z), (lambda p: W.at[:, 1, :, p], "y", y)])]


def row_straight(w, W, z, y):
    n = W.shape[-1] // 2
    a, b = pl.ds(0, n), pl.ds(n, n)
    return [straight(w, [(lambda p: W.at[z, p, :, a], "y", y), (lambda p: W.at[p, :, :, a], "z", z)]),
            straight(w, [(lambda p: W.at[p, y, :, b], "z", z), (lambda p: W.at[:, p, :, b], "y", y)])]


def pump(flows):
    for f in flows:
        next(f, None)


def gather8(w, src, dst):
    c, x, right, left, opp, to_r, to_l, to_c = cx_ring()
    rows = dst.shape[2]
    lo, hi = pl.ds(0, rows // 2), pl.ds(rows // 2, rows // 2)
    k = [w.new() for _ in range(10)]
    out = []
    out += [w.put(src.at[lo], dst.at[c, x, lo], k[0], to_r)]
    out += [w.put(src.at[hi], dst.at[c, x, hi], k[1], to_l)]
    out += [w.put(src.at[hi], dst.at[c, x, hi], k[2], to_r)]
    out += [w.put(src.at[lo], dst.at[c, x, lo], k[3], to_l)]
    out += [w.put(src, dst.at[c, x], k[4], to_c)]
    yield
    w.got(dst.at[c, left, lo], k[0], to_l)
    out += [w.put(dst.at[c, left, lo], dst.at[c, left, lo], k[5], to_r)]
    w.got(dst.at[c, right, hi], k[1], to_r)
    out += [w.put(dst.at[c, right, hi], dst.at[c, right, hi], k[6], to_l)]
    yield
    w.got(dst.at[c, left, hi], k[2], to_l)
    out += [w.put(dst.at[c, left], dst.at[c, left], k[7], to_c)]
    w.got(dst.at[c, right, lo], k[3], to_r)
    out += [w.put(dst.at[c, right], dst.at[c, right], k[8], to_c)]
    yield
    w.got(dst.at[c, opp, lo], k[5], to_l)
    w.got(dst.at[c, opp, hi], k[6], to_r)
    out += [w.put(dst.at[c, opp], dst.at[c, opp], k[9], to_c)]
    yield
    w.got(dst.at[1 - c, x], k[4], to_c)
    w.got(dst.at[1 - c, left], k[7], to_c)
    w.got(dst.at[1 - c, right], k[8], to_c)
    w.got(dst.at[1 - c, opp], k[9], to_c)
    w.settle(out)


def add_to(dst, other, r0, rows, step=16):
    @pl.loop(0, rows // step)
    def _(i):
        a = pl.ds(pl.multiple_of(r0 + i * step, step), step)
        b = pl.ds(pl.multiple_of(i * step, step), step)
        dst[a, :] = (dst[a, :].astype(F32) + other[b, :].astype(F32)).astype(dst.dtype)


def scatter8_core(w, p, core_r, state):
    c, x, right, left, opp, to_r, to_l, to_c = cx_ring()
    state["k"] = [w.new() for _ in range(4)]
    state["out"] = [
        w.put(p.at[1 - c, xx], core_r.at[i], state["k"][i], to_c) for i, xx in enumerate((opp, right, left, x))]


def scatter8_ring(w, p, core_r, hop, fin, state):
    c, x, right, left, opp, to_r, to_l, to_c = cx_ring()
    rows = p.shape[2]
    half = rows // 2
    lo, hi = pl.ds(0, half), pl.ds(half, half)
    kc, out = state["k"], state["out"]
    k = [w.new() for _ in range(6)]
    w.got(core_r.at[0], kc[0], to_c)
    add_to(p.at[c, opp], core_r.at[0], 0, rows)
    out += [w.put(p.at[c, opp, lo], hop.at[0], k[0], to_r)]
    out += [w.put(p.at[c, opp, hi], hop.at[1], k[1], to_l)]
    w.got(core_r.at[1], kc[1], to_c)
    add_to(p.at[c, right], core_r.at[1], 0, rows)
    out += [w.put(p.at[c, right, hi], fin.at[0, hi], k[2], to_r)]
    w.got(core_r.at[2], kc[2], to_c)
    add_to(p.at[c, left], core_r.at[2], 0, rows)
    out += [w.put(p.at[c, left, lo], fin.at[1, lo], k[3], to_l)]
    yield
    w.got(hop.at[0], k[0], to_l)
    add_to(p.at[c, right], hop.at[0], 0, half)
    out += [w.put(p.at[c, right, lo], fin.at[0, lo], k[4], to_r)]
    w.got(hop.at[1], k[1], to_r)
    add_to(p.at[c, left], hop.at[1], half, half)
    out += [w.put(p.at[c, left, hi], fin.at[1, hi], k[5], to_l)]
    yield
    w.got(core_r.at[3], kc[3], to_c)
    w.got(fin.at[0, hi], k[2], to_l)
    w.got(fin.at[1, lo], k[3], to_r)
    w.got(fin.at[0, lo], k[4], to_l)
    w.got(fin.at[1, hi], k[5], to_r)
    w.settle(out)


def lanes(shape):
    return lax.broadcasted_iota(jnp.int32, shape, len(shape) - 1)


def swap_halves(u):
    first = lax.rem(lanes(u.shape), 64) < 32
    return jnp.where(first, pltpu.roll(u, 96, u.ndim - 1), pltpu.roll(u, 32, u.ndim - 1))


def entry(peers, extra=None):
    barrier = pltpu.get_barrier_semaphore()
    for to in peers:
        pl.semaphore_signal(barrier, inc=1, device_id=to, device_id_type=pl.DeviceIdType.MESH)
    if extra is None:
        pl.semaphore_wait(barrier, len(peers))
        return
    more, to = extra

    @pl.when(more)
    def _():
        pl.semaphore_signal(barrier, inc=1, device_id=to, device_id_type=pl.DeviceIdType.MESH)
        pl.semaphore_wait(barrier, len(peers) + 1)

    @pl.when(jnp.logical_not(more))
    def _():
        pl.semaphore_wait(barrier, len(peers))


def tp_peers(c, x):
    r = 2 * x + c
    out = []
    for k in range(1, 8):
        rr = lax.rem(r + k, 8)
        out.append((rr, {"x": rr // 2, "core": lax.rem(rr, 2)}))
    return out


def spread(w, src, W, z, c, x, y, local_sem):
    ks = [w.new() for _ in range(7)]
    for k, (rr, to) in zip(ks, tp_peers(c, x)):
        w.put(src.at[rr], W.at[z, c, x, y], k, to)
    own = pltpu.make_async_copy(src.at[2 * x + c], W.at[z, c, x, y], local_sem)
    own.start()
    yield
    r = 2 * x + c
    for i, k in enumerate(ks):
        rr = lax.rem(r + 7 - i, 8)
        w.got(W.at[z, lax.rem(rr, 2), rr // 2, y], k, {"x": rr // 2, "core": lax.rem(rr, 2)})
    own.wait()


def transpose_zx(w, src, dst_of, z, x, local_sem):
    k = w.new()
    to = {"z": x, "x": z}

    def far():
        return pltpu.make_async_remote_copy(
            src_ref=src, dst_ref=dst_of(x), send_sem=w.ssem.at[k], recv_sem=w.rsem.at[k],
            device_id=to, device_id_type=pl.DeviceIdType.MESH)

    def near():
        return pltpu.make_async_copy(src, dst_of(x), local_sem)

    @pl.when(z != x)
    def _():
        far().start()

    @pl.when(z == x)
    def _():
        near().start()

    yield

    @pl.when(z != x)
    def _():
        far().wait_send()
        w.got(dst_of(z), k, to)

    @pl.when(z == x)
    def _():
        near().wait()


def attend(q, keys, j, y, c1, c2):
    m, n = q.shape[0], keys.shape[0]
    s = dott(q, keys)
    row = lax.broadcasted_iota(jnp.int32, (m, 1), 0)
    place = (4 * j + y) * 128 + lax.rem(row, 128)
    start = jnp.where(place >= c2, c2, jnp.where(place >= c1, c1, 0))
    at = lax.broadcasted_iota(jnp.int32, (m, n), 1)
    s = jnp.where((at >= start) & (at <= place), s, NEG)
    top = jnp.max(s, axis=1, keepdims=True)
    e = jnp.exp(s - top)
    total = jnp.sum(e, axis=1, keepdims=True)
    return dot(e.astype(BF), keys) / total, top + jnp.log(total)


def pair_heads(first, second, lower):
    low = lanes(first.shape) < 64
    if lower:
        return jnp.where(low, first, pltpu.roll(second, 64, 1))
    return jnp.where(low, pltpu.roll(first, 64, 1), second)


def forward_kernel(lens, x_ref, cos_in, sin_in, cot, qkv_s, out_s, gate_s, up_s, down_s,
                   h_out, n1_out, qp_out, kv_out, o_out, lse_out, wqkv_out, wout_out,
                   dh_out, da_out, s2, g_gate, g_up, g_down, r1_down,
                   cos, sin, h, qp, kv, o, lse, wqkv, wout, n1, cv, wg, wu, wd, p, core_r, hop, fin,
                   dact, a_all, dg_all, du_all, core2, d_down, ssem, rsem, lsem, osem):
    z, c, x, y = (lax.axis_index(a) for a in ALL)
    peers = [to for _, to in tp_peers(c, x)]
    for axis, q in (("y", y), ("z", z)):
        peers += [{axis: lax.rem(q + k, 4)} for k in (1, 2, 3)]
    entry(peers, (z != x, {"z": x, "x": z}))
    w = Mail(ssem, rsem)
    saved = []

    def save(src, dst):
        cp = pltpu.make_async_copy(src, dst, osem.at[len(saved)])
        cp.start()
        saved.append(cp)
        return cp

    sp_qkv = spread(w, qkv_s, wqkv, z, c, x, y, lsem.at[0])
    pump([sp_qkv])

    @pl.loop(0, 8)
    def _(i):
        rows = pl.ds(pl.multiple_of(i * 16, 16), 16)
        v = x_ref[rows, :].astype(F32)
        n1[c, x, rows, :] = (v * lax.rsqrt(jnp.mean(v * v, axis=1, keepdims=True) + EPS)).astype(BF)

    ag_n1 = gather8(w, n1.at[c, x], n1)
    pump([ag_n1])
    tr_out = transpose_zx(w, out_s, lambda zz: wout.at[zz, y], z, x, lsem.at[1])
    pump([tr_out])
    tables = [pltpu.make_async_copy(cos_in, cos, lsem.at[5]), pltpu.make_async_copy(sin_in, sin, lsem.at[6])]
    for cp in tables:
        cp.start()
    pump([sp_qkv])
    fl_qkv = col_straight(w, wqkv, z, y)
    pump(fl_qkv)
    pump([ag_n1])
    pump(fl_qkv)
    pump([tr_out])
    fl_out = row_straight(w, wout, z, y)
    pump(fl_out)
    pump([ag_n1])
    pump(fl_out)
    pump([ag_n1])
    pump(fl_qkv)
    pump([ag_n1])
    for cp in tables:
        cp.wait()
    weights = wqkv[...].reshape(2048, 384)

    def project(g, keys_too):
        u = dot(n1[g].reshape(512, 2048), weights)
        cs, sn = cos[g], sin[g]
        if keys_too:
            v = u[:, 256:384]
            turned = jnp.where(lanes(v.shape) < 64, v * cs + swap_halves(v) * sn, v)
            kv[g, :, y] = turned.astype(BF).reshape(4, 128, 128)
        for t in range(2):
            v = u[:, 128 * t: 128 * t + 128]
            v = (v * cs + swap_halves(v) * sn) * (HD ** -0.5)
            low = lanes(v.shape) < 64
            for b, head in enumerate((v, pltpu.roll(v, 64, 1))):
                rows = pl.ds(128 * (2 * t + b), 128)
                qp[g, :, rows, :] = jnp.where(low, head, 0.0).astype(BF).reshape(4, 128, 128)

    g0, g1 = 1 - c, c
    to_c = {"core": 1 - c}
    project(g0, True)
    fl_kv = [straight(w, [(lambda pp: kv.at[g0, :, pp], "y", y)])]
    pump(fl_kv)
    spreads = [spread(w, gate_s, wg, z, c, x, y, lsem.at[2]), spread(w, up_s, wu, z, c, x, y, lsem.at[3]),
               transpose_zx(w, down_s, lambda zz: wd.at[zz, y], z, x, lsem.at[4])]
    pump(spreads)
    project(g1, False)
    keep_n1 = save(n1, n1_out)
    save(wqkv, wqkv_out)
    keep_cot = save(cot, cv.at[c, x])
    pump(fl_out)
    pump(fl_kv)
    k_kv = w.new()
    w.put(kv.at[g0], kv.at[g0], k_kv, to_c)
    pump(spreads)
    fl_mlp = col_flows(w, wg, z, y) + col_flows(w, wu, z, y) + row_flows(w, wd, z, y)
    pump(fl_mlp)
    ag_cot = gather8(w, cot, cv)
    pump([ag_cot])

    state = {}
    out_w = wout[...].reshape(256, 2048)
    for turn_no, g in enumerate((g0, g1)):
        if turn_no == 1:
            w.got(kv.at[g], k_kv, to_c)
            save(kv, kv_out)
            save(qp, qp_out)
            save(wout, wout_out)
        for j in range(4):
            n = 512 * (j + 1)
            keys = kv[g, 0:j + 1].reshape(n, 128)
            for t in range(2):
                res, total = attend(qp[g, j, 256 * t: 256 * t + 256], keys, j, y, lens[g, 0], lens[g, 1])
                both = pair_heads(res[:128], res[128:], False)
                o[g, pl.ds(128 * j, 128), 128 * t: 128 * t + 128] = both.astype(BF)
                lse[g, pl.ds(j, 1), 256 * t: 256 * t + 256] = jnp.broadcast_to(total, (256, 128)).T[0:1, :]
            if turn_no == 0 and j == 2:
                pump(fl_mlp)
        pump([ag_cot])

        @pl.loop(0, 4)
        def _(i):
            p[g, i] = dot(o[g, pl.ds(pl.multiple_of(128 * i, 128), 128), :], out_w).astype(BF)

        if turn_no == 0:
            keep_n1.wait()
            scatter8_core(w, p, core_r, state)
            pump(fl_mlp)
            pump([ag_cot])
    rs = scatter8_ring(w, p, core_r, hop, fin, state)
    pump([rs])
    pump([ag_cot])
    save(o, o_out)
    save(lse, lse_out)
    pump([rs])
    pump([ag_cot])
    pump([rs])

    @pl.loop(0, 8)
    def _(i):
        rows = pl.ds(pl.multiple_of(i * 16, 16), 16)
        v = x_ref[rows, :].astype(F32) + p[c, x, rows, :].astype(F32) + core_r[3, rows, :].astype(F32)
        v = v + fin[0, rows, :].astype(F32) + fin[1, rows, :].astype(F32)
        h[rows, :] = v
        n1[c, x, rows, :] = (v * lax.rsqrt(jnp.mean(v * v, axis=1, keepdims=True) + EPS)).astype(BF)

    keep_h = save(h, h_out)
    n2v = n1
    ag = gather8(w, n2v.at[c, x], n2v)
    pump([ag])
    pump(fl_mlp)
    pump([ag])
    pump([ag])
    pump([ag])
    pump(fl_mlp)
    keep_cot.wait()
    down = wd[...].reshape(768, 2048)

    @pl.loop(0, 2)
    def _(g):
        for t in range(2):
            dact[g, pl.ds(256 * t, 256), :] = dott(cv[g, 2 * t: 2 * t + 2].reshape(256, 2048), down).astype(BF)

    gate, up = wg[...].reshape(2048, 768), wu[...].reshape(2048, 768)
    pump([ag])

    def half(g):
        @pl.loop(0, 2)
        def _(t):
            rows = pl.ds(pl.multiple_of(256 * t, 256), 256)
            xv = n2v[g, pl.ds(2 * t, 2)].reshape(256, 2048)
            gp, u = dot(xv, gate), dot(xv, up)
            sig = jax.nn.sigmoid(gp)
            act = gp * sig
            d = dact[g, rows, :].astype(F32)
            a_all[g, rows, :] = (act * u).astype(BF)
            dg_all[g, rows, :] = (d * u * sig * (1.0 + gp * (1.0 - sig))).astype(BF)
            du_all[g, rows, :] = (d * act).astype(BF)

        @pl.loop(0, 8)
        def _(i):
            part = dott(dg_all[g], wg[i // 2, i % 2].reshape(256, 768))
            part += dott(du_all[g], wu[i // 2, i % 2].reshape(256, 768))
            p[g, :, :, pl.ds(pl.multiple_of(256 * i, 256), 256)] = part.astype(BF).reshape(4, 128, 256)

    st3, st2 = {}, {}
    half(g0)
    scatter8_core(w, p, core_r, st3)
    half(g1)
    rs3 = scatter8_ring(w, p, core_r, hop, fin, st3)
    pump([rs3])

    at = a_all[...].reshape(1024, 768).T

    @pl.loop(0, 8)
    def _(i):
        cols = pl.ds(pl.multiple_of(256 * i, 256), 256)
        d_down[:, :, :, cols] = dot(at, cv[:, :, :, cols].reshape(1024, 256)).astype(BF).reshape(4, 4, 48, 256)

    left, right_cols = pl.ds(0, 1024), pl.ds(1024, 1024)
    landed = others(w, y, "y", lambda pp: d_down.at[:, pp, :, left], r1_down.at[0])
    landed += others(w, z, "z", lambda pp: d_down.at[pp, :, :, right_cols], r1_down.at[1])
    save(d_down, g_down)

    p2 = cv

    def out_part(g):
        @pl.loop(0, 8)
        def _(i):
            cols = pl.ds(pl.multiple_of(256 * i, 256), 256)
            p2[g, :, :, cols] = dot(a_all[g], wd[:, :, :, cols].reshape(768, 256)).astype(BF).reshape(4, 128, 256)

    out_part(g0)
    scatter8_core(w, p2, core2, st2)
    out_part(g1)
    pump([rs3])

    dg, du = dg_all[...].reshape(1024, 768), du_all[...].reshape(1024, 768)

    def stage(i, k):
        rows = pl.ds(256 * k, 256)
        return pltpu.make_async_copy(dact.at[i % 2, rows], (g_gate, g_up)[k].at[i], lsem.at[7 + 2 * (i % 2) + k])

    for i in range(8):
        t = n2v[:, :, :, 256 * i: 256 * i + 256].reshape(1024, 256).T
        if i >= 2:
            stage(i - 2, 0).wait()
            stage(i - 2, 1).wait()
        dact[i % 2, 0:256, :] = dot(t, dg).astype(BF)
        dact[i % 2, 256:512, :] = dot(t, du).astype(BF)
        stage(i, 0).start()
        stage(i, 1).start()

    cc, xx, right, left, opp, to_r, to_l, to_c = cx_ring()
    for i, b in enumerate((opp, right, left, x)):
        w.got(core2.at[i], st2["k"][i], to_c)
        add_to(p2.at[c, b], core2.at[i], 0, 128)
    save(p2.at[c], s2)
    pump([rs3])
    keep_h.wait()

    @pl.loop(0, 8)
    def _(i):
        rows = pl.ds(pl.multiple_of(i * 16, 16), 16)
        e = p[c, x, rows, :].astype(F32) + core_r[3, rows, :].astype(F32)
        e = e + fin[0, rows, :].astype(F32) + fin[1, rows, :].astype(F32)
        v = h[rows, :]
        r = lax.rsqrt(jnp.mean(v * v, axis=1, keepdims=True) + EPS)
        out = cot[rows, :].astype(F32) + r * e - v * (r * r * r * jnp.mean(e * v, axis=1, keepdims=True))
        h[rows, :] = out
        n1[c, x, rows, :] = out.astype(BF)

    save(h, dh_out)
    save(n1.at[c, x], da_out)
    w.drain()
    for i in (6, 7):
        stage(i, 0).wait()
        stage(i, 1).wait()
    for a in landed:
        w.got(*a)
    for cp in saved:
        if all(cp is not a for a in (keep_n1, keep_h, keep_cot)):
            cp.wait()


def forward_layer(lens, tokens, cos, sin, cot, qkv_s, out_s, gate_s, up_s, down_s, cid):
    sds = jax.ShapeDtypeStruct
    vm, hb = pl.BlockSpec(memory_space=VMEM), pl.BlockSpec(memory_space=ANY)
    col, big = (4, 2, 4, 4, 16, 768), (2, 4, 128, 2048)
    row = (128, 2048)
    mid = [((2, 4, 512, 128), BF), ((2, 4, 4, 128, 128), BF), ((2, 512, 256), BF), ((2, 4, 512), F32),
           ((4, 2, 4, 4, 16, 384), BF), ((4, 4, 16, 2048), BF)]
    outs = [(row, F32), (big, BF)] + mid + [
        (row, F32), (row, BF), ((4, 128, 2048), BF), ((8, 256, 768), BF), ((8, 256, 768), BF), ((4, 4, 48, 2048), BF),
        ((2, 3, 4, 48, 1024), BF)]
    scratch = [((2, 512, 128), F32)] * 2 + [(row, F32)] + mid + [
        (big, BF), (big, BF), (col, BF), (col, BF), ((4, 4, 48, 2048), BF),
        (big, BF), ((4, 128, 2048), BF), ((2, 64, 2048), BF), ((2, 128, 2048), BF),
        ((2, 512, 768), BF), ((2, 512, 768), BF), ((2, 512, 768), BF), ((2, 512, 768), BF),
        ((4, 128, 2048), BF), ((4, 4, 48, 2048), BF)]
    return pl.pallas_call(
        forward_kernel,
        out_shape=[sds(*a) for a in outs],
        in_specs=[pl.BlockSpec(memory_space=pltpu.SMEM), vm, hb, hb, vm] + [hb] * 5,
        out_specs=[hb] * len(outs),
        scratch_shapes=[VMEM(*a) for a in scratch] + [
            pltpu.SemaphoreType.DMA((170,)), pltpu.SemaphoreType.DMA((170,)), pltpu.SemaphoreType.DMA((13,)),
            pltpu.SemaphoreType.DMA((16,)),
        ],
        compiler_params=comm_params(cid, 63),
        name="forward_layer",
    )(lens, tokens, cos, sin, cot, qkv_s, out_s, gate_s, up_s, down_s)


def ring_tail(w, s, hop, fin):
    c, x, right, left, opp, to_r, to_l, to_c = cx_ring()
    half = s.shape[1] // 2
    lo, hi = pl.ds(0, half), pl.ds(half, half)
    k = [w.new() for _ in range(6)]
    w.put(s.at[opp, lo], hop.at[0], k[0], to_r)
    w.put(s.at[opp, hi], hop.at[1], k[1], to_l)
    w.put(s.at[right, hi], fin.at[0, hi], k[2], to_r)
    w.put(s.at[left, lo], fin.at[1, lo], k[3], to_l)
    yield
    w.got(hop.at[0], k[0], to_l)
    add_to(s.at[right], hop.at[0], 0, half)
    w.put(s.at[right, lo], fin.at[0, lo], k[4], to_r)
    w.got(hop.at[1], k[1], to_r)
    add_to(s.at[left], hop.at[1], half, half)
    w.put(s.at[left, hi], fin.at[1, hi], k[5], to_l)
    yield
    w.got(fin.at[0, hi], k[2], to_l)
    w.got(fin.at[1, lo], k[3], to_r)
    w.got(fin.at[0, lo], k[4], to_l)
    w.got(fin.at[1, hi], k[5], to_r)


def others(w, q, axis, piece, recv):
    ks = {}
    for k in (1, 3, 2):
        to = lax.rem(q + k, 4)
        ks[k] = w.new()
        w.put(piece(to), recv.at[k - 1], ks[k], {axis: to})
    return [(recv.at[k - 1], ks[k], {axis: lax.rem(q + 4 - k, 4)}) for k in (1, 3, 2)]


def sum_four(dst, own, recv, lead):
    total = math.prod(lead)

    @pl.loop(0, total)
    def _(i):
        at = (i,) if len(lead) == 1 else (i // lead[1], lax.rem(i, lead[1]))
        acc = own[at].astype(F32)
        for k in range(3):
            acc += recv[(k,) + at].astype(F32)
        dst[at] = acc.astype(dst.dtype)


def col_job(w, src, r1, t, r2, s, e, z, y, lsem):
    if e == 0:
        own, piece1, ax1, q1 = src.at[:, 0, :, y], lambda p: src.at[:, 0, :, p], "y", y
        piece2, ax2, q2 = lambda p: t.at[p], "z", z
    else:
        own, piece1, ax1, q1 = src.at[z, 1], lambda p: src.at[p, 1], "z", z
        piece2, ax2, q2 = lambda p: t.at[:, p], "y", y
    first = pltpu.make_async_copy(own, t, lsem)
    first.start()
    waits = others(w, q1, ax1, piece1, r1)
    yield
    first.wait()
    for a in waits:
        w.got(*a)
    sum_four(t, t, r1, (4, 4))
    waits = others(w, q2, ax2, piece2, r2)
    yield
    for a in waits:
        w.got(*a)
    sum_four(s.at[e], piece2(q2), r2, (4,))


def row_job(w, src, r1, t, r2, s, e, z, y, lsem, here=None):
    n = s.shape[-1] // 2
    rows = s.shape[0]
    cols = pl.ds(e * n, n)
    if len(src.shape) == 5:
        at = lambda *q: src.at[(e,) + q]
    else:
        at = lambda *q: src.at[q + (slice(None), cols)]
    if e == 0:
        piece1, ax1, q1, ax2, q2 = lambda p: at(slice(None), p), "y", y, "z", z
    else:
        piece1, ax1, q1, ax2, q2 = lambda p: at(p, slice(None)), "z", z, "y", y
    own = piece1(q1)
    first = pltpu.make_async_copy(own, t, lsem)
    first.start()
    waits = others(w, q1, ax1, piece1, r1) if here is None else []
    yield
    first.wait()
    for a in waits:
        w.got(*a)
    sum_four(t, t, r1, (4,))
    waits = others(w, q2, ax2, lambda p: t.at[p], r2)
    yield
    for a in waits:
        w.got(*a)

    @pl.loop(0, rows // 16)
    def _(i):
        at = pl.ds(pl.multiple_of(i * 16, 16), 16)
        acc = t[q2, at].astype(F32)
        for k in range(3):
            acc += r2[k, at].astype(F32)
        s[at, cols] = acc.astype(BF)


def hand_out(w, s, f, c, x):
    r = 2 * x + c
    ks = [w.new() for _ in range(7)]
    for k, (rr, to) in zip(ks, tp_peers(c, x)):
        w.put(s.at[lax.rem(rr, 2), rr // 2], f.at[r], k, to)
    f[r] = s[c, x]
    yield
    for i, k in enumerate(ks):
        rr = lax.rem(r + 7 - i, 8)
        w.got(f.at[rr], k, {"x": rr // 2, "core": lax.rem(rr, 2)})


def m3_kernel(lens, da, dh, x_ref, h, cos, sin, n1g, wqkv, wout, qp, kv, o, lse, s2, g_gate, g_up, g_down, r1_down,
              out, gt, f_gate, f_up, f_q, f_kv, f_down, f_out,
              dav, n1v, s2v, do4, delta, acc, kvt, dqt, dkv_s, dkv_r, dqkv, p4, core_r, hop, fin, hop2, fin2,
              d_q, d_kv, d_out,
              ra0, ra1, rb0, rb1, rc, rd0, rd1, re0, re1, rf0, rf1,
              ta0, ta1, tb0, tb1, tc0, tc1, td0, td1, te0, te1, tf0, tf1,
              qa0, qa1, qb0, qb1, qc0, qc1, qd0, qd1, qe0, qe1, qf0, qf1,
              s_gate, s_up, s_q, s_kv, s_down, s_out, ssem, rsem, lsem):
    z, c, x, y = (lax.axis_index(a) for a in ALL)
    peers = [to for _, to in tp_peers(c, x)]
    for axis, q in (("y", y), ("z", z)):
        peers += [{axis: lax.rem(q + k, 4)} for k in (1, 2, 3)]
    entry(peers, (z != x, {"z": x, "x": z}))
    w = Mail(ssem, rsem)
    ag = gather8(w, da, dav)
    pump([ag])
    loads = [pltpu.make_async_copy(a, b, lsem.at[i]) for i, (a, b) in enumerate(
        ((da, dav.at[c, x]), (s2, s2v), (n1g, n1v), (r1_down, rc)))]
    for cp in loads:
        cp.start()
    jobs_down = [
        row_job(w, g_down, rc.at[0], tc0, qc0, s_down, 0, z, y, lsem.at[7], loads[3]),
        row_job(w, g_down, rc.at[1], tc1, qc1, s_down, 1, z, y, lsem.at[8], loads[3]),
    ]
    jobs = [
        col_job(w, g_gate, ra0, ta0, qa0, s_gate, 0, z, y, lsem.at[4]),
        col_job(w, g_gate, ra1, ta1, qa1, s_gate, 1, z, y, lsem.at[5]),
        col_job(w, g_up, rb0, tb0, qb0, s_up, 0, z, y, lsem.at[6]),
        col_job(w, g_up, rb1, tb1, qb1, s_up, 1, z, y, lsem.at[9]),
    ]
    pump(jobs_down)
    pump(jobs)
    pump([ag])
    loads[0].wait()
    pump([ag])
    pump([ag])
    loads[1].wait()
    loads[3].wait()
    tail2 = ring_tail(w, s2v, hop2, fin2)
    pump([tail2])
    pump([ag])

    ow = wout[...].reshape(256, 2048)
    for g in range(2):
        dv = dott(dav[g].reshape(512, 2048), ow).astype(BF).astype(F32)
        ov = o[g].astype(F32)
        for t in range(2):
            v = dv[:, 128 * t: 128 * t + 128]
            pr = v * ov[:, 128 * t: 128 * t + 128]
            low = lanes(v.shape) < 64
            for b, head in enumerate((pltpu.roll(v, 64, 1), v)):
                rows = pl.ds(128 * (2 * t + b), 128)
                do4[g, :, rows, :] = jnp.where(low, 0.0, head).astype(BF).reshape(4, 128, 128)
                total = jnp.sum(jnp.where(low == (b == 0), pr, 0.0), axis=1, keepdims=True)
                total = jnp.broadcast_to(total, (512, 128)).T
                for j in range(4):
                    delta[g, pl.ds(j, 1), rows] = total[0:1, 128 * j: 128 * j + 128]

    ot = o[...].reshape(1024, 256).T

    @pl.loop(0, 8)
    def _(i):
        cols = pl.ds(pl.multiple_of(256 * i, 256), 256)
        d_out[:, :, :, cols] = dot(ot, dav[:, :, :, cols].reshape(1024, 256)).astype(BF).reshape(4, 4, 16, 256)

    jobs_out = [
        row_job(w, d_out, rd0, td0, qd0, s_out, 0, z, y, lsem.at[10]),
        row_job(w, d_out, rd1, td1, qd1, s_out, 1, z, y, lsem.at[11]),
    ]
    pump(jobs_out)

    g0, g1 = 1 - c, c
    waits = {}
    for no, g in enumerate((g0, g1)):
        kvt[...] = kv[g].reshape(2048, 128).T
        acc[...] = jnp.zeros_like(acc)
        for j in range(4):
            qj, doj = qp[g, j], do4[g, j]
            lse_row, delta_row = lse[g, pl.ds(j, 1), :], delta[g, pl.ds(j, 1), :]
            col = lanes((1, 512))
            place = (4 * j + y) * 128 + lax.rem(col, 128)
            start = jnp.where(place >= lens[g, 1], lens[g, 1], jnp.where(place >= lens[g, 0], lens[g, 0], 0))
            dqt[...] = jnp.zeros_like(dqt)

            @pl.loop(0, j + 1)
            def _(b):
                keys = kv[g, b].reshape(512, 128)
                at = 512 * b + lax.broadcasted_iota(jnp.int32, (512, 512), 0)
                ok = (at >= start) & (at <= place)
                pt = jnp.where(ok, jnp.exp(dott(keys, qj) - lse_row), 0.0)
                ds = (pt * (dott(keys, doj) - delta_row)).astype(BF)
                acc[b] += dot(ds, qj) + dot(pt.astype(BF), doj)
                dqt[...] += dot(kvt[:, pl.ds(pl.multiple_of(512 * b, 512), 512)], ds)

            dq = dqt[...].T
            rows = pl.ds(128 * j, 128)
            cs, sn = cos[g, rows, :], sin[g, rows, :]
            for t in range(2):
                v = pair_heads(dq[256 * t: 256 * t + 128], dq[256 * t + 128: 256 * t + 256], True) * (HD ** -0.5)
                dqkv[g, rows, 128 * t: 128 * t + 128] = (v * cs - swap_halves(v) * sn).astype(BF)
            if no == 0 and j == 2:
                pump([tail2])
            if no == 1 and j == 2:
                pump(jobs_out)
        dkv_s[no] = acc[...].astype(BF).reshape(4, 4, 128, 128)
        waits[no] = others(w, y, "y", lambda p, no=no: dkv_s.at[no, :, p], dkv_r.at[no])
        if no == 0:
            pump(jobs_down)
            pump(jobs)
    pump(jobs)
    ends = [hand_out(w, s_gate, f_gate, c, x), hand_out(w, s_up, f_up, c, x)]
    pump(ends)
    pump([tail2])
    loads[2].wait()
    dv = dqkv[:, :, 0:256].reshape(1024, 256)

    @pl.loop(0, 8)
    def _(i):
        cols = pl.ds(pl.multiple_of(256 * i, 256), 256)
        d_q[i // 2, i % 2] = dot(n1v[:, :, :, cols].reshape(1024, 256).T, dv).astype(BF).reshape(4, 4, 16, 256)

    jobs_q = [
        col_job(w, d_q, re0, te0, qe0, s_q, 0, z, y, lsem.at[12]),
        col_job(w, d_q, re1, te1, qe1, s_q, 1, z, y, lsem.at[13]),
    ]
    pump(jobs_q)

    state = {}
    for no, g in enumerate((g0, g1)):
        for a in waits[no]:
            w.got(*a)
        for j in range(4):
            rows = pl.ds(128 * j, 128)
            v = dkv_s[no, j, y].astype(F32)
            for k in range(3):
                v += dkv_r[no, k, j].astype(F32)
            turned = v * cos[g, rows, :] - swap_halves(v) * sin[g, rows, :]
            dqkv[g, rows, 256:384] = jnp.where(lanes(v.shape) < 64, turned, v).astype(BF)

        @pl.loop(0, 8)
        def _(i):
            wt = wqkv[i // 2, i % 2].reshape(256, 384)
            p4[g, :, :, pl.ds(pl.multiple_of(256 * i, 256), 256)] = dott(dqkv[g], wt).astype(BF).reshape(4, 128, 256)

        if no == 0:
            scatter8_core(w, p4, core_r, state)
    rs = scatter8_ring(w, p4, core_r, hop, fin, state)
    pump([rs])
    dv = dqkv[:, :, 256:384].reshape(1024, 128)

    @pl.loop(0, 8)
    def _(i):
        cols = pl.ds(pl.multiple_of(256 * i, 256), 256)
        d_kv[i // 2, i % 2] = dot(n1v[:, :, :, cols].reshape(1024, 256).T, dv).astype(BF).reshape(4, 4, 16, 128)

    jobs_kv = [
        col_job(w, d_kv, rf0, tf0, qf0, s_kv, 0, z, y, lsem.at[14]),
        col_job(w, d_kv, rf1, tf1, qf1, s_kv, 1, z, y, lsem.at[15]),
    ]
    pump(jobs_kv)

    @pl.loop(0, 8)
    def _(i):
        rows = pl.ds(pl.multiple_of(i * 16, 16), 16)
        v = h[rows, :] + s2v[x, rows, :].astype(F32) + fin2[0, rows, :].astype(F32) + fin2[1, rows, :].astype(F32)
        out[rows, :] = v.astype(BF)

    pump([rs])
    pump(jobs_out)
    pump(jobs_q)
    pump(jobs_kv)
    more = [transpose_zx(w, s_out, lambda zz: f_out, z, x, lsem.at[17])]
    pump(more)
    pump(jobs_q)
    pump(jobs_kv)
    more += [hand_out(w, s_q, f_q, c, x), hand_out(w, s_kv, f_kv, c, x)]
    pump(more[1:])
    pump(jobs_down)
    more += [transpose_zx(w, s_down, lambda zz: f_down, z, x, lsem.at[16])]
    pump(more[3:])
    ends += more
    pump([rs])

    @pl.loop(0, 8)
    def _(i):
        rows = pl.ds(pl.multiple_of(i * 16, 16), 16)
        e = p4[c, x, rows, :].astype(F32) + core_r[3, rows, :].astype(F32)
        e = e + fin[0, rows, :].astype(F32) + fin[1, rows, :].astype(F32)
        v = x_ref[rows, :].astype(F32)
        r = lax.rsqrt(jnp.mean(v * v, axis=1, keepdims=True) + EPS)
        gt[rows, :] = dh[rows, :] + r * e - v * (r * r * r * jnp.mean(e * v, axis=1, keepdims=True))

    pump(ends)
    w.drain()


def backward_attention(
        lens, da, dh, x, h, cos, sin, n1g, wqkv, wout, qp, kv, o, lse, s2, g_gate, g_up, g_down, r1_down, cid):
    sds = jax.ShapeDtypeStruct
    vm, hb = pl.BlockSpec(memory_space=VMEM), pl.BlockSpec(memory_space=ANY)
    outs = [sds((128, 2048), BF), sds((128, 2048), F32), sds((8, 16, 768), BF), sds((8, 16, 768), BF),
            sds((8, 16, 256), BF), sds((8, 16, 128), BF), sds((48, 2048), BF), sds((16, 2048), BF)]
    b = lambda *s: VMEM(s, BF)
    ns = (768, 768, 256, 128)
    r1 = [b(3, 4, 4, 16, 768)] * 4 + [b(2, 3, 4, 48, 1024)] + [b(3, 4, 16, 1024)] * 2
    r1 += [b(3, 4, 4, 16, 256)] * 2 + [b(3, 4, 4, 16, 128)] * 2
    t1 = [b(4, 4, 16, 768)] * 4 + [b(4, 48, 1024)] * 2 + [b(4, 16, 1024)] * 2
    t1 += [b(4, 4, 16, 256)] * 2 + [b(4, 4, 16, 128)] * 2
    r2 = [b(3, 4, 16, 768)] * 4 + [b(3, 48, 1024)] * 2 + [b(3, 16, 1024)] * 2
    r2 += [b(3, 4, 16, 256)] * 2 + [b(3, 4, 16, 128)] * 2
    return pl.pallas_call(
        m3_kernel,
        out_shape=outs,
        in_specs=[pl.BlockSpec(memory_space=pltpu.SMEM), hb] + [vm] * 5 + [hb] + [vm] * 6 + [hb] * 5,
        out_specs=[vm] * 8,
        scratch_shapes=[
            b(2, 4, 128, 2048), b(2, 4, 128, 2048), b(4, 128, 2048), b(2, 4, 512, 128), VMEM((2, 4, 512), F32),
            VMEM((4, 512, 128), F32), b(128, 2048), VMEM((128, 512), F32), b(2, 4, 4, 128, 128),
            b(2, 3, 4, 128, 128), b(2, 512, 384), b(2, 4, 128, 2048), b(4, 128, 2048), b(2, 64, 2048),
            b(2, 128, 2048), b(2, 64, 2048), b(2, 128, 2048),
            b(4, 2, 4, 4, 16, 256), b(4, 2, 4, 4, 16, 128), b(4, 4, 16, 2048),
        ] + r1 + t1 + r2 + [
            b(2, 4, 16, 768), b(2, 4, 16, 768), b(2, 4, 16, 256), b(2, 4, 16, 128), b(48, 2048), b(16, 2048),
            pltpu.SemaphoreType.DMA((150,)), pltpu.SemaphoreType.DMA((150,)), pltpu.SemaphoreType.DMA((18,)),
        ],
        compiler_params=comm_params(cid, 63),
        name="backward_attention",
    )(lens, da, dh, x, h, cos, sin, n1g, wqkv, wout, qp, kv, o, lse, s2, g_gate, g_up, g_down, r1_down)


def local(tokens, lengths, attn_gain, w_query, w_key, w_value, w_out, mlp_gain, w_gate, w_up, w_down, cotangent):
    y = lax.axis_index("y")
    gain1 = attn_gain.astype(F32)[:, None]
    gain2 = mlp_gain.astype(F32)[:, None]
    fold = lambda w, g: (w.astype(F32) * g).astype(BF)
    ranks_first = lambda w: w.transpose(1, 0, 2)
    pad_ff = lambda w: jnp.pad(w.reshape(16, 8, 16, 44), ((0, 0), (0, 0), (0, 0), (0, 4))).reshape(16, 8, 768)
    twice = lambda w: jnp.repeat(w.reshape(16, 4, HD), 2, axis=1)
    qkv_s = ranks_first(jnp.concatenate(
        [fold(w_query, gain1).reshape(16, 8, 256), twice(fold(w_key, gain1)), twice(fold(w_value, gain1))], axis=2))
    gate_s, up_s = ranks_first(pad_ff(fold(w_gate, gain2))), ranks_first(pad_ff(fold(w_up, gain2)))
    down_s = jnp.pad(w_down, ((0, 4), (0, 0)))

    both = lax.all_gather(lengths, "core", axis=0, tiled=True)
    place = ((4 * jnp.arange(4)[:, None] + y) * 128 + jnp.arange(128)[None, :]).reshape(1, 512).astype(jnp.int32)
    c1, c2 = both[:, 0:1], both[:, 0:1] + both[:, 1:2]
    lens = jnp.concatenate([c1, c2], axis=1)
    start = jnp.where(place >= c2, c2, jnp.where(place >= c1, c1, 0))
    lane = jnp.arange(128) % 32
    frequency = jnp.exp(lane.astype(F32) * (-2.0 * math.log(THETA) / HD))
    sign = jnp.where(jnp.arange(128) % 64 < 32, -1.0, 1.0)
    angle = (place - start)[:, :, None].astype(F32) * frequency
    cos, sin = jnp.cos(angle), jnp.sin(angle) * sign

    h, n1g, qp, kv, o, lse, wqkv, wout, dh, da, s2, g_gate, g_up, g_down, r1_down = forward_layer(
        lens, tokens, cos, sin, cotangent, qkv_s, w_out, gate_s, up_s, down_s, 1)
    col = (4, 2, 4, 4, 16, 768)
    g_gate, g_up = g_gate.reshape(col), g_up.reshape(col)
    output, grad_tokens, gate_s, up_s, q_s, kv_s, down_s, out_s = backward_attention(
        lens, da, dh, tokens, h, cos, sin, n1g, wqkv, wout, qp, kv, o, lse, s2, g_gate, g_up, g_down, r1_down, 3)

    wide = lambda v: v.astype(F32).transpose(1, 0, 2).reshape(16, -1)
    unpad = lambda v: v.reshape(16, 128, 48)[:, :, :44].reshape(16, 5632)
    g_gate, g_up = unpad(wide(gate_s)), unpad(wide(up_s))
    pair = lambda v: v.astype(F32).reshape(4, 2, 16, HD).sum(axis=1).transpose(1, 0, 2).reshape(16, -1)
    g_query, g_key, g_value = wide(q_s), pair(kv_s[..., :64]), pair(kv_s[..., 64:])
    rowdot = lambda w, gr: jnp.sum(w.astype(F32) * gr, axis=1)
    grad_attn_gain = rowdot(w_query, g_query) + rowdot(w_key, g_key) + rowdot(w_value, g_value)
    grad_mlp_gain = rowdot(w_gate, g_gate) + rowdot(w_up, g_up)
    return (output, grad_tokens, grad_attn_gain, gain1 * g_query, gain1 * g_key, gain1 * g_value,
            out_s.astype(F32), grad_mlp_gain, gain2 * g_gate, gain2 * g_up, down_s[:44].astype(F32))


def solution(mesh):
    fine = Mesh(mesh.devices.reshape(4, 2, 4, 4), ALL)
    rows, flat = P(ALL, None), P(ALL)
    in_specs = (rows, P(("z", "core"), None), flat, rows, rows, rows, rows, flat, rows, rows, rows, rows)
    out_specs = (rows, rows, flat, rows, rows, rows, rows, flat, rows, rows, rows)
    return jax.shard_map(local, mesh=fine, in_specs=in_specs, out_specs=out_specs, check_vma=False)
```

```python
import functools
import math

import jax
import jax.numpy as jnp
from jax import lax
from jax.experimental import pallas as pl
from jax.experimental.pallas import tpu as pltpu
from jax.sharding import Mesh
from jax.sharding import PartitionSpec as P

HEADS = 32
KV_HEADS = 4
HD = 64
EPS = 1e-05
THETA = 10000.0
NEG = -1e30
BF = jnp.bfloat16
F32 = jnp.float32
ANY = pl.ANY
VMEM = pltpu.VMEM
TP = ("x", "core")
DP = ("z", "y")
ALL = ("z", "core", "x", "y")


def tdot(a, b):
    return lax.dot_general(a, b, (((0,), (0,)), ((), ())), preferred_element_type=F32)


def dott(a, b):
    return lax.dot_general(a, b, (((1,), (1,)), ((), ())), preferred_element_type=F32)


def dot(a, b):
    return jnp.dot(a, b, preferred_element_type=F32)


class Wire:
    def __init__(self, ssem, rsem):
        self.ssem, self.rsem, self.sent = ssem, rsem, []

    def put(self, src, dst, k, to):
        cp = pltpu.make_async_remote_copy(
            src_ref=src, dst_ref=dst, send_sem=self.ssem.at[k], recv_sem=self.rsem.at[k],
            device_id=to, device_id_type=pl.DeviceIdType.MESH)
        cp.start()
        self.sent.append(cp)
        return cp

    def settle(self, copies):
        for cp in copies:
            cp.wait_send()
        done = {id(cp) for cp in copies}
        self.sent = [cp for cp in self.sent if id(cp) not in done]

    def got(self, dst, k, to):
        pltpu.make_async_remote_copy(
            src_ref=dst, dst_ref=dst, send_sem=self.ssem.at[k], recv_sem=self.rsem.at[k],
            device_id=to, device_id_type=pl.DeviceIdType.MESH).wait_recv()

    def drain(self):
        for cp in self.sent:
            cp.wait_send()


def greet(peers):
    barrier = pltpu.get_barrier_semaphore()
    for to in peers:
        pl.semaphore_signal(barrier, inc=1, device_id=to, device_id_type=pl.DeviceIdType.MESH)
    pl.semaphore_wait(barrier, len(peers))


def cx_ring():
    c, x = lax.axis_index("core"), lax.axis_index("x")
    right, left, opp = lax.rem(x + 1, 4), lax.rem(x + 3, 4), lax.rem(x + 2, 4)
    return c, x, right, left, opp, {"x": right}, {"x": left}, {"core": 1 - c}


def comm_params(cid, mb=None):
    kw = {} if mb is None else {"vmem_limit_bytes": mb << 20}
    return pltpu.CompilerParams(collective_id=cid, has_side_effects=True, **kw)


class Mail(Wire):
    def __init__(self, ssem, rsem):
        super().__init__(ssem, rsem)
        self.used = 0

    def new(self):
        self.used += 1
        return self.used - 1


def around(q):
    return lax.rem(q + 1, 4), lax.rem(q + 3, 4), lax.rem(q + 2, 4)


def ring(w, s, axis, q):
    right, left, opp = around(q)
    to_r, to_l = {axis: right}, {axis: left}
    k = [w.new() for _ in range(4)]
    w.put(s(q, None), s(q, None), k[0], to_r)
    w.put(s(q, None), s(q, None), k[1], to_l)
    yield
    w.got(s(left, None), k[0], to_l)
    w.put(s(left, 0), s(left, 0), k[2], to_r)
    w.got(s(right, None), k[1], to_r)
    w.put(s(right, 1), s(right, 1), k[3], to_l)
    yield
    w.got(s(opp, 0), k[2], to_l)
    w.got(s(opp, 1), k[3], to_r)


def col_flows(w, W, z, y):
    cut = lambda h: slice(None) if h is None else pl.ds(2 * h, 2)

    def first():
        yield from ring(w, lambda p, h: W.at[z, 0, cut(h), p], "y", y)
        yield from ring(w, lambda p, h: W.at[p, 0, cut(h)], "z", z)

    def second():
        yield from ring(w, lambda p, h: W.at[p, 1, cut(h), y], "z", z)
        yield from ring(w, lambda p, h: W.at[:, 1, cut(h), p], "y", y)

    return [first(), second()]


def row_flows(w, W, z, y):
    n = W.shape[-1] // 4
    cut = lambda b, h: pl.ds(2 * n * b, 2 * n) if h is None else pl.ds(2 * n * b + n * h, n)

    def first():
        yield from ring(w, lambda p, h: W.at[z, p, :, cut(0, h)], "y", y)
        yield from ring(w, lambda p, h: W.at[p, :, :, cut(0, h)], "z", z)

    def second():
        yield from ring(w, lambda p, h: W.at[p, y, :, cut(1, h)], "z", z)
        yield from ring(w, lambda p, h: W.at[:, p, :, cut(1, h)], "y", y)

    return [first(), second()]


def straight(w, stages):
    for s, axis, q in stages:
        ks = {}
        for k in (1, 3, 2):
            ks[k] = w.new()
            w.put(s(q), s(q), ks[k], {axis: lax.rem(q + k, 4)})
        yield
        for k in (1, 3, 2):
            frm = lax.rem(q + 4 - k, 4)
            w.got(s(frm), ks[k], {axis: frm})


def col_straight(w, W, z, y):
    return [straight(w, [(lambda p: W.at[z, 0, :, p], "y", y), (lambda p: W.at[p, 0], "z", z)]),
            straight(w, [(lambda p: W.at[p, 1, :, y], "z", z), (lambda p: W.at[:, 1, :, p], "y", y)])]


def row_straight(w, W, z, y):
    n = W.shape[-1] // 2
    a, b = pl.ds(0, n), pl.ds(n, n)
    return [straight(w, [(lambda p: W.at[z, p, :, a], "y", y), (lambda p: W.at[p, :, :, a], "z", z)]),
            straight(w, [(lambda p: W.at[p, y, :, b], "z", z), (lambda p: W.at[:, p, :, b], "y", y)])]


def pump(flows):
    for f in flows:
        next(f, None)


def gather8(w, src, dst):
    c, x, right, left, opp, to_r, to_l, to_c = cx_ring()
    rows = dst.shape[2]
    lo, hi = pl.ds(0, rows // 2), pl.ds(rows // 2, rows // 2)
    k = [w.new() for _ in range(10)]
    out = []
    out += [w.put(src.at[lo], dst.at[c, x, lo], k[0], to_r)]
    out += [w.put(src.at[hi], dst.at[c, x, hi], k[1], to_l)]
    out += [w.put(src.at[hi], dst.at[c, x, hi], k[2], to_r)]
    out += [w.put(src.at[lo], dst.at[c, x, lo], k[3], to_l)]
    out += [w.put(src, dst.at[c, x], k[4], to_c)]
    yield
    w.got(dst.at[c, left, lo], k[0], to_l)
    out += [w.put(dst.at[c, left, lo], dst.at[c, left, lo], k[5], to_r)]
    w.got(dst.at[c, right, hi], k[1], to_r)
    out += [w.put(dst.at[c, right, hi], dst.at[c, right, hi], k[6], to_l)]
    yield
    w.got(dst.at[1 - c, x], k[4], to_c)
    yield
    w.got(dst.at[c, left, hi], k[2], to_l)
    out += [w.put(dst.at[c, left], dst.at[c, left], k[7], to_c)]
    w.got(dst.at[c, right, lo], k[3], to_r)
    out += [w.put(dst.at[c, right], dst.at[c, right], k[8], to_c)]
    yield
    w.got(dst.at[1 - c, left], k[7], to_c)
    w.got(dst.at[1 - c, right], k[8], to_c)
    yield
    w.got(dst.at[c, opp, lo], k[5], to_l)
    w.got(dst.at[c, opp, hi], k[6], to_r)
    out += [w.put(dst.at[c, opp], dst.at[c, opp], k[9], to_c)]
    yield
    w.got(dst.at[1 - c, opp], k[9], to_c)
    w.settle(out)


def add_to(dst, other, r0, rows, step=16):
    @pl.loop(0, rows // step)
    def _(i):
        a = pl.ds(pl.multiple_of(r0 + i * step, step), step)
        b = pl.ds(pl.multiple_of(i * step, step), step)
        dst[a, :] = (dst[a, :].astype(F32) + other[b, :].astype(F32)).astype(dst.dtype)


def scatter8_core(w, p, core_r, state, only=None):
    c, x, right, left, opp, to_r, to_l, to_c = cx_ring()
    if not state:
        state["k"], state["out"] = [w.new() for _ in range(4)], []
    for i, xx in enumerate((opp, right, left, x)):
        if only is None or only == i:
            state["out"].append(w.put(p.at[1 - c, xx], core_r.at[i], state["k"][i], to_c))


def scatter8_ring(w, p, core_r, hop, fin, state):
    c, x, right, left, opp, to_r, to_l, to_c = cx_ring()
    rows = p.shape[2]
    half = rows // 2
    lo, hi = pl.ds(0, half), pl.ds(half, half)
    kc, out = state["k"], state["out"]
    k = [w.new() for _ in range(6)]
    w.got(core_r.at[0], kc[0], to_c)
    add_to(p.at[c, opp], core_r.at[0], 0, rows)
    out += [w.put(p.at[c, opp, lo], hop.at[0], k[0], to_r)]
    out += [w.put(p.at[c, opp, hi], hop.at[1], k[1], to_l)]
    yield
    w.got(core_r.at[1], kc[1], to_c)
    add_to(p.at[c, right], core_r.at[1], 0, rows)
    out += [w.put(p.at[c, right, hi], fin.at[0, hi], k[2], to_r)]
    w.got(core_r.at[2], kc[2], to_c)
    add_to(p.at[c, left], core_r.at[2], 0, rows)
    out += [w.put(p.at[c, left, lo], fin.at[1, lo], k[3], to_l)]
    yield
    w.got(hop.at[0], k[0], to_l)
    add_to(p.at[c, right], hop.at[0], 0, half)
    out += [w.put(p.at[c, right, lo], fin.at[0, lo], k[4], to_r)]
    w.got(hop.at[1], k[1], to_r)
    add_to(p.at[c, left], hop.at[1], half, half)
    out += [w.put(p.at[c, left, hi], fin.at[1, hi], k[5], to_l)]
    yield
    w.got(core_r.at[3], kc[3], to_c)
    w.got(fin.at[0, hi], k[2], to_l)
    w.got(fin.at[1, lo], k[3], to_r)
    w.got(fin.at[0, lo], k[4], to_l)
    w.got(fin.at[1, hi], k[5], to_r)
    w.settle(out)


def lanes(shape):
    return lax.broadcasted_iota(jnp.int32, shape, len(shape) - 1)


def take_lanes(load, moves):
    out = None
    for src, lo, hi in moves:
        a, shift = (src - lo) // 128, (src - lo) % 128
        split = 128 - shift
        turned = lambda t: pltpu.roll(load(t), (128 - shift) % 128, 1) if shift else load(t)
        if hi <= split:
            piece = turned(a)
        elif lo >= split:
            piece = turned(a + 1)
        else:
            piece = jnp.where(lanes((16, 128)) < split, turned(a), turned(a + 1))
        at = lanes(piece.shape)
        out = jnp.where((at >= lo) & (at < hi), piece, jnp.zeros_like(piece) if out is None else out)
    return out


def unit_place(z, c, x, y):
    return ((z * 2 + c) * 4 + x) * 4 + y


def spread_moves(r, t):
    out = []
    for s in range(16):
        d0 = 48 * s
        lo, hi = max(d0, 128 * t), min(d0 + 44, 128 * t + 128)
        if lo < hi:
            unit = unit_place(s // 4, r % 2, r // 2, s % 4)
            out.append((44 * unit + lo - d0, lo - 128 * t, hi - 128 * t))
    return out


def collect_moves(t):
    out = []
    for unit in range(128):
        d0 = 44 * unit
        lo, hi = max(d0, 128 * t), min(d0 + 44, 128 * t + 128)
        if lo < hi:
            z, c, x, y = unit // 32, unit // 16 % 2, unit // 4 % 4, unit % 4
            out.append((2 * x + c, (48 * (4 * z + y) + lo - d0, lo - 128 * t, hi - 128 * t)))
    return out


def swap_halves(u):
    first = lax.rem(lanes(u.shape), 64) < 32
    return jnp.where(first, pltpu.roll(u, 96, u.ndim - 1), pltpu.roll(u, 32, u.ndim - 1))


def entry(peers, extra=None):
    barrier = pltpu.get_barrier_semaphore()
    for to in peers:
        pl.semaphore_signal(barrier, inc=1, device_id=to, device_id_type=pl.DeviceIdType.MESH)
    if extra is None:
        pl.semaphore_wait(barrier, len(peers))
        return
    more, to = extra

    @pl.when(more)
    def _():
        pl.semaphore_signal(barrier, inc=1, device_id=to, device_id_type=pl.DeviceIdType.MESH)
        pl.semaphore_wait(barrier, len(peers) + 1)

    @pl.when(jnp.logical_not(more))
    def _():
        pl.semaphore_wait(barrier, len(peers))


def tp_peers(c, x):
    r = 2 * x + c
    out = []
    for k in range(1, 8):
        rr = lax.rem(r + k, 8)
        out.append((rr, {"x": rr // 2, "core": lax.rem(rr, 2)}))
    return out


def spread(w, src, W, z, c, x, y, local_sem):
    ks = [w.new() for _ in range(7)]
    for k, (rr, to) in zip(ks, tp_peers(c, x)):
        w.put(src.at[rr], W.at[z, c, x, y], k, to)
    own = pltpu.make_async_copy(src.at[2 * x + c], W.at[z, c, x, y], local_sem)
    own.start()
    yield
    r = 2 * x + c
    for i, k in enumerate(ks):
        rr = lax.rem(r + 7 - i, 8)
        w.got(W.at[z, lax.rem(rr, 2), rr // 2, y], k, {"x": rr // 2, "core": lax.rem(rr, 2)})
    own.wait()


def transpose_zx(w, src, dst_of, z, x, local_sem):
    k = w.new()
    to = {"z": x, "x": z}

    def far():
        return pltpu.make_async_remote_copy(
            src_ref=src, dst_ref=dst_of(x), send_sem=w.ssem.at[k], recv_sem=w.rsem.at[k],
            device_id=to, device_id_type=pl.DeviceIdType.MESH)

    def near():
        return pltpu.make_async_copy(src, dst_of(x), local_sem)

    @pl.when(z != x)
    def _():
        far().start()

    @pl.when(z == x)
    def _():
        near().start()

    yield

    @pl.when(z != x)
    def _():
        far().wait_send()
        w.got(dst_of(z), k, to)

    @pl.when(z == x)
    def _():
        near().wait()


def attend(q, keys, j, y, c1, c2):
    m, n = q.shape[0], keys.shape[0]
    s = dott(q, keys)
    row = lax.broadcasted_iota(jnp.int32, (m, 1), 0)
    place = (4 * j + y) * 128 + lax.rem(row, 128)
    start = jnp.where(place >= c2, c2, jnp.where(place >= c1, c1, 0))
    at = lax.broadcasted_iota(jnp.int32, (m, n), 1)
    s = jnp.where((at >= start) & (at <= place), s, NEG)
    top = jnp.max(s, axis=1, keepdims=True)
    e = jnp.exp(s - top)
    total = jnp.sum(e, axis=1, keepdims=True)
    return dot(e.astype(BF), keys) / total, top + jnp.log(total)


def pair_heads(first, second, lower):
    low = lanes(first.shape) < 64
    if lower:
        return jnp.where(low, first, pltpu.roll(second, 64, 1))
    return jnp.where(low, pltpu.roll(first, 64, 1), second)


def forward_kernel(lens, gains, x_ref, cot, wq, wk, wv, out_s, w_gate, w_up, w_down,
                   h_out, n1_out, qp_out, kv_out, o_out, lse_out, wqkv_out, wout_out, cos_out, sin_out,
                   dh_out, da_out, s2, g_gate, g_up, g_down, r1_down,
                   cos, sin, h, qp, kv, o, lse, wqkv, wout, n1, cv, wg, wu, wd, p, core_r, hop, fin,
                   dact, a_all, dg_all, du_all, core2, d_down, qkv_s, gate_s, up_s, ssem, rsem, lsem, osem):
    z, c, x, y = (lax.axis_index(a) for a in ALL)
    peers = [to for _, to in tp_peers(c, x)]
    for axis, q in (("y", y), ("z", z)):
        peers += [{axis: lax.rem(q + k, 4)} for k in (1, 2, 3)]
    w = Mail(ssem, rsem)
    saved = []

    def save(src, dst):
        cp = pltpu.make_async_copy(src, dst, osem.at[len(saved)])
        cp.start()
        saved.append(cp)
        return cp

    gain1, gain2 = gains[0], gains[1]
    for r in range(8):
        for t in range(2):
            at = 256 * r + 128 * t
            qkv_s[r, :, 128 * t: 128 * t + 128] = (wq[:, at: at + 128].astype(F32) * gain1).astype(BF)
        t, odd = r // 4, r // 2 % 2
        kt, vt = wk[:, 128 * t: 128 * t + 128].astype(F32), wv[:, 128 * t: 128 * t + 128].astype(F32)
        kt, vt = (pltpu.roll(kt, 64, 1), vt) if odd else (kt, pltpu.roll(vt, 64, 1))
        qkv_s[r, :, 256:384] = (jnp.where(lanes(kt.shape) < 64, kt, vt) * gain1).astype(BF)
    entry(peers, (z != x, {"z": x, "x": z}))

    sp_qkv = spread(w, qkv_s, wqkv, z, c, x, y, lsem.at[0])
    pump([sp_qkv])

    @pl.loop(0, 8)
    def _(i):
        rows = pl.ds(pl.multiple_of(i * 16, 16), 16)
        v = x_ref[rows, :].astype(F32)
        n1[c, x, rows, :] = (v * lax.rsqrt(jnp.mean(v * v, axis=1, keepdims=True) + EPS)).astype(BF)

    ag_n1 = gather8(w, n1.at[c, x], n1)
    pump([ag_n1])
    wd[z, y] = jnp.concatenate([w_down[...], jnp.zeros((4, 2048), BF)], axis=0)
    pump([sp_qkv])
    fl_qkv = col_straight(w, wqkv, z, y)
    pump(fl_qkv)
    for src, dst in ((w_gate, gate_s), (w_up, up_s)):
        for r in range(8):
            for t in range(6):
                load = lambda a: src[:, 128 * a: 128 * a + 128].astype(F32)
                dst[r, :, 128 * t: 128 * t + 128] = (take_lanes(load, spread_moves(r, t)) * gain2).astype(BF)
    pump([ag_n1])
    pump([ag_n1])
    pump(fl_qkv)
    spreads = [spread(w, gate_s, wg, z, c, x, y, lsem.at[2]), spread(w, up_s, wu, z, c, x, y, lsem.at[3])]
    pump(spreads)
    tr_out = transpose_zx(w, out_s, lambda zz: wout.at[zz, y], z, x, lsem.at[1])
    pump([tr_out])
    fl_down = row_flows(w, wd, z, y)
    pump(fl_down)

    for g in range(2):
        lane = lanes((128, 128))
        freq = jnp.exp(lax.rem(lane, 32).astype(F32) * (-2.0 * math.log(THETA) / HD))
        c1, c2 = lens[g, 0], lens[g, 0] + lens[g, 1]

        @pl.loop(0, 4)
        def _(j):
            place = (4 * j + y) * 128 + lax.broadcasted_iota(jnp.int32, (128, 128), 0)
            start = jnp.where(place >= c2, c2, jnp.where(place >= c1, c1, 0))
            angle = (place - start).astype(F32) * freq
            rows = pl.ds(pl.multiple_of(128 * j, 128), 128)
            cos[g, rows, :] = jnp.cos(angle)
            turned = jnp.sin(angle)
            sin[g, rows, :] = jnp.where(lax.rem(lane, 64) < 32, -turned, turned)

    pump([ag_n1])
    pump([tr_out])
    fl_out = row_straight(w, wout, z, y)
    pump(fl_out)
    pump(spreads)
    fl_gu = col_flows(w, wg, z, y) + col_flows(w, wu, z, y)
    pump(fl_gu)
    fl_mlp = fl_down + fl_gu
    pump([ag_n1])
    pump([ag_n1])
    pump(fl_qkv)
    pump([ag_n1])
    weights = wqkv[...].reshape(2048, 384)

    def project(g, keys_too):
        u = dot(n1[g].reshape(512, 2048), weights)
        cs, sn = cos[g], sin[g]
        if keys_too:
            v = u[:, 256:384]
            turned = jnp.where(lanes(v.shape) < 64, v * cs + swap_halves(v) * sn, v)
            kv[g, :, y] = turned.astype(BF).reshape(4, 128, 128)
        for t in range(2):
            v = u[:, 128 * t: 128 * t + 128]
            v = (v * cs + swap_halves(v) * sn) * (HD ** -0.5)
            low = lanes(v.shape) < 64
            for b, head in enumerate((v, pltpu.roll(v, 64, 1))):
                rows = pl.ds(128 * (2 * t + b), 128)
                qp[g, :, rows, :] = jnp.where(low, head, 0.0).astype(BF).reshape(4, 128, 128)

    g0, g1 = 1 - c, c
    to_c = {"core": 1 - c}
    pump(fl_mlp)
    project(g0, True)
    fl_kv = [straight(w, [(lambda pp: kv.at[g0, :, pp], "y", y)])]
    pump(fl_kv)
    pump(fl_out)
    ag_cot = gather8(w, cot, cv)
    pump([ag_cot])
    project(g1, False)
    keep_n1 = save(n1, n1_out)
    save(wqkv, wqkv_out)
    save(cos, cos_out)
    save(sin, sin_out)
    keep_cot = save(cot, cv.at[c, x])
    pump(fl_mlp[0::2])
    pump(fl_kv)
    k_kv = w.new()
    w.put(kv.at[g0], kv.at[g0], k_kv, to_c)
    pump(fl_mlp[1::2])

    state = {}
    for turn_no, g in enumerate((g0, g1)):
        if turn_no == 1:
            w.got(kv.at[g], k_kv, to_c)
            save(kv, kv_out)
            save(qp, qp_out)
            save(wout, wout_out)
        for j in range(4):
            n = 512 * (j + 1)
            keys = kv[g, 0:j + 1].reshape(n, 128)
            for t in range(2):
                part = qp[g, j, 256 * t: 256 * t + 256]
                res, total = attend(part, keys, j, y, lens[g, 0], lens[g, 0] + lens[g, 1])
                both = pair_heads(res[:128], res[128:], False)
                o[g, pl.ds(128 * j, 128), 128 * t: 128 * t + 128] = both.astype(BF)
                lse[g, pl.ds(j, 1), 256 * t: 256 * t + 256] = jnp.broadcast_to(total, (256, 128)).T[0:1, :]
            if j == 2:
                pump([ag_cot])
        pump(fl_out)
        out_w = wout[...].reshape(256, 2048)

        @pl.loop(0, 4)
        def _(i):
            p[g, i] = dot(o[g, pl.ds(pl.multiple_of(128 * i, 128), 128), :], out_w).astype(BF)

        if turn_no == 0:
            keep_n1.wait()
            scatter8_core(w, p, core_r, state)
    rs = scatter8_ring(w, p, core_r, hop, fin, state)
    pump([rs])
    pump([rs])
    save(o, o_out)
    save(lse, lse_out)
    pump([ag_cot])
    pump([ag_cot])
    pump([ag_cot])
    pump([rs])
    pump([ag_cot])
    pump(fl_mlp[0::2])
    pump([rs])
    pump(fl_mlp[1::2])

    @pl.loop(0, 8)
    def _(i):
        rows = pl.ds(pl.multiple_of(i * 16, 16), 16)
        v = x_ref[rows, :].astype(F32) + p[c, x, rows, :].astype(F32) + core_r[3, rows, :].astype(F32)
        v = v + fin[0, rows, :].astype(F32) + fin[1, rows, :].astype(F32)
        h[rows, :] = v
        n1[c, x, rows, :] = (v * lax.rsqrt(jnp.mean(v * v, axis=1, keepdims=True) + EPS)).astype(BF)

    keep_h = save(h, h_out)
    n2v = n1
    ag = gather8(w, n2v.at[c, x], n2v)
    pump([ag])
    pump([ag])
    pump([ag])
    pump(fl_mlp)
    keep_cot.wait()
    down = wd[...].reshape(768, 2048)

    @pl.loop(0, 2)
    def _(g):
        for t in range(2):
            v = dott(cv[g, 2 * t: 2 * t + 2].reshape(256, 2048), down)
            dact[g, 2 * t: 2 * t + 2] = v.astype(BF).reshape(2, 128, 768)

    cc, xx, right, left, opp, to_r, to_l, to_c = cx_ring()
    gate, up = wg[...].reshape(2048, 768), wu[...].reshape(2048, 768)
    st3, st2 = {}, {}

    def block(b, number):
        gp, u = dot(n2v[:, b].reshape(256, 2048), gate), dot(n2v[:, b].reshape(256, 2048), up)
        sig = jax.nn.sigmoid(gp)
        act = gp * sig
        d = dact[:, b].reshape(256, 768).astype(F32)
        a_all[:, b] = (act * u).astype(BF).reshape(2, 128, 768)
        dg_all[:, b] = (d * u * sig * (1.0 + gp * (1.0 - sig))).astype(BF).reshape(2, 128, 768)
        du_all[:, b] = (d * act).astype(BF).reshape(2, 128, 768)

        @pl.loop(0, 8)
        def _(i):
            part = dott(dg_all[:, b].reshape(256, 768), wg[i // 2, i % 2].reshape(256, 768))
            part += dott(du_all[:, b].reshape(256, 768), wu[i // 2, i % 2].reshape(256, 768))
            p[:, b, :, pl.ds(pl.multiple_of(256 * i, 256), 256)] = part.astype(BF).reshape(2, 128, 256)

        scatter8_core(w, p, core_r, st3, number)

    block(x, 3)
    pump([ag])
    pump([ag])
    block(left, 2)
    pump([ag])
    pump([ag])
    block(opp, 0)
    rs3 = scatter8_ring(w, p, core_r, hop, fin, st3)
    pump([rs3])
    block(right, 1)
    pump([rs3])
    at = a_all[...].reshape(1024, 768).T

    @pl.loop(0, 8)
    def _(i):
        cols = pl.ds(pl.multiple_of(256 * i, 256), 256)
        d_down[:, :, :, cols] = dot(at, cv[:, :, :, cols].reshape(1024, 256)).astype(BF).reshape(4, 4, 48, 256)

    first, second = pl.ds(0, 1024), pl.ds(1024, 1024)
    landed = others(w, y, "y", lambda pp: d_down.at[:, pp, :, first], r1_down.at[0])
    landed += others(w, z, "z", lambda pp: d_down.at[pp, :, :, second], r1_down.at[1])
    save(d_down, g_down)

    p2 = cv

    def out_part(g):
        @pl.loop(0, 8)
        def _(i):
            cols = pl.ds(pl.multiple_of(256 * i, 256), 256)
            part = dot(a_all[g].reshape(512, 768), wd[:, :, :, cols].reshape(768, 256))
            p2[g, :, :, cols] = part.astype(BF).reshape(4, 128, 256)

    pump([rs3])
    out_part(g0)
    scatter8_core(w, p2, core2, st2)
    out_part(g1)

    dg, du = dg_all[...].reshape(1024, 768), du_all[...].reshape(1024, 768)

    def stage(i, k):
        return pltpu.make_async_copy(
            dact.at[i % 2, pl.ds(2 * k, 2)], (g_gate, g_up)[k].at[i], lsem.at[4 + 2 * (i % 2) + k])

    for i in range(8):
        t = n2v[:, :, :, 256 * i: 256 * i + 256].reshape(1024, 256).T
        if i >= 2:
            stage(i - 2, 0).wait()
            stage(i - 2, 1).wait()
        dact[i % 2, 0:2] = dot(t, dg).astype(BF).reshape(2, 128, 768)
        dact[i % 2, 2:4] = dot(t, du).astype(BF).reshape(2, 128, 768)
        stage(i, 0).start()
        stage(i, 1).start()

    for i, b in enumerate((opp, right, left, x)):
        w.got(core2.at[i], st2["k"][i], to_c)
        add_to(p2.at[c, b], core2.at[i], 0, 128)
    save(p2.at[c], s2)
    pump([rs3])
    keep_h.wait()

    @pl.loop(0, 8)
    def _(i):
        rows = pl.ds(pl.multiple_of(i * 16, 16), 16)
        e = p[c, x, rows, :].astype(F32) + core_r[3, rows, :].astype(F32)
        e = e + fin[0, rows, :].astype(F32) + fin[1, rows, :].astype(F32)
        v = h[rows, :]
        r = lax.rsqrt(jnp.mean(v * v, axis=1, keepdims=True) + EPS)
        out = cot[rows, :].astype(F32) + r * e - v * (r * r * r * jnp.mean(e * v, axis=1, keepdims=True))
        h[rows, :] = out
        n1[c, x, rows, :] = out.astype(BF)

    save(h, dh_out)
    save(n1.at[c, x], da_out)
    w.drain()
    for i in (6, 7):
        stage(i, 0).wait()
        stage(i, 1).wait()
    for a in landed:
        w.got(*a)
    for cp in saved:
        if all(cp is not a for a in (keep_n1, keep_h, keep_cot)):
            cp.wait()


def forward_layer(lens, gains, tokens, cot, wq, wk, wv, out_s, w_gate, w_up, w_down, cid):
    sds = jax.ShapeDtypeStruct
    vm, hb = pl.BlockSpec(memory_space=VMEM), pl.BlockSpec(memory_space=ANY)
    col, big = (4, 2, 4, 4, 16, 768), (2, 4, 128, 2048)
    row, half, table = (128, 2048), (2, 4, 128, 768), ((2, 512, 128), F32)
    mid = [((2, 4, 512, 128), BF), ((2, 4, 4, 128, 128), BF), ((2, 512, 256), BF), ((2, 4, 512), F32),
           ((4, 2, 4, 4, 16, 384), BF), ((4, 4, 16, 2048), BF)]
    outs = [(row, F32), (big, BF)] + mid + [table, table] + [
        (row, F32), (row, BF), ((4, 128, 2048), BF), ((8, 2, 128, 768), BF), ((8, 2, 128, 768), BF),
        ((4, 4, 48, 2048), BF), ((2, 3, 4, 48, 1024), BF)]
    scratch = [table, table, (row, F32)] + mid + [
        (big, BF), (big, BF), (col, BF), (col, BF), ((4, 4, 48, 2048), BF),
        (big, BF), ((4, 128, 2048), BF), ((2, 64, 2048), BF), ((2, 128, 2048), BF),
        (half, BF), (half, BF), (half, BF), (half, BF), ((4, 128, 2048), BF), ((4, 4, 48, 2048), BF),
        ((8, 16, 384), BF), ((8, 16, 768), BF), ((8, 16, 768), BF)]
    return pl.pallas_call(
        forward_kernel,
        out_shape=[sds(*a) for a in outs],
        in_specs=[pl.BlockSpec(memory_space=pltpu.SMEM)] + [vm] * 6 + [hb] + [vm] * 3,
        out_specs=[hb] * len(outs),
        scratch_shapes=[VMEM(*a) for a in scratch] + [
            pltpu.SemaphoreType.DMA((170,)), pltpu.SemaphoreType.DMA((170,)), pltpu.SemaphoreType.DMA((8,)),
            pltpu.SemaphoreType.DMA((18,)),
        ],
        compiler_params=comm_params(cid, 63),
        name="forward_layer",
    )(lens, gains, tokens, cot, wq, wk, wv, out_s, w_gate, w_up, w_down)


def ring_tail(w, s, hop, fin):
    c, x, right, left, opp, to_r, to_l, to_c = cx_ring()
    half = s.shape[1] // 2
    lo, hi = pl.ds(0, half), pl.ds(half, half)
    k = [w.new() for _ in range(6)]
    w.put(s.at[opp, lo], hop.at[0], k[0], to_r)
    w.put(s.at[opp, hi], hop.at[1], k[1], to_l)
    w.put(s.at[right, hi], fin.at[0, hi], k[2], to_r)
    w.put(s.at[left, lo], fin.at[1, lo], k[3], to_l)
    yield
    w.got(hop.at[0], k[0], to_l)
    add_to(s.at[right], hop.at[0], 0, half)
    w.put(s.at[right, lo], fin.at[0, lo], k[4], to_r)
    w.got(hop.at[1], k[1], to_r)
    add_to(s.at[left], hop.at[1], half, half)
    w.put(s.at[left, hi], fin.at[1, hi], k[5], to_l)
    yield
    w.got(fin.at[0, hi], k[2], to_l)
    w.got(fin.at[1, lo], k[3], to_r)
    w.got(fin.at[0, lo], k[4], to_l)
    w.got(fin.at[1, hi], k[5], to_r)


def others(w, q, axis, piece, recv):
    ks = {}
    for k in (1, 3, 2):
        to = lax.rem(q + k, 4)
        ks[k] = w.new()
        w.put(piece(to), recv.at[k - 1], ks[k], {axis: to})
    return [(recv.at[k - 1], ks[k], {axis: lax.rem(q + 4 - k, 4)}) for k in (1, 3, 2)]


def sum_four(dst, own, recv, lead):
    total = math.prod(lead)

    @pl.loop(0, total)
    def _(i):
        at = (i,) if len(lead) == 1 else (i // lead[1], lax.rem(i, lead[1]))
        acc = own[at].astype(F32)
        for k in range(3):
            acc += recv[(k,) + at].astype(F32)
        dst[at] = acc.astype(dst.dtype)


def col_job(w, src, r1, t, r2, s, e, z, y, lsem):
    if e == 0:
        own, piece1, ax1, q1 = src.at[:, 0, :, y], lambda p: src.at[:, 0, :, p], "y", y
        piece2, ax2, q2 = lambda p: t.at[p], "z", z
    else:
        own, piece1, ax1, q1 = src.at[z, 1], lambda p: src.at[p, 1], "z", z
        piece2, ax2, q2 = lambda p: t.at[:, p], "y", y
    first = pltpu.make_async_copy(own, t, lsem)
    first.start()
    waits = others(w, q1, ax1, piece1, r1)
    yield
    first.wait()
    for a in waits:
        w.got(*a)
    sum_four(t, t, r1, (4, 4))
    waits = others(w, q2, ax2, piece2, r2)
    yield
    for a in waits:
        w.got(*a)
    sum_four(s.at[e], piece2(q2), r2, (4,))


def row_job(w, src, r1, t, r2, s, e, z, y, lsem, here=None):
    n = s.shape[-1] // 2
    rows = s.shape[0]
    cols = pl.ds(e * n, n)
    if len(src.shape) == 5:
        at = lambda *q: src.at[(e,) + q]
    else:
        at = lambda *q: src.at[q + (slice(None), cols)]
    if e == 0:
        piece1, ax1, q1, ax2, q2 = lambda p: at(slice(None), p), "y", y, "z", z
    else:
        piece1, ax1, q1, ax2, q2 = lambda p: at(p, slice(None)), "z", z, "y", y
    own = piece1(q1)
    first = pltpu.make_async_copy(own, t, lsem)
    first.start()
    waits = others(w, q1, ax1, piece1, r1) if here is None else []
    yield
    first.wait()
    for a in waits:
        w.got(*a)
    sum_four(t, t, r1, (4,))
    waits = others(w, q2, ax2, lambda p: t.at[p], r2)
    yield
    for a in waits:
        w.got(*a)

    @pl.loop(0, rows // 16)
    def _(i):
        at = pl.ds(pl.multiple_of(i * 16, 16), 16)
        acc = t[q2, at].astype(F32)
        for k in range(3):
            acc += r2[k, at].astype(F32)
        s[at, cols] = acc.astype(BF)


def hand_out(w, s, f, c, x):
    r = 2 * x + c
    ks = [w.new() for _ in range(7)]
    for k, (rr, to) in zip(ks, tp_peers(c, x)):
        w.put(s.at[lax.rem(rr, 2), rr // 2], f.at[r], k, to)
    f[r] = s[c, x]
    yield
    for i, k in enumerate(ks):
        rr = lax.rem(r + 7 - i, 8)
        w.got(f.at[rr], k, {"x": rr // 2, "core": lax.rem(rr, 2)})


def m3_kernel(lens, gains, wq, wk, wv, w_gate, w_up, da, dh, x_ref, h, cos, sin, n1g, wqkv, wout, qp, kv, o, lse,
              s2, g_gate, g_up, g_down, r1_down,
              out, gt, gain_out, q_out, k_out, v_out, wo_out, gate_out, up_out, down_out,
              f_gate, f_up, f_q, f_kv, f_out,
              dav, n1v, s2v, do4, delta, acc, kvt, dqt, dkv_s, dkv_r, dqkv, p4, core_r, hop, fin, hop2, fin2,
              d_q, d_kv, d_out,
              ra0, ra1, rb0, rb1, rc, rd0, rd1, re0, re1, rf0, rf1,
              ta0, ta1, tb0, tb1, tc0, tc1, td0, td1, te0, te1, tf0, tf1,
              qa0, qa1, qb0, qb1, qc0, qc1, qd0, qd1, qe0, qe1, qf0, qf1,
              s_gate, s_up, s_q, s_kv, s_down, s_out, ssem, rsem, lsem):
    z, c, x, y = (lax.axis_index(a) for a in ALL)
    peers = [to for _, to in tp_peers(c, x)]
    for axis, q in (("y", y), ("z", z)):
        peers += [{axis: lax.rem(q + k, 4)} for k in (1, 2, 3)]
    entry(peers, (z != x, {"z": x, "x": z}))
    w = Mail(ssem, rsem)
    ag = gather8(w, da, dav)
    pump([ag])
    loads = [pltpu.make_async_copy(a, b, lsem.at[i]) for i, (a, b) in enumerate(
        ((da, dav.at[c, x]), (s2, s2v), (n1g, n1v), (r1_down, rc)))]
    for cp in loads:
        cp.start()
    jobs_down = [
        row_job(w, g_down, rc.at[0], tc0, qc0, s_down, 0, z, y, lsem.at[7], loads[3]),
        row_job(w, g_down, rc.at[1], tc1, qc1, s_down, 1, z, y, lsem.at[8], loads[3]),
    ]
    jobs = [
        col_job(w, g_gate, ra0, ta0, qa0, s_gate, 0, z, y, lsem.at[4]),
        col_job(w, g_gate, ra1, ta1, qa1, s_gate, 1, z, y, lsem.at[5]),
        col_job(w, g_up, rb0, tb0, qb0, s_up, 0, z, y, lsem.at[6]),
        col_job(w, g_up, rb1, tb1, qb1, s_up, 1, z, y, lsem.at[9]),
    ]
    pump(jobs_down)
    pump(jobs)
    pump([ag])
    loads[0].wait()
    pump([ag])
    pump([ag])
    pump([ag])
    pump([ag])
    loads[1].wait()
    loads[3].wait()
    tail2 = ring_tail(w, s2v, hop2, fin2)
    pump([tail2])
    pump([ag])

    ow = wout[...].reshape(256, 2048)
    for g in range(2):
        dv = dott(dav[g].reshape(512, 2048), ow).astype(BF).astype(F32)
        ov = o[g].astype(F32)
        for t in range(2):
            v = dv[:, 128 * t: 128 * t + 128]
            pr = v * ov[:, 128 * t: 128 * t + 128]
            low = lanes(v.shape) < 64
            for b, head in enumerate((pltpu.roll(v, 64, 1), v)):
                rows = pl.ds(128 * (2 * t + b), 128)
                do4[g, :, rows, :] = jnp.where(low, 0.0, head).astype(BF).reshape(4, 128, 128)
                total = jnp.sum(jnp.where(low == (b == 0), pr, 0.0), axis=1, keepdims=True)
                total = jnp.broadcast_to(total, (512, 128)).T
                for j in range(4):
                    delta[g, pl.ds(j, 1), rows] = total[0:1, 128 * j: 128 * j + 128]

    ot = o[...].reshape(1024, 256).T

    @pl.loop(0, 8)
    def _(i):
        cols = pl.ds(pl.multiple_of(256 * i, 256), 256)
        d_out[:, :, :, cols] = dot(ot, dav[:, :, :, cols].reshape(1024, 256)).astype(BF).reshape(4, 4, 16, 256)

    jobs_out = [
        row_job(w, d_out, rd0, td0, qd0, s_out, 0, z, y, lsem.at[10]),
        row_job(w, d_out, rd1, td1, qd1, s_out, 1, z, y, lsem.at[11]),
    ]
    pump(jobs_out)

    g0, g1 = 1 - c, c
    waits = {}
    for no, g in enumerate((g0, g1)):
        kvt[...] = kv[g].reshape(2048, 128).T
        acc[...] = jnp.zeros_like(acc)
        for j in range(4):
            qj, doj = qp[g, j], do4[g, j]
            lse_row, delta_row = lse[g, pl.ds(j, 1), :], delta[g, pl.ds(j, 1), :]
            col = lanes((1, 512))
            place = (4 * j + y) * 128 + lax.rem(col, 128)
            c1, c2 = lens[g, 0], lens[g, 0] + lens[g, 1]
            start = jnp.where(place >= c2, c2, jnp.where(place >= c1, c1, 0))
            dqt[...] = jnp.zeros_like(dqt)

            @pl.loop(0, j + 1)
            def _(b):
                keys = kv[g, b].reshape(512, 128)
                at = 512 * b + lax.broadcasted_iota(jnp.int32, (512, 512), 0)
                ok = (at >= start) & (at <= place)
                pt = jnp.where(ok, jnp.exp(dott(keys, qj) - lse_row), 0.0)
                ds = (pt * (dott(keys, doj) - delta_row)).astype(BF)
                acc[b] += dot(ds, qj) + dot(pt.astype(BF), doj)
                dqt[...] += dot(kvt[:, pl.ds(pl.multiple_of(512 * b, 512), 512)], ds)

            dq = dqt[...].T
            rows = pl.ds(128 * j, 128)
            cs, sn = cos[g, rows, :], sin[g, rows, :]
            for t in range(2):
                v = pair_heads(dq[256 * t: 256 * t + 128], dq[256 * t + 128: 256 * t + 256], True) * (HD ** -0.5)
                dqkv[g, rows, 128 * t: 128 * t + 128] = (v * cs - swap_halves(v) * sn).astype(BF)
            if no == 0 and j == 2:
                pump([tail2])
            if no == 1 and j == 2:
                pump(jobs_out)
        dkv_s[no] = acc[...].astype(BF).reshape(4, 4, 128, 128)
        waits[no] = others(w, y, "y", lambda p, no=no: dkv_s.at[no, :, p], dkv_r.at[no])
        if no == 0:
            pump(jobs_down)
            pump(jobs)
    pump(jobs)
    ends = [hand_out(w, s_gate, f_gate, c, x), hand_out(w, s_up, f_up, c, x)]
    pump(ends)
    pump([tail2])
    loads[2].wait()
    dv = dqkv[:, :, 0:256].reshape(1024, 256)

    @pl.loop(0, 8)
    def _(i):
        cols = pl.ds(pl.multiple_of(256 * i, 256), 256)
        d_q[i // 2, i % 2] = dot(n1v[:, :, :, cols].reshape(1024, 256).T, dv).astype(BF).reshape(4, 4, 16, 256)

    jobs_q = [
        col_job(w, d_q, re0, te0, qe0, s_q, 0, z, y, lsem.at[12]),
        col_job(w, d_q, re1, te1, qe1, s_q, 1, z, y, lsem.at[13]),
    ]
    pump(jobs_q)

    state = {}
    for no, g in enumerate((g0, g1)):
        for a in waits[no]:
            w.got(*a)
        for j in range(4):
            rows = pl.ds(128 * j, 128)
            v = dkv_s[no, j, y].astype(F32)
            for k in range(3):
                v += dkv_r[no, k, j].astype(F32)
            turned = v * cos[g, rows, :] - swap_halves(v) * sin[g, rows, :]
            dqkv[g, rows, 256:384] = jnp.where(lanes(v.shape) < 64, turned, v).astype(BF)

        @pl.loop(0, 8)
        def _(i):
            wt = wqkv[i // 2, i % 2].reshape(256, 384)
            p4[g, :, :, pl.ds(pl.multiple_of(256 * i, 256), 256)] = dott(dqkv[g], wt).astype(BF).reshape(4, 128, 256)

        if no == 0:
            scatter8_core(w, p4, core_r, state)
    rs = scatter8_ring(w, p4, core_r, hop, fin, state)
    pump([rs])
    pump([rs])
    dv = dqkv[:, :, 256:384].reshape(1024, 128)

    @pl.loop(0, 8)
    def _(i):
        cols = pl.ds(pl.multiple_of(256 * i, 256), 256)
        d_kv[i // 2, i % 2] = dot(n1v[:, :, :, cols].reshape(1024, 256).T, dv).astype(BF).reshape(4, 4, 16, 128)

    jobs_kv = [
        col_job(w, d_kv, rf0, tf0, qf0, s_kv, 0, z, y, lsem.at[14]),
        col_job(w, d_kv, rf1, tf1, qf1, s_kv, 1, z, y, lsem.at[15]),
    ]
    pump(jobs_kv)

    @pl.loop(0, 8)
    def _(i):
        rows = pl.ds(pl.multiple_of(i * 16, 16), 16)
        v = h[rows, :] + s2v[x, rows, :].astype(F32) + fin2[0, rows, :].astype(F32) + fin2[1, rows, :].astype(F32)
        out[rows, :] = v.astype(BF)

    pump([rs])
    pump(jobs_out)
    pump(jobs_q)
    pump(jobs_kv)
    more = [transpose_zx(w, s_out, lambda zz: f_out, z, x, lsem.at[17])]
    pump(more)
    pump(jobs_q)
    pump(jobs_kv)
    more += [hand_out(w, s_q, f_q, c, x), hand_out(w, s_kv, f_kv, c, x)]
    pump(more[1:])
    pump(jobs_down)
    down_out[...] = s_down[0:44, :].astype(F32)
    pump(ends)
    gain1, gain2 = gains[0], gains[1]
    total = jnp.zeros((16, 128), F32)
    for f, wt, res in ((f_gate, w_gate, gate_out), (f_up, w_up, up_out)):
        for t in range(44):
            tile = None
            for r, move in collect_moves(t):
                piece = take_lanes(lambda a: f[r, :, 128 * a: 128 * a + 128].astype(F32), [move])
                tile = piece if tile is None else tile + piece
            cols = slice(128 * t, 128 * t + 128)
            total += tile * wt[:, cols].astype(F32)
            res[:, cols] = tile * gain2
    gain_out[1] = jnp.broadcast_to(jnp.sum(total, axis=1, keepdims=True), (16, 128))
    pump([rs])

    @pl.loop(0, 8)
    def _(i):
        rows = pl.ds(pl.multiple_of(i * 16, 16), 16)
        e = p4[c, x, rows, :].astype(F32) + core_r[3, rows, :].astype(F32)
        e = e + fin[0, rows, :].astype(F32) + fin[1, rows, :].astype(F32)
        v = x_ref[rows, :].astype(F32)
        r = lax.rsqrt(jnp.mean(v * v, axis=1, keepdims=True) + EPS)
        gt[rows, :] = dh[rows, :] + r * e - v * (r * r * r * jnp.mean(e * v, axis=1, keepdims=True))

    pump(more)
    wo_out[...] = f_out[...].astype(F32)
    total = jnp.zeros((16, 128), F32)
    for r in range(8):
        for t in range(2):
            cols = slice(256 * r + 128 * t, 256 * r + 128 * t + 128)
            tile = f_q[r, :, 128 * t: 128 * t + 128].astype(F32)
            total += tile * wq[:, cols].astype(F32)
            q_out[:, cols] = tile * gain1
    heads = [f_kv[2 * a].astype(F32) + f_kv[2 * a + 1].astype(F32) for a in range(4)]
    for t in range(2):
        cols = slice(128 * t, 128 * t + 128)
        for res, wt, lower in ((k_out, wk, True), (v_out, wv, False)):
            tile = pair_heads(heads[2 * t], heads[2 * t + 1], lower)
            total += tile * wt[:, cols].astype(F32)
            res[:, cols] = tile * gain1
    gain_out[0] = jnp.broadcast_to(jnp.sum(total, axis=1, keepdims=True), (16, 128))
    w.drain()


def backward_attention(
        lens, gains, wq, wk, wv, w_gate, w_up, da, dh, x, h, cos, sin, n1g, wqkv, wout, qp, kv, o, lse,
        s2, g_gate, g_up, g_down, r1_down, cid):
    sds = jax.ShapeDtypeStruct
    vm, hb = pl.BlockSpec(memory_space=VMEM), pl.BlockSpec(memory_space=ANY)
    outs = [sds((128, 2048), BF)] + [sds(a, F32) for a in (
        (128, 2048), (2, 16, 128), (16, 2048), (16, 256), (16, 256), (16, 2048), (16, 5632), (16, 5632), (44, 2048))]
    b = lambda *s: VMEM(s, BF)
    ns = (768, 768, 256, 128)
    r1 = [b(3, 4, 4, 16, 768)] * 4 + [b(2, 3, 4, 48, 1024)] + [b(3, 4, 16, 1024)] * 2
    r1 += [b(3, 4, 4, 16, 256)] * 2 + [b(3, 4, 4, 16, 128)] * 2
    t1 = [b(4, 4, 16, 768)] * 4 + [b(4, 48, 1024)] * 2 + [b(4, 16, 1024)] * 2
    t1 += [b(4, 4, 16, 256)] * 2 + [b(4, 4, 16, 128)] * 2
    r2 = [b(3, 4, 16, 768)] * 4 + [b(3, 48, 1024)] * 2 + [b(3, 16, 1024)] * 2
    r2 += [b(3, 4, 16, 256)] * 2 + [b(3, 4, 16, 128)] * 2
    return pl.pallas_call(
        m3_kernel,
        out_shape=outs,
        in_specs=[pl.BlockSpec(memory_space=pltpu.SMEM)] + [vm] * 6 + [hb] + [vm] * 5 + [hb] + [vm] * 6 + [hb] * 5,
        out_specs=[vm] * 10,
        scratch_shapes=[
            b(8, 16, 768), b(8, 16, 768), b(8, 16, 256), b(8, 16, 128), b(16, 2048),
            b(2, 4, 128, 2048), b(2, 4, 128, 2048), b(4, 128, 2048), b(2, 4, 512, 128), VMEM((2, 4, 512), F32),
            VMEM((4, 512, 128), F32), b(128, 2048), VMEM((128, 512), F32), b(2, 4, 4, 128, 128),
            b(2, 3, 4, 128, 128), b(2, 512, 384), b(2, 4, 128, 2048), b(4, 128, 2048), b(2, 64, 2048),
            b(2, 128, 2048), b(2, 64, 2048), b(2, 128, 2048),
            b(4, 2, 4, 4, 16, 256), b(4, 2, 4, 4, 16, 128), b(4, 4, 16, 2048),
        ] + r1 + t1 + r2 + [
            b(2, 4, 16, 768), b(2, 4, 16, 768), b(2, 4, 16, 256), b(2, 4, 16, 128), b(48, 2048), b(16, 2048),
            pltpu.SemaphoreType.DMA((150,)), pltpu.SemaphoreType.DMA((150,)), pltpu.SemaphoreType.DMA((18,)),
        ],
        compiler_params=comm_params(cid, 63),
        name="backward_attention",
    )(lens, gains, wq, wk, wv, w_gate, w_up, da, dh, x, h, cos, sin, n1g, wqkv, wout, qp, kv, o, lse, s2, g_gate, g_up, g_down, r1_down)


def copy_kernel(*refs):
    n = len(refs) // 2
    copies = [pltpu.make_async_copy(refs[i], refs[n + i], refs[-1].at[i]) for i in range(n)]
    for cp in copies:
        cp.start()
    for cp in copies:
        cp.wait()


def copied(arrays):
    hb = pl.BlockSpec(memory_space=ANY)
    return pl.pallas_call(
        copy_kernel,
        out_shape=[jax.ShapeDtypeStruct(a.shape, a.dtype) for a in arrays],
        in_specs=[hb] * len(arrays),
        out_specs=[hb] * len(arrays),
        scratch_shapes=[pltpu.SemaphoreType.DMA((len(arrays),))],
        name="results",
    )(*arrays)


def local(tokens, lengths, attn_gain, w_query, w_key, w_value, w_out, mlp_gain, w_gate, w_up, w_down, cotangent):
    lens = lax.all_gather(lengths, "core", axis=0, tiled=True)
    gains = jnp.broadcast_to(jnp.stack([attn_gain, mlp_gain]).astype(F32)[..., None], (2, 16, 128))
    h, n1g, qp, kv, o, lse, wqkv, wout, cos, sin, dh, da, s2, g_gate, g_up, g_down, r1_down = forward_layer(
        lens, gains, tokens, cotangent, w_query, w_key, w_value, w_out, w_gate, w_up, w_down, 1)
    col = (4, 2, 4, 4, 16, 768)
    output, grad_tokens, gain, g_q, g_k, g_v, g_o, g_gate, g_up, g_down = backward_attention(
        lens, gains, w_query, w_key, w_value, w_gate, w_up, da, dh, tokens, h, cos, sin, n1g, wqkv, wout,
        qp, kv, o, lse, s2, g_gate.reshape(col), g_up.reshape(col), g_down, r1_down, 2)
    output, grad_tokens, g_q, g_k, g_v, g_o, g_gate, g_up, g_down = copied(
        (output, grad_tokens, g_q, g_k, g_v, g_o, g_gate, g_up, g_down))
    return (output, grad_tokens, gain[0, :, 0], g_q, g_k, g_v, g_o, gain[1, :, 0], g_gate, g_up, g_down)


def solution(mesh):
    fine = Mesh(mesh.devices.reshape(4, 2, 4, 4), ALL)
    rows, flat = P(ALL, None), P(ALL)
    in_specs = (rows, P(("z", "core"), None), flat, rows, rows, rows, rows, flat, rows, rows, rows, rows)
    out_specs = (rows, rows, flat, rows, rows, rows, rows, flat, rows, rows, rows)
    return jax.shard_map(local, mesh=fine, in_specs=in_specs, out_specs=out_specs, check_vma=False)
```

```python
import functools
import math

import jax
import jax.numpy as jnp
from jax import lax
from jax.experimental import pallas as pl
from jax.experimental.pallas import tpu as pltpu
from jax.sharding import Mesh
from jax.sharding import PartitionSpec as P

HEADS = 32
KV_HEADS = 4
HD = 64
EPS = 1e-05
THETA = 10000.0
NEG = -1e30
BF = jnp.bfloat16
F32 = jnp.float32
ANY = pl.ANY
VMEM = pltpu.VMEM
TP = ("x", "core")
DP = ("z", "y")
ALL = ("z", "core", "x", "y")


def tdot(a, b):
    return lax.dot_general(a, b, (((0,), (0,)), ((), ())), preferred_element_type=F32)


def dott(a, b):
    return lax.dot_general(a, b, (((1,), (1,)), ((), ())), preferred_element_type=F32)


def dot(a, b):
    return jnp.dot(a, b, preferred_element_type=F32)


class Wire:
    def __init__(self, ssem, rsem):
        self.ssem, self.rsem, self.sent = ssem, rsem, []

    def put(self, src, dst, k, to):
        cp = pltpu.make_async_remote_copy(
            src_ref=src, dst_ref=dst, send_sem=self.ssem.at[k], recv_sem=self.rsem.at[k],
            device_id=to, device_id_type=pl.DeviceIdType.MESH)
        cp.start()
        self.sent.append(cp)
        return cp

    def settle(self, copies):
        for cp in copies:
            cp.wait_send()
        done = {id(cp) for cp in copies}
        self.sent = [cp for cp in self.sent if id(cp) not in done]

    def got(self, dst, k, to):
        pltpu.make_async_remote_copy(
            src_ref=dst, dst_ref=dst, send_sem=self.ssem.at[k], recv_sem=self.rsem.at[k],
            device_id=to, device_id_type=pl.DeviceIdType.MESH).wait_recv()

    def drain(self):
        for cp in self.sent:
            cp.wait_send()


def greet(peers):
    barrier = pltpu.get_barrier_semaphore()
    for to in peers:
        pl.semaphore_signal(barrier, inc=1, device_id=to, device_id_type=pl.DeviceIdType.MESH)
    pl.semaphore_wait(barrier, len(peers))


def cx_ring():
    c, x = lax.axis_index("core"), lax.axis_index("x")
    right, left, opp = lax.rem(x + 1, 4), lax.rem(x + 3, 4), lax.rem(x + 2, 4)
    return c, x, right, left, opp, {"x": right}, {"x": left}, {"core": 1 - c}


def comm_params(cid, mb=None):
    kw = {} if mb is None else {"vmem_limit_bytes": mb << 20}
    return pltpu.CompilerParams(collective_id=cid, has_side_effects=True, **kw)


class Mail(Wire):
    def __init__(self, ssem, rsem):
        super().__init__(ssem, rsem)
        self.used = 0

    def new(self):
        self.used += 1
        return self.used - 1


def around(q):
    return lax.rem(q + 1, 4), lax.rem(q + 3, 4), lax.rem(q + 2, 4)


def ring(w, s, axis, q):
    right, left, opp = around(q)
    to_r, to_l = {axis: right}, {axis: left}
    k = [w.new() for _ in range(4)]
    w.put(s(q, None), s(q, None), k[0], to_r)
    w.put(s(q, None), s(q, None), k[1], to_l)
    yield
    w.got(s(left, None), k[0], to_l)
    w.put(s(left, 0), s(left, 0), k[2], to_r)
    w.got(s(right, None), k[1], to_r)
    w.put(s(right, 1), s(right, 1), k[3], to_l)
    yield
    w.got(s(opp, 0), k[2], to_l)
    w.got(s(opp, 1), k[3], to_r)


def col_flows(w, W, z, y):
    cut = lambda h: slice(None) if h is None else pl.ds(2 * h, 2)

    def first():
        yield from ring(w, lambda p, h: W.at[z, 0, cut(h), p], "y", y)
        yield from ring(w, lambda p, h: W.at[p, 0, cut(h)], "z", z)

    def second():
        yield from ring(w, lambda p, h: W.at[p, 1, cut(h), y], "z", z)
        yield from ring(w, lambda p, h: W.at[:, 1, cut(h), p], "y", y)

    return [first(), second()]


def row_flows(w, W, z, y):
    n = W.shape[-1] // 4
    cut = lambda b, h: pl.ds(2 * n * b, 2 * n) if h is None else pl.ds(2 * n * b + n * h, n)

    def first():
        yield from ring(w, lambda p, h: W.at[z, p, :, cut(0, h)], "y", y)
        yield from ring(w, lambda p, h: W.at[p, :, :, cut(0, h)], "z", z)

    def second():
        yield from ring(w, lambda p, h: W.at[p, y, :, cut(1, h)], "z", z)
        yield from ring(w, lambda p, h: W.at[:, p, :, cut(1, h)], "y", y)

    return [first(), second()]


def straight(w, stages):
    for s, axis, q in stages:
        ks = {}
        for k in (1, 3, 2):
            ks[k] = w.new()
            w.put(s(q), s(q), ks[k], {axis: lax.rem(q + k, 4)})
        yield
        for k in (1, 3, 2):
            frm = lax.rem(q + 4 - k, 4)
            w.got(s(frm), ks[k], {axis: frm})


def col_straight(w, W, z, y):
    return [straight(w, [(lambda p: W.at[z, 0, :, p], "y", y), (lambda p: W.at[p, 0], "z", z)]),
            straight(w, [(lambda p: W.at[p, 1, :, y], "z", z), (lambda p: W.at[:, 1, :, p], "y", y)])]


def row_straight(w, W, z, y):
    n = W.shape[-1] // 2
    a, b = pl.ds(0, n), pl.ds(n, n)
    return [straight(w, [(lambda p: W.at[z, p, :, a], "y", y), (lambda p: W.at[p, :, :, a], "z", z)]),
            straight(w, [(lambda p: W.at[p, y, :, b], "z", z), (lambda p: W.at[:, p, :, b], "y", y)])]


def pump(flows):
    for f in flows:
        next(f, None)


def gather8(w, src, dst):
    c, x, right, left, opp, to_r, to_l, to_c = cx_ring()
    rows = dst.shape[2]
    lo, hi = pl.ds(0, rows // 2), pl.ds(rows // 2, rows // 2)
    k = [w.new() for _ in range(10)]
    out = []
    out += [w.put(src.at[lo], dst.at[c, x, lo], k[0], to_r)]
    out += [w.put(src.at[hi], dst.at[c, x, hi], k[1], to_l)]
    out += [w.put(src.at[hi], dst.at[c, x, hi], k[2], to_r)]
    out += [w.put(src.at[lo], dst.at[c, x, lo], k[3], to_l)]
    out += [w.put(src, dst.at[c, x], k[4], to_c)]
    yield
    w.got(dst.at[c, left, lo], k[0], to_l)
    out += [w.put(dst.at[c, left, lo], dst.at[c, left, lo], k[5], to_r)]
    w.got(dst.at[c, right, hi], k[1], to_r)
    out += [w.put(dst.at[c, right, hi], dst.at[c, right, hi], k[6], to_l)]
    yield
    w.got(dst.at[1 - c, x], k[4], to_c)
    yield
    w.got(dst.at[c, left, hi], k[2], to_l)
    out += [w.put(dst.at[c, left], dst.at[c, left], k[7], to_c)]
    w.got(dst.at[c, right, lo], k[3], to_r)
    out += [w.put(dst.at[c, right], dst.at[c, right], k[8], to_c)]
    yield
    w.got(dst.at[1 - c, left], k[7], to_c)
    w.got(dst.at[1 - c, right], k[8], to_c)
    yield
    w.got(dst.at[c, opp, lo], k[5], to_l)
    w.got(dst.at[c, opp, hi], k[6], to_r)
    out += [w.put(dst.at[c, opp], dst.at[c, opp], k[9], to_c)]
    yield
    w.got(dst.at[1 - c, opp], k[9], to_c)
    w.settle(out)


def add_to(dst, other, r0, rows, step=16):
    @pl.loop(0, rows // step)
    def _(i):
        a = pl.ds(pl.multiple_of(r0 + i * step, step), step)
        b = pl.ds(pl.multiple_of(i * step, step), step)
        dst[a, :] = (dst[a, :].astype(F32) + other[b, :].astype(F32)).astype(dst.dtype)


def scatter8_core(w, p, core_r, state, only=None):
    c, x, right, left, opp, to_r, to_l, to_c = cx_ring()
    if not state:
        state["k"], state["out"] = [w.new() for _ in range(4)], []
    for i, xx in enumerate((opp, right, left, x)):
        if only is None or only == i:
            state["out"].append(w.put(p.at[1 - c, xx], core_r.at[i], state["k"][i], to_c))


def scatter8_ring(w, p, core_r, hop, fin, state):
    c, x, right, left, opp, to_r, to_l, to_c = cx_ring()
    rows = p.shape[2]
    half = rows // 2
    lo, hi = pl.ds(0, half), pl.ds(half, half)
    kc, out = state["k"], state["out"]
    k = [w.new() for _ in range(6)]
    w.got(core_r.at[0], kc[0], to_c)
    add_to(p.at[c, opp], core_r.at[0], 0, rows)
    out += [w.put(p.at[c, opp, lo], hop.at[0], k[0], to_r)]
    out += [w.put(p.at[c, opp, hi], hop.at[1], k[1], to_l)]
    yield
    w.got(core_r.at[1], kc[1], to_c)
    add_to(p.at[c, right], core_r.at[1], 0, rows)
    out += [w.put(p.at[c, right, hi], fin.at[0, hi], k[2], to_r)]
    w.got(core_r.at[2], kc[2], to_c)
    add_to(p.at[c, left], core_r.at[2], 0, rows)
    out += [w.put(p.at[c, left, lo], fin.at[1, lo], k[3], to_l)]
    yield
    w.got(hop.at[0], k[0], to_l)
    add_to(p.at[c, right], hop.at[0], 0, half)
    out += [w.put(p.at[c, right, lo], fin.at[0, lo], k[4], to_r)]
    w.got(hop.at[1], k[1], to_r)
    add_to(p.at[c, left], hop.at[1], half, half)
    out += [w.put(p.at[c, left, hi], fin.at[1, hi], k[5], to_l)]
    yield
    w.got(core_r.at[3], kc[3], to_c)
    w.got(fin.at[0, hi], k[2], to_l)
    w.got(fin.at[1, lo], k[3], to_r)
    w.got(fin.at[0, lo], k[4], to_l)
    w.got(fin.at[1, hi], k[5], to_r)
    w.settle(out)


def lanes(shape):
    return lax.broadcasted_iota(jnp.int32, shape, len(shape) - 1)


def take_lanes(load, moves):
    out = None
    for src, lo, hi in moves:
        a, shift = (src - lo) // 128, (src - lo) % 128
        split = 128 - shift
        turned = lambda t: pltpu.roll(load(t), (128 - shift) % 128, 1) if shift else load(t)
        if hi <= split:
            piece = turned(a)
        elif lo >= split:
            piece = turned(a + 1)
        else:
            piece = jnp.where(lanes((16, 128)) < split, turned(a), turned(a + 1))
        at = lanes(piece.shape)
        out = jnp.where((at >= lo) & (at < hi), piece, jnp.zeros_like(piece) if out is None else out)
    return out


def fetch(pairs, sems):
    copies = [pltpu.make_async_copy(src, dst, sems.at[i]) for i, (src, dst) in enumerate(pairs)]
    for cp in copies:
        cp.start()
    return copies


def unit_place(z, c, x, y):
    return ((z * 2 + c) * 4 + x) * 4 + y


def spread_moves(r, t):
    out = []
    for s in range(16):
        d0 = 48 * s
        lo, hi = max(d0, 128 * t), min(d0 + 44, 128 * t + 128)
        if lo < hi:
            unit = unit_place(s // 4, r % 2, r // 2, s % 4)
            out.append((44 * unit + lo - d0, lo - 128 * t, hi - 128 * t))
    return out


def collect_moves(t):
    out = []
    for unit in range(128):
        d0 = 44 * unit
        lo, hi = max(d0, 128 * t), min(d0 + 44, 128 * t + 128)
        if lo < hi:
            z, c, x, y = unit // 32, unit // 16 % 2, unit // 4 % 4, unit % 4
            out.append((2 * x + c, (48 * (4 * z + y) + lo - d0, lo - 128 * t, hi - 128 * t)))
    return out


def swap_halves(u):
    first = lax.rem(lanes(u.shape), 64) < 32
    return jnp.where(first, pltpu.roll(u, 96, u.ndim - 1), pltpu.roll(u, 32, u.ndim - 1))


def entry(peers, extra=None):
    barrier = pltpu.get_barrier_semaphore()
    for to in peers:
        pl.semaphore_signal(barrier, inc=1, device_id=to, device_id_type=pl.DeviceIdType.MESH)
    if extra is None:
        pl.semaphore_wait(barrier, len(peers))
        return
    more, to = extra

    @pl.when(more)
    def _():
        pl.semaphore_signal(barrier, inc=1, device_id=to, device_id_type=pl.DeviceIdType.MESH)
        pl.semaphore_wait(barrier, len(peers) + 1)

    @pl.when(jnp.logical_not(more))
    def _():
        pl.semaphore_wait(barrier, len(peers))


def tp_peers(c, x):
    r = 2 * x + c
    out = []
    for k in range(1, 8):
        rr = lax.rem(r + k, 8)
        out.append((rr, {"x": rr // 2, "core": lax.rem(rr, 2)}))
    return out


def spread(w, src, W, z, c, x, y, local_sem):
    ks = [w.new() for _ in range(7)]
    for k, (rr, to) in zip(ks, tp_peers(c, x)):
        w.put(src.at[rr], W.at[z, c, x, y], k, to)
    own = pltpu.make_async_copy(src.at[2 * x + c], W.at[z, c, x, y], local_sem)
    own.start()
    yield
    r = 2 * x + c
    for i, k in enumerate(ks):
        rr = lax.rem(r + 7 - i, 8)
        w.got(W.at[z, lax.rem(rr, 2), rr // 2, y], k, {"x": rr // 2, "core": lax.rem(rr, 2)})
    own.wait()


def transpose_zx(w, src, dst_of, z, x, local_sem):
    k = w.new()
    to = {"z": x, "x": z}

    def far():
        return pltpu.make_async_remote_copy(
            src_ref=src, dst_ref=dst_of(x), send_sem=w.ssem.at[k], recv_sem=w.rsem.at[k],
            device_id=to, device_id_type=pl.DeviceIdType.MESH)

    def near():
        return pltpu.make_async_copy(src, dst_of(x), local_sem)

    @pl.when(z != x)
    def _():
        far().start()

    @pl.when(z == x)
    def _():
        near().start()

    yield

    @pl.when(z != x)
    def _():
        far().wait_send()
        w.got(dst_of(z), k, to)

    @pl.when(z == x)
    def _():
        near().wait()


def attend(q, keys, j, y, c1, c2):
    m, n = q.shape[0], keys.shape[0]
    s = dott(q, keys)
    row = lax.broadcasted_iota(jnp.int32, (m, 1), 0)
    place = (4 * j + y) * 128 + lax.rem(row, 128)
    start = jnp.where(place >= c2, c2, jnp.where(place >= c1, c1, 0))
    at = lax.broadcasted_iota(jnp.int32, (m, n), 1)
    s = jnp.where((at >= start) & (at <= place), s, NEG)
    top = jnp.max(s, axis=1, keepdims=True)
    e = jnp.exp(s - top)
    total = jnp.sum(e, axis=1, keepdims=True)
    return dot(e.astype(BF), keys) / total, top + jnp.log(total)


def pair_heads(first, second, lower):
    low = lanes(first.shape) < 64
    if lower:
        return jnp.where(low, first, pltpu.roll(second, 64, 1))
    return jnp.where(low, pltpu.roll(first, 64, 1), second)


def forward_kernel(lens, gains_in, x_in, cot_in, wq_in, wk_in, wv_in, out_s, gate_in, up_in, down_in,
                   h_out, n1_out, qp_out, kv_out, o_out, lse_out, wqkv_out, wout_out, cos_out, sin_out,
                   dh_out, da_out, s2, g_gate, g_up, g_down, r1_down,
                   cos, sin, h, qp, kv, o, lse, wqkv, wout, n1, cv, wg, wu, wd, p, core_r, hop, fin,
                   dact, a_all, dg_all, du_all, core2, d_down, qkv_s, gate_s, up_s,
                   gains, x_ref, cot, wq, wk, wv, w_gate, w_up, w_down, ssem, rsem, lsem, osem, isem):
    z, c, x, y = (lax.axis_index(a) for a in ALL)
    peers = [to for _, to in tp_peers(c, x)]
    for axis, q in (("y", y), ("z", z)):
        peers += [{axis: lax.rem(q + k, 4)} for k in (1, 2, 3)]
    w = Mail(ssem, rsem)
    loads = fetch(((gains_in, gains), (wq_in, wq), (wk_in, wk), (wv_in, wv), (x_in, x_ref), (down_in, w_down),
                   (gate_in, w_gate), (up_in, w_up), (cot_in, cot)), isem)
    saved = []

    def save(src, dst):
        cp = pltpu.make_async_copy(src, dst, osem.at[len(saved)])
        cp.start()
        saved.append(cp)
        return cp

    for cp in loads[:4]:
        cp.wait()
    gain1, gain2 = gains[0], gains[1]
    for r in range(8):
        for t in range(2):
            at = 256 * r + 128 * t
            qkv_s[r, :, 128 * t: 128 * t + 128] = (wq[:, at: at + 128].astype(F32) * gain1).astype(BF)
        t, odd = r // 4, r // 2 % 2
        kt, vt = wk[:, 128 * t: 128 * t + 128].astype(F32), wv[:, 128 * t: 128 * t + 128].astype(F32)
        kt, vt = (pltpu.roll(kt, 64, 1), vt) if odd else (kt, pltpu.roll(vt, 64, 1))
        qkv_s[r, :, 256:384] = (jnp.where(lanes(kt.shape) < 64, kt, vt) * gain1).astype(BF)
    entry(peers, (z != x, {"z": x, "x": z}))

    sp_qkv = spread(w, qkv_s, wqkv, z, c, x, y, lsem.at[0])
    pump([sp_qkv])
    loads[4].wait()

    @pl.loop(0, 8)
    def _(i):
        rows = pl.ds(pl.multiple_of(i * 16, 16), 16)
        v = x_ref[rows, :].astype(F32)
        n1[c, x, rows, :] = (v * lax.rsqrt(jnp.mean(v * v, axis=1, keepdims=True) + EPS)).astype(BF)

    ag_n1 = gather8(w, n1.at[c, x], n1)
    pump([ag_n1])
    for cp in loads[5:]:
        cp.wait()
    wd[z, y] = jnp.concatenate([w_down[...], jnp.zeros((4, 2048), BF)], axis=0)
    pump([sp_qkv])
    fl_qkv = col_straight(w, wqkv, z, y)
    pump(fl_qkv)
    for src, dst in ((w_gate, gate_s), (w_up, up_s)):
        for r in range(8):
            for t in range(6):
                load = lambda a: src[:, 128 * a: 128 * a + 128].astype(F32)
                dst[r, :, 128 * t: 128 * t + 128] = (take_lanes(load, spread_moves(r, t)) * gain2).astype(BF)
    pump([ag_n1])
    pump([ag_n1])
    pump(fl_qkv)
    spreads = [spread(w, gate_s, wg, z, c, x, y, lsem.at[2]), spread(w, up_s, wu, z, c, x, y, lsem.at[3])]
    pump(spreads)
    tr_out = transpose_zx(w, out_s, lambda zz: wout.at[zz, y], z, x, lsem.at[1])
    pump([tr_out])
    fl_down = row_flows(w, wd, z, y)
    pump(fl_down)

    for g in range(2):
        lane = lanes((128, 128))
        freq = jnp.exp(lax.rem(lane, 32).astype(F32) * (-2.0 * math.log(THETA) / HD))
        c1, c2 = lens[g, 0], lens[g, 0] + lens[g, 1]

        @pl.loop(0, 4)
        def _(j):
            place = (4 * j + y) * 128 + lax.broadcasted_iota(jnp.int32, (128, 128), 0)
            start = jnp.where(place >= c2, c2, jnp.where(place >= c1, c1, 0))
            angle = (place - start).astype(F32) * freq
            rows = pl.ds(pl.multiple_of(128 * j, 128), 128)
            cos[g, rows, :] = jnp.cos(angle)
            turned = jnp.sin(angle)
            sin[g, rows, :] = jnp.where(lax.rem(lane, 64) < 32, -turned, turned)

    pump([ag_n1])
    pump([tr_out])
    fl_out = row_straight(w, wout, z, y)
    pump(fl_out)
    pump(spreads)
    fl_gu = col_flows(w, wg, z, y) + col_flows(w, wu, z, y)
    pump(fl_gu)
    fl_mlp = fl_down + fl_gu
    pump([ag_n1])
    pump([ag_n1])
    pump(fl_qkv)
    pump([ag_n1])
    weights = wqkv[...].reshape(2048, 384)

    def project(g, keys_too):
        u = dot(n1[g].reshape(512, 2048), weights)
        cs, sn = cos[g], sin[g]
        if keys_too:
            v = u[:, 256:384]
            turned = jnp.where(lanes(v.shape) < 64, v * cs + swap_halves(v) * sn, v)
            kv[g, :, y] = turned.astype(BF).reshape(4, 128, 128)
        for t in range(2):
            v = u[:, 128 * t: 128 * t + 128]
            v = (v * cs + swap_halves(v) * sn) * (HD ** -0.5)
            low = lanes(v.shape) < 64
            for b, head in enumerate((v, pltpu.roll(v, 64, 1))):
                rows = pl.ds(128 * (2 * t + b), 128)
                qp[g, :, rows, :] = jnp.where(low, head, 0.0).astype(BF).reshape(4, 128, 128)

    g0, g1 = 1 - c, c
    to_c = {"core": 1 - c}
    pump(fl_mlp)
    project(g0, True)
    fl_kv = [straight(w, [(lambda pp: kv.at[g0, :, pp], "y", y)])]
    pump(fl_kv)
    pump(fl_out)
    ag_cot = gather8(w, cot, cv)
    pump([ag_cot])
    project(g1, False)
    keep_n1 = save(n1, n1_out)
    save(wqkv, wqkv_out)
    save(cos, cos_out)
    save(sin, sin_out)
    keep_cot = save(cot, cv.at[c, x])
    pump(fl_mlp[0::2])
    pump(fl_kv)
    k_kv = w.new()
    w.put(kv.at[g0], kv.at[g0], k_kv, to_c)
    pump(fl_mlp[1::2])

    state = {}
    for turn_no, g in enumerate((g0, g1)):
        if turn_no == 1:
            w.got(kv.at[g], k_kv, to_c)
            save(kv, kv_out)
            save(qp, qp_out)
            save(wout, wout_out)
        for j in range(4):
            n = 512 * (j + 1)
            keys = kv[g, 0:j + 1].reshape(n, 128)
            for t in range(2):
                part = qp[g, j, 256 * t: 256 * t + 256]
                res, total = attend(part, keys, j, y, lens[g, 0], lens[g, 0] + lens[g, 1])
                both = pair_heads(res[:128], res[128:], False)
                o[g, pl.ds(128 * j, 128), 128 * t: 128 * t + 128] = both.astype(BF)
                lse[g, pl.ds(j, 1), 256 * t: 256 * t + 256] = jnp.broadcast_to(total, (256, 128)).T[0:1, :]
            if j == 2:
                pump([ag_cot])
        pump(fl_out)
        out_w = wout[...].reshape(256, 2048)

        @pl.loop(0, 4)
        def _(i):
            p[g, i] = dot(o[g, pl.ds(pl.multiple_of(128 * i, 128), 128), :], out_w).astype(BF)

        if turn_no == 0:
            keep_n1.wait()
            scatter8_core(w, p, core_r, state)
    rs = scatter8_ring(w, p, core_r, hop, fin, state)
    pump([rs])
    pump([rs])
    save(o, o_out)
    save(lse, lse_out)
    pump([ag_cot])
    pump([ag_cot])
    pump([ag_cot])
    pump([rs])
    pump([ag_cot])
    pump(fl_mlp[0::2])
    pump(fl_mlp[1::2])
    pump([rs])

    @pl.loop(0, 8)
    def _(i):
        rows = pl.ds(pl.multiple_of(i * 16, 16), 16)
        v = x_ref[rows, :].astype(F32) + p[c, x, rows, :].astype(F32) + core_r[3, rows, :].astype(F32)
        v = v + fin[0, rows, :].astype(F32) + fin[1, rows, :].astype(F32)
        h[rows, :] = v
        n1[c, x, rows, :] = (v * lax.rsqrt(jnp.mean(v * v, axis=1, keepdims=True) + EPS)).astype(BF)

    keep_h = save(h, h_out)
    n2v = n1
    ag = gather8(w, n2v.at[c, x], n2v)
    pump([ag])
    pump(fl_down)
    keep_cot.wait()
    down = wd[...].reshape(768, 2048)

    @pl.loop(0, 2)
    def _(g):
        for t in range(2):
            v = dott(cv[g, 2 * t: 2 * t + 2].reshape(256, 2048), down)
            dact[g, 2 * t: 2 * t + 2] = v.astype(BF).reshape(2, 128, 768)

    pump([ag])
    pump([ag])
    pump(fl_gu)
    cc, xx, right, left, opp, to_r, to_l, to_c = cx_ring()
    st3, st2 = {}, {}

    def block(b, number):
        @pl.loop(0, 3)
        def _(i):
            cols = pl.ds(pl.multiple_of(256 * i, 256), 256)
            nv = n2v[:, b].reshape(256, 2048)
            gp = dot(nv, wg[:, :, :, :, :, cols].reshape(2048, 256))
            u = dot(nv, wu[:, :, :, :, :, cols].reshape(2048, 256))
            sig = jax.nn.sigmoid(gp)
            act = gp * sig
            d = dact[:, b, :, cols].reshape(256, 256).astype(F32)
            a_all[:, b, :, cols] = (act * u).astype(BF).reshape(2, 128, 256)
            dg_all[:, b, :, cols] = (d * u * sig * (1.0 + gp * (1.0 - sig))).astype(BF).reshape(2, 128, 256)
            du_all[:, b, :, cols] = (d * act).astype(BF).reshape(2, 128, 256)

        @pl.loop(0, 8)
        def _(i):
            part = dott(dg_all[:, b].reshape(256, 768), wg[i // 2, i % 2].reshape(256, 768))
            part += dott(du_all[:, b].reshape(256, 768), wu[i // 2, i % 2].reshape(256, 768))
            p[:, b, :, pl.ds(pl.multiple_of(256 * i, 256), 256)] = part.astype(BF).reshape(2, 128, 256)

        scatter8_core(w, p, core_r, st3, number)

    block(x, 3)
    pump([ag])
    pump([ag])
    block(left, 2)
    pump([ag])
    pump([ag])
    block(opp, 0)
    rs3 = scatter8_ring(w, p, core_r, hop, fin, st3)
    pump([rs3])
    block(right, 1)
    pump([rs3])
    at = a_all[...].reshape(1024, 768).T

    @pl.loop(0, 8)
    def _(i):
        cols = pl.ds(pl.multiple_of(256 * i, 256), 256)
        d_down[:, :, :, cols] = dot(at, cv[:, :, :, cols].reshape(1024, 256)).astype(BF).reshape(4, 4, 48, 256)

    first, second = pl.ds(0, 1024), pl.ds(1024, 1024)
    landed = others(w, y, "y", lambda pp: d_down.at[:, pp, :, first], r1_down.at[0])
    landed += others(w, z, "z", lambda pp: d_down.at[pp, :, :, second], r1_down.at[1])
    save(d_down, g_down)

    p2 = cv

    def out_part(g):
        @pl.loop(0, 8)
        def _(i):
            cols = pl.ds(pl.multiple_of(256 * i, 256), 256)
            part = dot(a_all[g].reshape(512, 768), wd[:, :, :, cols].reshape(768, 256))
            p2[g, :, :, cols] = part.astype(BF).reshape(4, 128, 256)

    pump([rs3])
    out_part(g0)
    scatter8_core(w, p2, core2, st2)
    out_part(g1)

    dg, du = dg_all[...].reshape(1024, 768), du_all[...].reshape(1024, 768)

    def stage(i, slot, k):
        return pltpu.make_async_copy(
            dact.at[slot, pl.ds(2 * k, 2)], (g_gate, g_up)[k].at[i], lsem.at[4 + 2 * slot + k])

    @pl.loop(0, 4)
    def _(i):
        for slot in range(2):
            cols = pl.ds(pl.multiple_of(512 * i + 256 * slot, 256), 256)
            t = n2v[:, :, :, cols].reshape(1024, 256).T

            @pl.when(i > 0)
            def _():
                stage(2 * i + slot - 2, slot, 0).wait()
                stage(2 * i + slot - 2, slot, 1).wait()

            dact[slot, 0:2] = dot(t, dg).astype(BF).reshape(2, 128, 768)
            dact[slot, 2:4] = dot(t, du).astype(BF).reshape(2, 128, 768)
            stage(2 * i + slot, slot, 0).start()
            stage(2 * i + slot, slot, 1).start()

    for i, b in enumerate((opp, right, left, x)):
        w.got(core2.at[i], st2["k"][i], to_c)
        add_to(p2.at[c, b], core2.at[i], 0, 128)
    save(p2.at[c], s2)
    pump([rs3])
    keep_h.wait()

    @pl.loop(0, 8)
    def _(i):
        rows = pl.ds(pl.multiple_of(i * 16, 16), 16)
        e = p[c, x, rows, :].astype(F32) + core_r[3, rows, :].astype(F32)
        e = e + fin[0, rows, :].astype(F32) + fin[1, rows, :].astype(F32)
        v = h[rows, :]
        r = lax.rsqrt(jnp.mean(v * v, axis=1, keepdims=True) + EPS)
        out = cot[rows, :].astype(F32) + r * e - v * (r * r * r * jnp.mean(e * v, axis=1, keepdims=True))
        h[rows, :] = out
        n1[c, x, rows, :] = out.astype(BF)

    save(h, dh_out)
    save(n1.at[c, x], da_out)
    w.drain()
    for slot in range(2):
        stage(6 + slot, slot, 0).wait()
        stage(6 + slot, slot, 1).wait()
    for a in landed:
        w.got(*a)
    for cp in saved:
        if all(cp is not a for a in (keep_n1, keep_h, keep_cot)):
            cp.wait()


def forward_layer(lens, gains, tokens, cot, wq, wk, wv, out_s, w_gate, w_up, w_down, cid):
    sds = jax.ShapeDtypeStruct
    hb = pl.BlockSpec(memory_space=ANY)
    col, big = (4, 2, 4, 4, 16, 768), (2, 4, 128, 2048)
    row, half, table = (128, 2048), (2, 4, 128, 768), ((2, 512, 128), F32)
    mid = [((2, 4, 512, 128), BF), ((2, 4, 4, 128, 128), BF), ((2, 512, 256), BF), ((2, 4, 512), F32),
           ((4, 2, 4, 4, 16, 384), BF), ((4, 4, 16, 2048), BF)]
    outs = [(row, F32), (big, BF)] + mid + [table, table] + [
        (row, F32), (row, BF), ((4, 128, 2048), BF), ((8, 2, 128, 768), BF), ((8, 2, 128, 768), BF),
        ((4, 4, 48, 2048), BF), ((2, 3, 4, 48, 1024), BF)]
    scratch = [table, table, (row, F32)] + mid + [
        (big, BF), (big, BF), (col, BF), (col, BF), ((4, 4, 48, 2048), BF),
        (big, BF), ((4, 128, 2048), BF), ((2, 64, 2048), BF), ((2, 128, 2048), BF),
        (half, BF), (half, BF), (half, BF), (half, BF), ((4, 128, 2048), BF), ((4, 4, 48, 2048), BF),
        ((8, 16, 384), BF), ((8, 16, 768), BF), ((8, 16, 768), BF),
        ((2, 16, 128), F32), (row, BF), (row, BF), ((16, 2048), BF), ((16, 256), BF), ((16, 256), BF),
        ((16, 5632), BF), ((16, 5632), BF), ((44, 2048), BF)]
    return pl.pallas_call(
        forward_kernel,
        out_shape=[sds(*a) for a in outs],
        in_specs=[pl.BlockSpec(memory_space=pltpu.SMEM)] + [hb] * 10,
        out_specs=[hb] * len(outs),
        scratch_shapes=[VMEM(*a) for a in scratch] + [
            pltpu.SemaphoreType.DMA((170,)), pltpu.SemaphoreType.DMA((170,)), pltpu.SemaphoreType.DMA((8,)),
            pltpu.SemaphoreType.DMA((18,)), pltpu.SemaphoreType.DMA((9,)),
        ],
        compiler_params=comm_params(cid, 63),
        name="forward_layer",
    )(lens, gains, tokens, cot, wq, wk, wv, out_s, w_gate, w_up, w_down)


def ring_tail(w, s, hop, fin):
    c, x, right, left, opp, to_r, to_l, to_c = cx_ring()
    half = s.shape[1] // 2
    lo, hi = pl.ds(0, half), pl.ds(half, half)
    k = [w.new() for _ in range(6)]
    w.put(s.at[opp, lo], hop.at[0], k[0], to_r)
    w.put(s.at[opp, hi], hop.at[1], k[1], to_l)
    w.put(s.at[right, hi], fin.at[0, hi], k[2], to_r)
    w.put(s.at[left, lo], fin.at[1, lo], k[3], to_l)
    yield
    w.got(hop.at[0], k[0], to_l)
    add_to(s.at[right], hop.at[0], 0, half)
    w.put(s.at[right, lo], fin.at[0, lo], k[4], to_r)
    w.got(hop.at[1], k[1], to_r)
    add_to(s.at[left], hop.at[1], half, half)
    w.put(s.at[left, hi], fin.at[1, hi], k[5], to_l)
    yield
    w.got(fin.at[0, hi], k[2], to_l)
    w.got(fin.at[1, lo], k[3], to_r)
    w.got(fin.at[0, lo], k[4], to_l)
    w.got(fin.at[1, hi], k[5], to_r)


def others(w, q, axis, piece, recv):
    ks = {}
    for k in (1, 3, 2):
        to = lax.rem(q + k, 4)
        ks[k] = w.new()
        w.put(piece(to), recv.at[k - 1], ks[k], {axis: to})
    return [(recv.at[k - 1], ks[k], {axis: lax.rem(q + 4 - k, 4)}) for k in (1, 3, 2)]


def sum_four(dst, own, recv, lead):
    total = math.prod(lead)

    @pl.loop(0, total)
    def _(i):
        at = (i,) if len(lead) == 1 else (i // lead[1], lax.rem(i, lead[1]))
        acc = own[at].astype(F32)
        for k in range(3):
            acc += recv[(k,) + at].astype(F32)
        dst[at] = acc.astype(dst.dtype)


def col_job(w, src, r1, t, r2, s, e, z, y, lsem):
    if e == 0:
        own, piece1, ax1, q1 = src.at[:, 0, :, y], lambda p: src.at[:, 0, :, p], "y", y
        piece2, ax2, q2 = lambda p: t.at[p], "z", z
    else:
        own, piece1, ax1, q1 = src.at[z, 1], lambda p: src.at[p, 1], "z", z
        piece2, ax2, q2 = lambda p: t.at[:, p], "y", y
    first = pltpu.make_async_copy(own, t, lsem)
    first.start()
    waits = others(w, q1, ax1, piece1, r1)
    yield
    first.wait()
    for a in waits:
        w.got(*a)
    sum_four(t, t, r1, (4, 4))
    waits = others(w, q2, ax2, piece2, r2)
    yield
    for a in waits:
        w.got(*a)
    sum_four(s.at[e], piece2(q2), r2, (4,))


def row_job(w, src, r1, t, r2, s, e, z, y, lsem, here=None):
    n = s.shape[-1] // 2
    rows = s.shape[0]
    cols = pl.ds(e * n, n)
    if len(src.shape) == 5:
        at = lambda *q: src.at[(e,) + q]
    else:
        at = lambda *q: src.at[q + (slice(None), cols)]
    if e == 0:
        piece1, ax1, q1, ax2, q2 = lambda p: at(slice(None), p), "y", y, "z", z
    else:
        piece1, ax1, q1, ax2, q2 = lambda p: at(p, slice(None)), "z", z, "y", y
    own = piece1(q1)
    first = pltpu.make_async_copy(own, t, lsem)
    first.start()
    waits = others(w, q1, ax1, piece1, r1) if here is None else []
    yield
    first.wait()
    for a in waits:
        w.got(*a)
    sum_four(t, t, r1, (4,))
    waits = others(w, q2, ax2, lambda p: t.at[p], r2)
    yield
    for a in waits:
        w.got(*a)

    @pl.loop(0, rows // 16)
    def _(i):
        at = pl.ds(pl.multiple_of(i * 16, 16), 16)
        acc = t[q2, at].astype(F32)
        for k in range(3):
            acc += r2[k, at].astype(F32)
        s[at, cols] = acc.astype(BF)


def hand_out(w, s, f, c, x):
    r = 2 * x + c
    ks = [w.new() for _ in range(7)]
    for k, (rr, to) in zip(ks, tp_peers(c, x)):
        w.put(s.at[lax.rem(rr, 2), rr // 2], f.at[r], k, to)
    f[r] = s[c, x]
    yield
    for i, k in enumerate(ks):
        rr = lax.rem(r + 7 - i, 8)
        w.got(f.at[rr], k, {"x": rr // 2, "core": lax.rem(rr, 2)})


def m3_kernel(lens, gains_in, wq_in, wk_in, wv_in, gate_in, up_in, da, dh_in, x_in, h_in, cos_in, sin_in, n1g, wqkv_in,
              wout_in, qp_in, kv_in, o_in, lse_in, s2, g_gate, g_up, g_down, r1_down,
              *rest):
    outs, rest = rest[:10], rest[10:]
    vals, rest = rest[:10], rest[10:]
    ins, rest = rest[:17], rest[17:]
    backward_body(lens, (gains_in, wq_in, wk_in, wv_in, gate_in, up_in, dh_in, x_in, h_in, cos_in, sin_in, wqkv_in,
                         wout_in, qp_in, kv_in, o_in, lse_in), ins, da, n1g, s2, g_gate, g_up, g_down, r1_down,
                  outs, vals, *rest)


def backward_body(lens, ins_from, ins, da, n1g, s2, g_gate, g_up, g_down, r1_down, outs, vals,
              f_gate, f_up, f_q, f_kv, f_out,
              dav, n1v, s2v, do4, delta, acc, kvt, dqt, dkv_s, dkv_r, dqkv, p4, core_r, hop, fin, hop2, fin2,
              d_q, d_kv, d_out,
              ra0, ra1, rb0, rb1, rc, rd0, rd1, re0, re1, rf0, rf1,
              ta0, ta1, tb0, tb1, tc0, tc1, td0, td1, te0, te1, tf0, tf1,
              qa0, qa1, qb0, qb1, qc0, qc1, qd0, qd1, qe0, qe1, qf0, qf1,
              s_gate, s_up, s_q, s_kv, s_down, s_out, ssem, rsem, lsem, isem, osem):
    gains, wq, wk, wv, w_gate, w_up, dh, x_ref, h, cos, sin, wqkv, wout, qp, kv, o, lse = ins
    out, gt, gain_out, q_out, k_out, v_out, wo_out, gate_out, up_out, down_out = vals
    z, c, x, y = (lax.axis_index(a) for a in ALL)
    peers = [to for _, to in tp_peers(c, x)]
    for axis, q in (("y", y), ("z", z)):
        peers += [{axis: lax.rem(q + k, 4)} for k in (1, 2, 3)]
    first = (12, 15, 13, 14, 16, 9, 10)
    order = first + tuple(i for i in range(17) if i not in first)
    loaded = fetch([(ins_from[i], ins[i]) for i in order], isem)
    saved = []

    def give(i):
        cp = pltpu.make_async_copy(vals[i], outs[i], osem.at[i])
        cp.start()
        saved.append(cp)

    entry(peers, (z != x, {"z": x, "x": z}))
    w = Mail(ssem, rsem)
    ag = gather8(w, da, dav)
    pump([ag])
    loads = [pltpu.make_async_copy(a, b, lsem.at[i]) for i, (a, b) in enumerate(
        ((da, dav.at[c, x]), (s2, s2v), (n1g, n1v), (r1_down, rc)))]
    for cp in loads:
        cp.start()
    jobs_down = [
        row_job(w, g_down, rc.at[0], tc0, qc0, s_down, 0, z, y, lsem.at[7], loads[3]),
        row_job(w, g_down, rc.at[1], tc1, qc1, s_down, 1, z, y, lsem.at[8], loads[3]),
    ]
    jobs = [
        col_job(w, g_gate, ra0, ta0, qa0, s_gate, 0, z, y, lsem.at[4]),
        col_job(w, g_gate, ra1, ta1, qa1, s_gate, 1, z, y, lsem.at[5]),
        col_job(w, g_up, rb0, tb0, qb0, s_up, 0, z, y, lsem.at[6]),
        col_job(w, g_up, rb1, tb1, qb1, s_up, 1, z, y, lsem.at[9]),
    ]
    pump(jobs_down)
    pump(jobs)
    pump([ag])
    loads[0].wait()
    pump([ag])
    pump([ag])
    pump([ag])
    pump([ag])
    loads[1].wait()
    loads[3].wait()
    tail2 = ring_tail(w, s2v, hop2, fin2)
    pump([tail2])
    pump([ag])

    for cp in loaded:
        cp.wait()
    ow = wout[...].reshape(256, 2048)
    for g in range(2):
        dv = dott(dav[g].reshape(512, 2048), ow).astype(BF).astype(F32)
        ov = o[g].astype(F32)
        for t in range(2):
            v = dv[:, 128 * t: 128 * t + 128]
            pr = v * ov[:, 128 * t: 128 * t + 128]
            low = lanes(v.shape) < 64
            for b, head in enumerate((pltpu.roll(v, 64, 1), v)):
                rows = pl.ds(128 * (2 * t + b), 128)
                do4[g, :, rows, :] = jnp.where(low, 0.0, head).astype(BF).reshape(4, 128, 128)
                total = jnp.sum(jnp.where(low == (b == 0), pr, 0.0), axis=1, keepdims=True)
                total = jnp.broadcast_to(total, (512, 128)).T
                for j in range(4):
                    delta[g, pl.ds(j, 1), rows] = total[0:1, 128 * j: 128 * j + 128]

    ot = o[...].reshape(1024, 256).T

    @pl.loop(0, 8)
    def _(i):
        cols = pl.ds(pl.multiple_of(256 * i, 256), 256)
        d_out[:, :, :, cols] = dot(ot, dav[:, :, :, cols].reshape(1024, 256)).astype(BF).reshape(4, 4, 16, 256)

    jobs_out = [
        row_job(w, d_out, rd0, td0, qd0, s_out, 0, z, y, lsem.at[10]),
        row_job(w, d_out, rd1, td1, qd1, s_out, 1, z, y, lsem.at[11]),
    ]
    pump(jobs_out)

    g0, g1 = 1 - c, c
    waits = {}
    for no, g in enumerate((g0, g1)):
        kvt[...] = kv[g].reshape(2048, 128).T
        acc[...] = jnp.zeros_like(acc)
        for j in range(4):
            qj, doj = qp[g, j], do4[g, j]
            lse_row, delta_row = lse[g, pl.ds(j, 1), :], delta[g, pl.ds(j, 1), :]
            col = lanes((1, 512))
            place = (4 * j + y) * 128 + lax.rem(col, 128)
            c1, c2 = lens[g, 0], lens[g, 0] + lens[g, 1]
            start = jnp.where(place >= c2, c2, jnp.where(place >= c1, c1, 0))
            dqt[...] = jnp.zeros_like(dqt)

            @pl.loop(0, j + 1)
            def _(b):
                keys = kv[g, b].reshape(512, 128)
                at = 512 * b + lax.broadcasted_iota(jnp.int32, (512, 512), 0)
                ok = (at >= start) & (at <= place)
                pt = jnp.where(ok, jnp.exp(dott(keys, qj) - lse_row), 0.0)
                ds = (pt * (dott(keys, doj) - delta_row)).astype(BF)
                acc[b] += dot(ds, qj) + dot(pt.astype(BF), doj)
                dqt[...] += dot(kvt[:, pl.ds(pl.multiple_of(512 * b, 512), 512)], ds)

            dq = dqt[...].T
            rows = pl.ds(128 * j, 128)
            cs, sn = cos[g, rows, :], sin[g, rows, :]
            for t in range(2):
                v = pair_heads(dq[256 * t: 256 * t + 128], dq[256 * t + 128: 256 * t + 256], True) * (HD ** -0.5)
                dqkv[g, rows, 128 * t: 128 * t + 128] = (v * cs - swap_halves(v) * sn).astype(BF)
            if no == 0 and j == 2:
                pump([tail2])
            if no == 1 and j == 2:
                pump(jobs_out)
        dkv_s[no] = acc[...].astype(BF).reshape(4, 4, 128, 128)
        waits[no] = others(w, y, "y", lambda p, no=no: dkv_s.at[no, :, p], dkv_r.at[no])
        if no == 0:
            pump(jobs_down)
            pump(jobs)
    pump(jobs)
    ends = [hand_out(w, s_gate, f_gate, c, x), hand_out(w, s_up, f_up, c, x)]
    pump(ends)
    pump([tail2])
    loads[2].wait()
    dv = dqkv[:, :, 0:256].reshape(1024, 256)

    @pl.loop(0, 8)
    def _(i):
        cols = pl.ds(pl.multiple_of(256 * i, 256), 256)
        d_q[i // 2, i % 2] = dot(n1v[:, :, :, cols].reshape(1024, 256).T, dv).astype(BF).reshape(4, 4, 16, 256)

    jobs_q = [
        col_job(w, d_q, re0, te0, qe0, s_q, 0, z, y, lsem.at[12]),
        col_job(w, d_q, re1, te1, qe1, s_q, 1, z, y, lsem.at[13]),
    ]
    pump(jobs_q)

    state = {}
    for no, g in enumerate((g0, g1)):
        for a in waits[no]:
            w.got(*a)
        for j in range(4):
            rows = pl.ds(128 * j, 128)
            v = dkv_s[no, j, y].astype(F32)
            for k in range(3):
                v += dkv_r[no, k, j].astype(F32)
            turned = v * cos[g, rows, :] - swap_halves(v) * sin[g, rows, :]
            dqkv[g, rows, 256:384] = jnp.where(lanes(v.shape) < 64, turned, v).astype(BF)

        @pl.loop(0, 8)
        def _(i):
            wt = wqkv[i // 2, i % 2].reshape(256, 384)
            p4[g, :, :, pl.ds(pl.multiple_of(256 * i, 256), 256)] = dott(dqkv[g], wt).astype(BF).reshape(4, 128, 256)

        if no == 0:
            scatter8_core(w, p4, core_r, state)
    rs = scatter8_ring(w, p4, core_r, hop, fin, state)
    pump([rs])
    pump([rs])
    dv = dqkv[:, :, 256:384].reshape(1024, 128)

    @pl.loop(0, 8)
    def _(i):
        cols = pl.ds(pl.multiple_of(256 * i, 256), 256)
        d_kv[i // 2, i % 2] = dot(n1v[:, :, :, cols].reshape(1024, 256).T, dv).astype(BF).reshape(4, 4, 16, 128)

    jobs_kv = [
        col_job(w, d_kv, rf0, tf0, qf0, s_kv, 0, z, y, lsem.at[14]),
        col_job(w, d_kv, rf1, tf1, qf1, s_kv, 1, z, y, lsem.at[15]),
    ]
    pump(jobs_kv)

    @pl.loop(0, 8)
    def _(i):
        rows = pl.ds(pl.multiple_of(i * 16, 16), 16)
        v = h[rows, :] + s2v[x, rows, :].astype(F32) + fin2[0, rows, :].astype(F32) + fin2[1, rows, :].astype(F32)
        out[rows, :] = v.astype(BF)

    give(0)

    pump([rs])
    pump(jobs_out)
    pump(jobs_q)
    pump(jobs_kv)
    more = [transpose_zx(w, s_out, lambda zz: f_out, z, x, lsem.at[17])]
    pump(more)
    pump(jobs_q)
    pump(jobs_kv)
    more += [hand_out(w, s_q, f_q, c, x), hand_out(w, s_kv, f_kv, c, x)]
    pump(more[1:])
    pump(jobs_down)
    down_out[...] = s_down[0:44, :].astype(F32)
    give(9)
    pump(ends)
    gain1, gain2 = gains[0], gains[1]
    total = jnp.zeros((16, 128), F32)
    for f, wt, res in ((f_gate, w_gate, gate_out), (f_up, w_up, up_out)):
        for t in range(44):
            tile = None
            for r, move in collect_moves(t):
                piece = take_lanes(lambda a: f[r, :, 128 * a: 128 * a + 128].astype(F32), [move])
                tile = piece if tile is None else tile + piece
            cols = slice(128 * t, 128 * t + 128)
            total += tile * wt[:, cols].astype(F32)
            res[:, cols] = tile * gain2
    give(7)
    give(8)
    gain_out[1] = jnp.broadcast_to(jnp.sum(total, axis=1, keepdims=True), (16, 128))
    pump([rs])

    @pl.loop(0, 8)
    def _(i):
        rows = pl.ds(pl.multiple_of(i * 16, 16), 16)
        e = p4[c, x, rows, :].astype(F32) + core_r[3, rows, :].astype(F32)
        e = e + fin[0, rows, :].astype(F32) + fin[1, rows, :].astype(F32)
        v = x_ref[rows, :].astype(F32)
        r = lax.rsqrt(jnp.mean(v * v, axis=1, keepdims=True) + EPS)
        gt[rows, :] = dh[rows, :] + r * e - v * (r * r * r * jnp.mean(e * v, axis=1, keepdims=True))

    give(1)
    pump(more)
    wo_out[...] = f_out[...].astype(F32)
    total = jnp.zeros((16, 128), F32)
    for r in range(8):
        for t in range(2):
            cols = slice(256 * r + 128 * t, 256 * r + 128 * t + 128)
            tile = f_q[r, :, 128 * t: 128 * t + 128].astype(F32)
            total += tile * wq[:, cols].astype(F32)
            q_out[:, cols] = tile * gain1
    heads = [f_kv[2 * a].astype(F32) + f_kv[2 * a + 1].astype(F32) for a in range(4)]
    for t in range(2):
        cols = slice(128 * t, 128 * t + 128)
        for res, wt, lower in ((k_out, wk, True), (v_out, wv, False)):
            tile = pair_heads(heads[2 * t], heads[2 * t + 1], lower)
            total += tile * wt[:, cols].astype(F32)
            res[:, cols] = tile * gain1
    gain_out[0] = jnp.broadcast_to(jnp.sum(total, axis=1, keepdims=True), (16, 128))
    for i in (2, 3, 4, 5, 6):
        give(i)
    w.drain()
    for cp in saved:
        cp.wait()


def backward_attention(
        lens, gains, wq, wk, wv, w_gate, w_up, da, dh, x, h, cos, sin, n1g, wqkv, wout, qp, kv, o, lse,
        s2, g_gate, g_up, g_down, r1_down, cid):
    sds = jax.ShapeDtypeStruct
    hb = pl.BlockSpec(memory_space=ANY)
    outs = [sds((128, 2048), BF)] + [sds(a, F32) for a in (
        (128, 2048), (2, 16, 128), (16, 2048), (16, 256), (16, 256), (16, 2048), (16, 5632), (16, 5632), (44, 2048))]
    b = lambda *s: VMEM(s, BF)
    ns = (768, 768, 256, 128)
    r1 = [b(3, 4, 4, 16, 768)] * 4 + [b(2, 3, 4, 48, 1024)] + [b(3, 4, 16, 1024)] * 2
    r1 += [b(3, 4, 4, 16, 256)] * 2 + [b(3, 4, 4, 16, 128)] * 2
    t1 = [b(4, 4, 16, 768)] * 4 + [b(4, 48, 1024)] * 2 + [b(4, 16, 1024)] * 2
    t1 += [b(4, 4, 16, 256)] * 2 + [b(4, 4, 16, 128)] * 2
    r2 = [b(3, 4, 16, 768)] * 4 + [b(3, 48, 1024)] * 2 + [b(3, 16, 1024)] * 2
    r2 += [b(3, 4, 16, 256)] * 2 + [b(3, 4, 16, 128)] * 2
    return pl.pallas_call(
        m3_kernel,
        out_shape=outs,
        in_specs=[pl.BlockSpec(memory_space=pltpu.SMEM)] + [hb] * 24,
        out_specs=[hb] * 10,
        scratch_shapes=[VMEM(a.shape, a.dtype) for a in outs] + [VMEM(a.shape, a.dtype) for a in (
            gains, wq, wk, wv, w_gate, w_up, dh, x, h, cos, sin, wqkv, wout, qp, kv, o, lse)] + [
            b(8, 16, 768), b(8, 16, 768), b(8, 16, 256), b(8, 16, 128), b(16, 2048),
            b(2, 4, 128, 2048), b(2, 4, 128, 2048), b(4, 128, 2048), b(2, 4, 512, 128), VMEM((2, 4, 512), F32),
            VMEM((4, 512, 128), F32), b(128, 2048), VMEM((128, 512), F32), b(2, 4, 4, 128, 128),
            b(2, 3, 4, 128, 128), b(2, 512, 384), b(2, 4, 128, 2048), b(4, 128, 2048), b(2, 64, 2048),
            b(2, 128, 2048), b(2, 64, 2048), b(2, 128, 2048),
            b(4, 2, 4, 4, 16, 256), b(4, 2, 4, 4, 16, 128), b(4, 4, 16, 2048),
        ] + r1 + t1 + r2 + [
            b(2, 4, 16, 768), b(2, 4, 16, 768), b(2, 4, 16, 256), b(2, 4, 16, 128), b(48, 2048), b(16, 2048),
            pltpu.SemaphoreType.DMA((150,)), pltpu.SemaphoreType.DMA((150,)), pltpu.SemaphoreType.DMA((18,)),
            pltpu.SemaphoreType.DMA((17,)), pltpu.SemaphoreType.DMA((10,)),
        ],
        compiler_params=comm_params(cid, 63),
        name="backward_attention",
    )(lens, gains, wq, wk, wv, w_gate, w_up, da, dh, x, h, cos, sin, n1g, wqkv, wout, qp, kv, o, lse, s2, g_gate, g_up, g_down, r1_down)


def copy_kernel(n, *refs):
    ins, outs, held, isem, osem = refs[:n], refs[n:2 * n], refs[2 * n:3 * n], refs[-2], refs[-1]
    loads = fetch(list(zip(ins, held)), isem)
    stores = [pltpu.make_async_copy(held[i], outs[i], osem.at[i]) for i in range(n)]
    for i in range(n):
        loads[i].wait()
        stores[i].start()
    for cp in stores:
        cp.wait()


def copied(arrays):
    hb = pl.BlockSpec(memory_space=ANY)
    return pl.pallas_call(
        functools.partial(copy_kernel, len(arrays)),
        out_shape=[jax.ShapeDtypeStruct(a.shape, a.dtype) for a in arrays],
        in_specs=[hb] * len(arrays),
        out_specs=[hb] * len(arrays),
        scratch_shapes=[VMEM(a.shape, a.dtype) for a in arrays] + [pltpu.SemaphoreType.DMA((len(arrays),))] * 2,
        name="results",
    )(*arrays)


def local(tokens, lengths, attn_gain, w_query, w_key, w_value, w_out, mlp_gain, w_gate, w_up, w_down, cotangent):
    lens = lax.all_gather(lengths, "core", axis=0, tiled=True)
    gains = jnp.broadcast_to(jnp.stack([attn_gain, mlp_gain]).astype(F32)[..., None], (2, 16, 128))
    h, n1g, qp, kv, o, lse, wqkv, wout, cos, sin, dh, da, s2, g_gate, g_up, g_down, r1_down = forward_layer(
        lens, gains, tokens, cotangent, w_query, w_key, w_value, w_out, w_gate, w_up, w_down, 1)
    col = (4, 2, 4, 4, 16, 768)
    output, grad_tokens, gain, g_q, g_k, g_v, g_o, g_gate, g_up, g_down = backward_attention(
        lens, gains, w_query, w_key, w_value, w_gate, w_up, da, dh, tokens, h, cos, sin, n1g, wqkv, wout,
        qp, kv, o, lse, s2, g_gate.reshape(col), g_up.reshape(col), g_down, r1_down, 2)
    output, grad_tokens, g_q, g_k, g_v, g_o, g_gate, g_up, g_down = copied(
        (output, grad_tokens, g_q, g_k, g_v, g_o, g_gate, g_up, g_down))
    return (output, grad_tokens, gain[0, :, 0], g_q, g_k, g_v, g_o, gain[1, :, 0], g_gate, g_up, g_down)


def solution(mesh):
    fine = Mesh(mesh.devices.reshape(4, 2, 4, 4), ALL)
    rows, flat = P(ALL, None), P(ALL)
    in_specs = (rows, P(("z", "core"), None), flat, rows, rows, rows, rows, flat, rows, rows, rows, rows)
    out_specs = (rows, rows, flat, rows, rows, rows, rows, flat, rows, rows, rows)
    return jax.shard_map(local, mesh=fine, in_specs=in_specs, out_specs=out_specs, check_vma=False)
```

```python
import functools
import math

import jax
import jax.numpy as jnp
from jax import lax
from jax.experimental import pallas as pl
from jax.experimental.pallas import tpu as pltpu
from jax.sharding import Mesh
from jax.sharding import PartitionSpec as P

HEADS = 32
KV_HEADS = 4
HD = 64
EPS = 1e-05
THETA = 10000.0
NEG = -1e30
BF = jnp.bfloat16
F32 = jnp.float32
ANY = pl.ANY
VMEM = pltpu.VMEM
TP = ("x", "core")
DP = ("z", "y")
ALL = ("z", "core", "x", "y")


def tdot(a, b):
    return lax.dot_general(a, b, (((0,), (0,)), ((), ())), preferred_element_type=F32)


def dott(a, b):
    return lax.dot_general(a, b, (((1,), (1,)), ((), ())), preferred_element_type=F32)


def dot(a, b):
    return jnp.dot(a, b, preferred_element_type=F32)


class Wire:
    def __init__(self, ssem, rsem):
        self.ssem, self.rsem, self.sent = ssem, rsem, []

    def put(self, src, dst, k, to):
        cp = pltpu.make_async_remote_copy(
            src_ref=src, dst_ref=dst, send_sem=self.ssem.at[k], recv_sem=self.rsem.at[k],
            device_id=to, device_id_type=pl.DeviceIdType.MESH)
        cp.start()
        self.sent.append(cp)
        return cp

    def settle(self, copies):
        for cp in copies:
            cp.wait_send()
        done = {id(cp) for cp in copies}
        self.sent = [cp for cp in self.sent if id(cp) not in done]

    def got(self, dst, k, to):
        pltpu.make_async_remote_copy(
            src_ref=dst, dst_ref=dst, send_sem=self.ssem.at[k], recv_sem=self.rsem.at[k],
            device_id=to, device_id_type=pl.DeviceIdType.MESH).wait_recv()

    def drain(self):
        for cp in self.sent:
            cp.wait_send()


def greet(peers):
    barrier = pltpu.get_barrier_semaphore()
    for to in peers:
        pl.semaphore_signal(barrier, inc=1, device_id=to, device_id_type=pl.DeviceIdType.MESH)
    pl.semaphore_wait(barrier, len(peers))


def cx_ring():
    c, x = lax.axis_index("core"), lax.axis_index("x")
    right, left, opp = lax.rem(x + 1, 4), lax.rem(x + 3, 4), lax.rem(x + 2, 4)
    return c, x, right, left, opp, {"x": right}, {"x": left}, {"core": 1 - c}


def comm_params(cid, mb=None):
    kw = {} if mb is None else {"vmem_limit_bytes": mb << 20}
    return pltpu.CompilerParams(collective_id=cid, has_side_effects=True, **kw)


class Mail(Wire):
    def __init__(self, ssem, rsem):
        super().__init__(ssem, rsem)
        self.used = 0

    def new(self):
        self.used += 1
        return self.used - 1


def around(q):
    return lax.rem(q + 1, 4), lax.rem(q + 3, 4), lax.rem(q + 2, 4)


def ring(w, s, axis, q):
    right, left, opp = around(q)
    to_r, to_l = {axis: right}, {axis: left}
    k = [w.new() for _ in range(4)]
    w.put(s(q, None), s(q, None), k[0], to_r)
    w.put(s(q, None), s(q, None), k[1], to_l)
    yield
    w.got(s(left, None), k[0], to_l)
    w.put(s(left, 0), s(left, 0), k[2], to_r)
    w.got(s(right, None), k[1], to_r)
    w.put(s(right, 1), s(right, 1), k[3], to_l)
    yield
    w.got(s(opp, 0), k[2], to_l)
    w.got(s(opp, 1), k[3], to_r)


def col_flows(w, W, z, y):
    cut = lambda h: slice(None) if h is None else pl.ds(2 * h, 2)

    def first():
        yield from ring(w, lambda p, h: W.at[z, 0, cut(h), p], "y", y)
        yield from ring(w, lambda p, h: W.at[p, 0, cut(h)], "z", z)

    def second():
        yield from ring(w, lambda p, h: W.at[p, 1, cut(h), y], "z", z)
        yield from ring(w, lambda p, h: W.at[:, 1, cut(h), p], "y", y)

    return [first(), second()]


def row_flows(w, W, z, y):
    n = W.shape[-1] // 4
    cut = lambda b, h: pl.ds(2 * n * b, 2 * n) if h is None else pl.ds(2 * n * b + n * h, n)

    def first():
        yield from ring(w, lambda p, h: W.at[z, p, :, cut(0, h)], "y", y)
        yield from ring(w, lambda p, h: W.at[p, :, :, cut(0, h)], "z", z)

    def second():
        yield from ring(w, lambda p, h: W.at[p, y, :, cut(1, h)], "z", z)
        yield from ring(w, lambda p, h: W.at[:, p, :, cut(1, h)], "y", y)

    return [first(), second()]


def straight(w, stages):
    for s, axis, q in stages:
        ks = {}
        for k in (1, 3, 2):
            ks[k] = w.new()
            w.put(s(q), s(q), ks[k], {axis: lax.rem(q + k, 4)})
        yield
        for k in (1, 3, 2):
            frm = lax.rem(q + 4 - k, 4)
            w.got(s(frm), ks[k], {axis: frm})


def col_straight(w, W, z, y):
    return [straight(w, [(lambda p: W.at[z, 0, :, p], "y", y), (lambda p: W.at[p, 0], "z", z)]),
            straight(w, [(lambda p: W.at[p, 1, :, y], "z", z), (lambda p: W.at[:, 1, :, p], "y", y)])]


def row_straight(w, W, z, y):
    n = W.shape[-1] // 2
    a, b = pl.ds(0, n), pl.ds(n, n)
    return [straight(w, [(lambda p: W.at[z, p, :, a], "y", y), (lambda p: W.at[p, :, :, a], "z", z)]),
            straight(w, [(lambda p: W.at[p, y, :, b], "z", z), (lambda p: W.at[:, p, :, b], "y", y)])]


def pump(flows):
    for f in flows:
        next(f, None)


def gather8(w, src, dst):
    c, x, right, left, opp, to_r, to_l, to_c = cx_ring()
    rows = dst.shape[2]
    lo, hi = pl.ds(0, rows // 2), pl.ds(rows // 2, rows // 2)
    k = [w.new() for _ in range(10)]
    out = []
    out += [w.put(src.at[lo], dst.at[c, x, lo], k[0], to_r)]
    out += [w.put(src.at[hi], dst.at[c, x, hi], k[1], to_l)]
    out += [w.put(src.at[hi], dst.at[c, x, hi], k[2], to_r)]
    out += [w.put(src.at[lo], dst.at[c, x, lo], k[3], to_l)]
    out += [w.put(src, dst.at[c, x], k[4], to_c)]
    yield
    w.got(dst.at[c, left, lo], k[0], to_l)
    out += [w.put(dst.at[c, left, lo], dst.at[c, left, lo], k[5], to_r)]
    w.got(dst.at[c, right, hi], k[1], to_r)
    out += [w.put(dst.at[c, right, hi], dst.at[c, right, hi], k[6], to_l)]
    yield
    w.got(dst.at[1 - c, x], k[4], to_c)
    yield
    w.got(dst.at[c, left, hi], k[2], to_l)
    out += [w.put(dst.at[c, left], dst.at[c, left], k[7], to_c)]
    w.got(dst.at[c, right, lo], k[3], to_r)
    out += [w.put(dst.at[c, right], dst.at[c, right], k[8], to_c)]
    yield
    w.got(dst.at[1 - c, left], k[7], to_c)
    w.got(dst.at[1 - c, right], k[8], to_c)
    yield
    w.got(dst.at[c, opp, lo], k[5], to_l)
    w.got(dst.at[c, opp, hi], k[6], to_r)
    out += [w.put(dst.at[c, opp], dst.at[c, opp], k[9], to_c)]
    yield
    w.got(dst.at[1 - c, opp], k[9], to_c)
    w.settle(out)


def add_to(dst, other, r0, rows, step=16):
    @pl.loop(0, rows // step)
    def _(i):
        a = pl.ds(pl.multiple_of(r0 + i * step, step), step)
        b = pl.ds(pl.multiple_of(i * step, step), step)
        dst[a, :] = (dst[a, :].astype(F32) + other[b, :].astype(F32)).astype(dst.dtype)


def scatter8_core(w, p, core_r, state, only=None):
    c, x, right, left, opp, to_r, to_l, to_c = cx_ring()
    if not state:
        state["k"], state["out"] = [w.new() for _ in range(4)], []
    for i, xx in enumerate((opp, right, left, x)):
        if only is None or only == i:
            state["out"].append(w.put(p.at[1 - c, xx], core_r.at[i], state["k"][i], to_c))


def scatter8_ring(w, p, core_r, hop, fin, state):
    c, x, right, left, opp, to_r, to_l, to_c = cx_ring()
    rows = p.shape[2]
    half = rows // 2
    lo, hi = pl.ds(0, half), pl.ds(half, half)
    kc, out = state["k"], state["out"]
    k = [w.new() for _ in range(6)]
    w.got(core_r.at[0], kc[0], to_c)
    add_to(p.at[c, opp], core_r.at[0], 0, rows)
    out += [w.put(p.at[c, opp, lo], hop.at[0], k[0], to_r)]
    out += [w.put(p.at[c, opp, hi], hop.at[1], k[1], to_l)]
    yield
    w.got(core_r.at[1], kc[1], to_c)
    add_to(p.at[c, right], core_r.at[1], 0, rows)
    out += [w.put(p.at[c, right, hi], fin.at[0, hi], k[2], to_r)]
    w.got(core_r.at[2], kc[2], to_c)
    add_to(p.at[c, left], core_r.at[2], 0, rows)
    out += [w.put(p.at[c, left, lo], fin.at[1, lo], k[3], to_l)]
    yield
    w.got(hop.at[0], k[0], to_l)
    add_to(p.at[c, right], hop.at[0], 0, half)
    out += [w.put(p.at[c, right, lo], fin.at[0, lo], k[4], to_r)]
    w.got(hop.at[1], k[1], to_r)
    add_to(p.at[c, left], hop.at[1], half, half)
    out += [w.put(p.at[c, left, hi], fin.at[1, hi], k[5], to_l)]
    yield
    w.got(core_r.at[3], kc[3], to_c)
    w.got(fin.at[0, hi], k[2], to_l)
    w.got(fin.at[1, lo], k[3], to_r)
    w.got(fin.at[0, lo], k[4], to_l)
    w.got(fin.at[1, hi], k[5], to_r)
    w.settle(out)


def lanes(shape):
    return lax.broadcasted_iota(jnp.int32, shape, len(shape) - 1)


def take_lanes(load, moves):
    out = None
    for src, lo, hi in moves:
        a, shift = (src - lo) // 128, (src - lo) % 128
        split = 128 - shift
        turned = lambda t: pltpu.roll(load(t), (128 - shift) % 128, 1) if shift else load(t)
        if hi <= split:
            piece = turned(a)
        elif lo >= split:
            piece = turned(a + 1)
        else:
            piece = jnp.where(lanes((16, 128)) < split, turned(a), turned(a + 1))
        at = lanes(piece.shape)
        out = jnp.where((at >= lo) & (at < hi), piece, jnp.zeros_like(piece) if out is None else out)
    return out


def fetch(pairs, sems):
    copies = [pltpu.make_async_copy(src, dst, sems.at[i]) for i, (src, dst) in enumerate(pairs)]
    for cp in copies:
        cp.start()
    return copies


def unit_place(z, c, x, y):
    return ((z * 2 + c) * 4 + x) * 4 + y


def spread_moves(r, t):
    out = []
    for s in range(16):
        d0 = 48 * s
        lo, hi = max(d0, 128 * t), min(d0 + 44, 128 * t + 128)
        if lo < hi:
            unit = unit_place(s // 4, r % 2, r // 2, s % 4)
            out.append((44 * unit + lo - d0, lo - 128 * t, hi - 128 * t))
    return out


def collect_moves(t):
    out = []
    for unit in range(128):
        d0 = 44 * unit
        lo, hi = max(d0, 128 * t), min(d0 + 44, 128 * t + 128)
        if lo < hi:
            z, c, x, y = unit // 32, unit // 16 % 2, unit // 4 % 4, unit % 4
            out.append((2 * x + c, (48 * (4 * z + y) + lo - d0, lo - 128 * t, hi - 128 * t)))
    return out


def swap_halves(u):
    first = lax.rem(lanes(u.shape), 64) < 32
    return jnp.where(first, pltpu.roll(u, 96, u.ndim - 1), pltpu.roll(u, 32, u.ndim - 1))


def entry(peers, extra=None):
    barrier = pltpu.get_barrier_semaphore()
    for to in peers:
        pl.semaphore_signal(barrier, inc=1, device_id=to, device_id_type=pl.DeviceIdType.MESH)
    if extra is None:
        pl.semaphore_wait(barrier, len(peers))
        return
    more, to = extra

    @pl.when(more)
    def _():
        pl.semaphore_signal(barrier, inc=1, device_id=to, device_id_type=pl.DeviceIdType.MESH)
        pl.semaphore_wait(barrier, len(peers) + 1)

    @pl.when(jnp.logical_not(more))
    def _():
        pl.semaphore_wait(barrier, len(peers))


def tp_peers(c, x):
    r = 2 * x + c
    out = []
    for k in range(1, 8):
        rr = lax.rem(r + k, 8)
        out.append((rr, {"x": rr // 2, "core": lax.rem(rr, 2)}))
    return out


def spread(w, src, W, z, c, x, y, local_sem):
    ks = [w.new() for _ in range(7)]
    for k, (rr, to) in zip(ks, tp_peers(c, x)):
        w.put(src.at[rr], W.at[z, c, x, y], k, to)
    own = pltpu.make_async_copy(src.at[2 * x + c], W.at[z, c, x, y], local_sem)
    own.start()
    yield
    r = 2 * x + c
    for i, k in enumerate(ks):
        rr = lax.rem(r + 7 - i, 8)
        w.got(W.at[z, lax.rem(rr, 2), rr // 2, y], k, {"x": rr // 2, "core": lax.rem(rr, 2)})
    own.wait()


def transpose_zx(w, src, dst_of, z, x, local_sem):
    k = w.new()
    to = {"z": x, "x": z}

    def far():
        return pltpu.make_async_remote_copy(
            src_ref=src, dst_ref=dst_of(x), send_sem=w.ssem.at[k], recv_sem=w.rsem.at[k],
            device_id=to, device_id_type=pl.DeviceIdType.MESH)

    def near():
        return pltpu.make_async_copy(src, dst_of(x), local_sem)

    @pl.when(z != x)
    def _():
        far().start()

    @pl.when(z == x)
    def _():
        near().start()

    yield

    @pl.when(z != x)
    def _():
        far().wait_send()
        w.got(dst_of(z), k, to)

    @pl.when(z == x)
    def _():
        near().wait()


def attend(q, keys, j, y, c1, c2):
    m, n = q.shape[0], keys.shape[0]
    s = dott(q, keys)
    row = lax.broadcasted_iota(jnp.int32, (m, 1), 0)
    place = (4 * j + y) * 128 + lax.rem(row, 128)
    start = jnp.where(place >= c2, c2, jnp.where(place >= c1, c1, 0))
    at = lax.broadcasted_iota(jnp.int32, (m, n), 1)
    s = jnp.where((at >= start) & (at <= place), s, NEG)
    top = jnp.max(s, axis=1, keepdims=True)
    e = jnp.exp(s - top)
    total = jnp.sum(e, axis=1, keepdims=True)
    return dot(e.astype(BF), keys) / total, top + jnp.log(total)


def pair_heads(first, second, lower):
    low = lanes(first.shape) < 64
    if lower:
        return jnp.where(low, first, pltpu.roll(second, 64, 1))
    return jnp.where(low, pltpu.roll(first, 64, 1), second)


def forward_kernel(lens, gains_in, x_in, n1_in, cot_in, wq_in, wk_in, wv_in, out_s, gate_in, up_in, down_in,
                   h_out, n1_out, qp_out, kv_out, o_out, lse_out, wqkv_out, wout_out, cos_out, sin_out,
                   dh_out, da_out, s2, g_gate, g_up, g_down, r1_down,
                   cos, sin, h, qp, kv, o, lse, wqkv, wout, n1, cv, wg, wu, wd, p, core_r, hop, fin,
                   dact, a_all, dg_all, du_all, core2, d_down, qkv_s, gate_s, up_s,
                   gains, x_ref, cot, wq, wk, wv, w_gate, w_up, w_down, ssem, rsem, lsem, osem, isem):
    z, c, x, y = (lax.axis_index(a) for a in ALL)
    peers = [to for _, to in tp_peers(c, x)]
    for axis, q in (("y", y), ("z", z)):
        peers += [{axis: lax.rem(q + k, 4)} for k in (1, 2, 3)]
    w = Mail(ssem, rsem)
    loads = fetch(((gains_in, gains), (wq_in, wq), (wk_in, wk), (wv_in, wv), (n1_in, n1.at[c, x]), (down_in, w_down),
                   (gate_in, w_gate), (up_in, w_up), (cot_in, cot), (x_in, x_ref)), isem)
    saved = []

    def save(src, dst):
        cp = pltpu.make_async_copy(src, dst, osem.at[len(saved)])
        cp.start()
        saved.append(cp)
        return cp

    for cp in loads[:4]:
        cp.wait()
    gain1, gain2 = gains[0], gains[1]
    for r in range(8):
        for t in range(2):
            at = 256 * r + 128 * t
            qkv_s[r, :, 128 * t: 128 * t + 128] = (wq[:, at: at + 128].astype(F32) * gain1).astype(BF)
        t, odd = r // 4, r // 2 % 2
        kt, vt = wk[:, 128 * t: 128 * t + 128].astype(F32), wv[:, 128 * t: 128 * t + 128].astype(F32)
        kt, vt = (pltpu.roll(kt, 64, 1), vt) if odd else (kt, pltpu.roll(vt, 64, 1))
        qkv_s[r, :, 256:384] = (jnp.where(lanes(kt.shape) < 64, kt, vt) * gain1).astype(BF)
    entry(peers, (z != x, {"z": x, "x": z}))

    sp_qkv = spread(w, qkv_s, wqkv, z, c, x, y, lsem.at[0])
    pump([sp_qkv])
    loads[4].wait()
    ag_n1 = gather8(w, n1.at[c, x], n1)
    pump([ag_n1])
    for cp in loads[5:]:
        cp.wait()
    wd[z, y] = jnp.concatenate([w_down[...], jnp.zeros((4, 2048), BF)], axis=0)
    pump([sp_qkv])
    fl_qkv = col_straight(w, wqkv, z, y)
    pump(fl_qkv)
    for src, dst in ((w_gate, gate_s), (w_up, up_s)):
        for r in range(8):
            for t in range(6):
                load = lambda a: src[:, 128 * a: 128 * a + 128].astype(F32)
                dst[r, :, 128 * t: 128 * t + 128] = (take_lanes(load, spread_moves(r, t)) * gain2).astype(BF)
    pump([ag_n1])
    pump([ag_n1])
    pump(fl_qkv)
    spreads = [spread(w, gate_s, wg, z, c, x, y, lsem.at[2]), spread(w, up_s, wu, z, c, x, y, lsem.at[3])]
    pump(spreads)
    tr_out = transpose_zx(w, out_s, lambda zz: wout.at[zz, y], z, x, lsem.at[1])
    pump([tr_out])
    fl_down = row_flows(w, wd, z, y)
    pump(fl_down)

    for g in range(2):
        lane = lanes((128, 128))
        freq = jnp.exp(lax.rem(lane, 32).astype(F32) * (-2.0 * math.log(THETA) / HD))
        c1, c2 = lens[g, 0], lens[g, 0] + lens[g, 1]

        @pl.loop(0, 4)
        def _(j):
            place = (4 * j + y) * 128 + lax.broadcasted_iota(jnp.int32, (128, 128), 0)
            start = jnp.where(place >= c2, c2, jnp.where(place >= c1, c1, 0))
            angle = (place - start).astype(F32) * freq
            rows = pl.ds(pl.multiple_of(128 * j, 128), 128)
            cos[g, rows, :] = jnp.cos(angle)
            turned = jnp.sin(angle)
            sin[g, rows, :] = jnp.where(lax.rem(lane, 64) < 32, -turned, turned)

    pump([ag_n1])
    pump([tr_out])
    fl_out = row_straight(w, wout, z, y)
    pump(fl_out)
    pump(spreads)
    fl_gu = col_flows(w, wg, z, y) + col_flows(w, wu, z, y)
    pump(fl_gu)
    fl_mlp = fl_down + fl_gu
    pump([ag_n1])
    pump([ag_n1])
    pump(fl_qkv)
    pump([ag_n1])
    weights = wqkv[...].reshape(2048, 384)

    def project(g, keys_too):
        u = dot(n1[g].reshape(512, 2048), weights)
        cs, sn = cos[g], sin[g]
        if keys_too:
            v = u[:, 256:384]
            turned = jnp.where(lanes(v.shape) < 64, v * cs + swap_halves(v) * sn, v)
            kv[g, :, y] = turned.astype(BF).reshape(4, 128, 128)
        for t in range(2):
            v = u[:, 128 * t: 128 * t + 128]
            v = (v * cs + swap_halves(v) * sn) * (HD ** -0.5)
            low = lanes(v.shape) < 64
            for b, head in enumerate((v, pltpu.roll(v, 64, 1))):
                rows = pl.ds(128 * (2 * t + b), 128)
                qp[g, :, rows, :] = jnp.where(low, head, 0.0).astype(BF).reshape(4, 128, 128)

    g0, g1 = 1 - c, c
    to_c = {"core": 1 - c}
    pump(fl_mlp)
    project(g0, True)
    fl_kv = [straight(w, [(lambda pp: kv.at[g0, :, pp], "y", y)])]
    pump(fl_kv)
    pump(fl_out)
    ag_cot = gather8(w, cot, cv)
    pump([ag_cot])
    project(g1, False)
    keep_n1 = save(n1, n1_out)
    save(wqkv, wqkv_out)
    save(cos, cos_out)
    save(sin, sin_out)
    keep_cot = save(cot, cv.at[c, x])
    pump(fl_mlp[0::2])
    pump(fl_kv)
    k_kv = w.new()
    w.put(kv.at[g0], kv.at[g0], k_kv, to_c)
    pump(fl_mlp[1::2])

    state = {}
    for turn_no, g in enumerate((g0, g1)):
        if turn_no == 1:
            w.got(kv.at[g], k_kv, to_c)
            save(kv, kv_out)
            save(qp, qp_out)
            save(wout, wout_out)
        for j in range(4):
            n = 512 * (j + 1)
            keys = kv[g, 0:j + 1].reshape(n, 128)
            for t in range(2):
                part = qp[g, j, 256 * t: 256 * t + 256]
                res, total = attend(part, keys, j, y, lens[g, 0], lens[g, 0] + lens[g, 1])
                both = pair_heads(res[:128], res[128:], False)
                o[g, pl.ds(128 * j, 128), 128 * t: 128 * t + 128] = both.astype(BF)
                lse[g, pl.ds(j, 1), 256 * t: 256 * t + 256] = jnp.broadcast_to(total, (256, 128)).T[0:1, :]
            if j == 2:
                pump([ag_cot])
        pump(fl_out)
        out_w = wout[...].reshape(256, 2048)

        @pl.loop(0, 4)
        def _(i):
            p[g, i] = dot(o[g, pl.ds(pl.multiple_of(128 * i, 128), 128), :], out_w).astype(BF)

        if turn_no == 0:
            keep_n1.wait()
            scatter8_core(w, p, core_r, state)
    rs = scatter8_ring(w, p, core_r, hop, fin, state)
    pump([rs])
    pump([rs])
    save(o, o_out)
    save(lse, lse_out)
    pump([ag_cot])
    pump([ag_cot])
    pump([ag_cot])
    pump([rs])
    pump([ag_cot])
    pump(fl_mlp[0::2])
    pump(fl_mlp[1::2])
    pump([rs])

    @pl.loop(0, 8)
    def _(i):
        rows = pl.ds(pl.multiple_of(i * 16, 16), 16)
        v = x_ref[rows, :].astype(F32) + p[c, x, rows, :].astype(F32) + core_r[3, rows, :].astype(F32)
        v = v + fin[0, rows, :].astype(F32) + fin[1, rows, :].astype(F32)
        h[rows, :] = v
        n1[c, x, rows, :] = (v * lax.rsqrt(jnp.mean(v * v, axis=1, keepdims=True) + EPS)).astype(BF)

    keep_h = save(h, h_out)
    n2v = n1
    ag = gather8(w, n2v.at[c, x], n2v)
    pump([ag])
    pump(fl_down)
    keep_cot.wait()
    down = wd[...].reshape(768, 2048)

    @pl.loop(0, 2)
    def _(g):
        for t in range(2):
            v = dott(cv[g, 2 * t: 2 * t + 2].reshape(256, 2048), down)
            dact[g, 2 * t: 2 * t + 2] = v.astype(BF).reshape(2, 128, 768)

    pump([ag])
    pump([ag])
    pump(fl_gu)
    cc, xx, right, left, opp, to_r, to_l, to_c = cx_ring()
    st3, st2 = {}, {}

    def block(b, number):
        @pl.loop(0, 3)
        def _(i):
            cols = pl.ds(pl.multiple_of(256 * i, 256), 256)
            nv = n2v[:, b].reshape(256, 2048)
            gp = dot(nv, wg[:, :, :, :, :, cols].reshape(2048, 256))
            u = dot(nv, wu[:, :, :, :, :, cols].reshape(2048, 256))
            sig = jax.nn.sigmoid(gp)
            act = gp * sig
            d = dact[:, b, :, cols].reshape(256, 256).astype(F32)
            a_all[:, b, :, cols] = (act * u).astype(BF).reshape(2, 128, 256)
            dg_all[:, b, :, cols] = (d * u * sig * (1.0 + gp * (1.0 - sig))).astype(BF).reshape(2, 128, 256)
            du_all[:, b, :, cols] = (d * act).astype(BF).reshape(2, 128, 256)

        @pl.loop(0, 8)
        def _(i):
            part = dott(dg_all[:, b].reshape(256, 768), wg[i // 2, i % 2].reshape(256, 768))
            part += dott(du_all[:, b].reshape(256, 768), wu[i // 2, i % 2].reshape(256, 768))
            p[:, b, :, pl.ds(pl.multiple_of(256 * i, 256), 256)] = part.astype(BF).reshape(2, 128, 256)

        scatter8_core(w, p, core_r, st3, number)

    block(x, 3)
    pump([ag])
    pump([ag])
    block(left, 2)
    pump([ag])
    pump([ag])
    block(opp, 0)
    rs3 = scatter8_ring(w, p, core_r, hop, fin, st3)
    pump([rs3])
    block(right, 1)
    pump([rs3])
    at = a_all[...].reshape(1024, 768).T

    @pl.loop(0, 8)
    def _(i):
        cols = pl.ds(pl.multiple_of(256 * i, 256), 256)
        d_down[:, :, :, cols] = dot(at, cv[:, :, :, cols].reshape(1024, 256)).astype(BF).reshape(4, 4, 48, 256)

    first, second = pl.ds(0, 1024), pl.ds(1024, 1024)
    landed = others(w, y, "y", lambda pp: d_down.at[:, pp, :, first], r1_down.at[0])
    landed += others(w, z, "z", lambda pp: d_down.at[pp, :, :, second], r1_down.at[1])
    save(d_down, g_down)

    p2 = cv

    def out_part(g):
        @pl.loop(0, 8)
        def _(i):
            cols = pl.ds(pl.multiple_of(256 * i, 256), 256)
            part = dot(a_all[g].reshape(512, 768), wd[:, :, :, cols].reshape(768, 256))
            p2[g, :, :, cols] = part.astype(BF).reshape(4, 128, 256)

    pump([rs3])
    out_part(g0)
    scatter8_core(w, p2, core2, st2)
    out_part(g1)

    dg, du = dg_all[...].reshape(1024, 768), du_all[...].reshape(1024, 768)

    def stage(i, slot, k):
        return pltpu.make_async_copy(
            dact.at[slot, pl.ds(2 * k, 2)], (g_gate, g_up)[k].at[i], lsem.at[4 + 2 * slot + k])

    @pl.loop(0, 4)
    def _(i):
        for slot in range(2):
            cols = pl.ds(pl.multiple_of(512 * i + 256 * slot, 256), 256)
            t = n2v[:, :, :, cols].reshape(1024, 256).T

            @pl.when(i > 0)
            def _():
                stage(2 * i + slot - 2, slot, 0).wait()
                stage(2 * i + slot - 2, slot, 1).wait()

            dact[slot, 0:2] = dot(t, dg).astype(BF).reshape(2, 128, 768)
            dact[slot, 2:4] = dot(t, du).astype(BF).reshape(2, 128, 768)
            stage(2 * i + slot, slot, 0).start()
            stage(2 * i + slot, slot, 1).start()

    for i, b in enumerate((opp, right, left, x)):
        w.got(core2.at[i], st2["k"][i], to_c)
        add_to(p2.at[c, b], core2.at[i], 0, 128)
    save(p2.at[c], s2)
    pump([rs3])
    keep_h.wait()

    @pl.loop(0, 8)
    def _(i):
        rows = pl.ds(pl.multiple_of(i * 16, 16), 16)
        e = p[c, x, rows, :].astype(F32) + core_r[3, rows, :].astype(F32)
        e = e + fin[0, rows, :].astype(F32) + fin[1, rows, :].astype(F32)
        v = h[rows, :]
        r = lax.rsqrt(jnp.mean(v * v, axis=1, keepdims=True) + EPS)
        out = cot[rows, :].astype(F32) + r * e - v * (r * r * r * jnp.mean(e * v, axis=1, keepdims=True))
        h[rows, :] = out
        n1[c, x, rows, :] = out.astype(BF)

    save(h, dh_out)
    save(n1.at[c, x], da_out)
    w.drain()
    for slot in range(2):
        stage(6 + slot, slot, 0).wait()
        stage(6 + slot, slot, 1).wait()
    for a in landed:
        w.got(*a)
    for cp in saved:
        if all(cp is not a for a in (keep_n1, keep_h, keep_cot)):
            cp.wait()


def forward_layer(lens, gains, tokens, n1, cot, wq, wk, wv, out_s, w_gate, w_up, w_down, cid):
    sds = jax.ShapeDtypeStruct
    hb = pl.BlockSpec(memory_space=ANY)
    col, big = (4, 2, 4, 4, 16, 768), (2, 4, 128, 2048)
    row, half, table = (128, 2048), (2, 4, 128, 768), ((2, 512, 128), F32)
    mid = [((2, 4, 512, 128), BF), ((2, 4, 4, 128, 128), BF), ((2, 512, 256), BF), ((2, 4, 512), F32),
           ((4, 2, 4, 4, 16, 384), BF), ((4, 4, 16, 2048), BF)]
    outs = [(row, F32), (big, BF)] + mid + [table, table] + [
        (row, F32), (row, BF), ((4, 128, 2048), BF), ((8, 2, 128, 768), BF), ((8, 2, 128, 768), BF),
        ((4, 4, 48, 2048), BF), ((2, 3, 4, 48, 1024), BF)]
    scratch = [table, table, (row, F32)] + mid + [
        (big, BF), (big, BF), (col, BF), (col, BF), ((4, 4, 48, 2048), BF),
        (big, BF), ((4, 128, 2048), BF), ((2, 64, 2048), BF), ((2, 128, 2048), BF),
        (half, BF), (half, BF), (half, BF), (half, BF), ((4, 128, 2048), BF), ((4, 4, 48, 2048), BF),
        ((8, 16, 384), BF), ((8, 16, 768), BF), ((8, 16, 768), BF),
        ((2, 16, 128), F32), (row, BF), (row, BF), ((16, 2048), BF), ((16, 256), BF), ((16, 256), BF),
        ((16, 5632), BF), ((16, 5632), BF), ((44, 2048), BF)]
    return pl.pallas_call(
        forward_kernel,
        out_shape=[sds(*a) for a in outs],
        in_specs=[pl.BlockSpec(memory_space=pltpu.SMEM)] + [hb] * 11,
        out_specs=[hb] * len(outs),
        scratch_shapes=[VMEM(*a) for a in scratch] + [
            pltpu.SemaphoreType.DMA((170,)), pltpu.SemaphoreType.DMA((170,)), pltpu.SemaphoreType.DMA((8,)),
            pltpu.SemaphoreType.DMA((18,)), pltpu.SemaphoreType.DMA((10,)),
        ],
        compiler_params=comm_params(cid, 63),
        name="forward_layer",
    )(lens, gains, tokens, n1, cot, wq, wk, wv, out_s, w_gate, w_up, w_down)


def ring_tail(w, s, hop, fin):
    c, x, right, left, opp, to_r, to_l, to_c = cx_ring()
    half = s.shape[1] // 2
    lo, hi = pl.ds(0, half), pl.ds(half, half)
    k = [w.new() for _ in range(6)]
    w.put(s.at[opp, lo], hop.at[0], k[0], to_r)
    w.put(s.at[opp, hi], hop.at[1], k[1], to_l)
    w.put(s.at[right, hi], fin.at[0, hi], k[2], to_r)
    w.put(s.at[left, lo], fin.at[1, lo], k[3], to_l)
    yield
    w.got(hop.at[0], k[0], to_l)
    add_to(s.at[right], hop.at[0], 0, half)
    w.put(s.at[right, lo], fin.at[0, lo], k[4], to_r)
    w.got(hop.at[1], k[1], to_r)
    add_to(s.at[left], hop.at[1], half, half)
    w.put(s.at[left, hi], fin.at[1, hi], k[5], to_l)
    yield
    w.got(fin.at[0, hi], k[2], to_l)
    w.got(fin.at[1, lo], k[3], to_r)
    w.got(fin.at[0, lo], k[4], to_l)
    w.got(fin.at[1, hi], k[5], to_r)


def others(w, q, axis, piece, recv):
    ks = {}
    for k in (1, 3, 2):
        to = lax.rem(q + k, 4)
        ks[k] = w.new()
        w.put(piece(to), recv.at[k - 1], ks[k], {axis: to})
    return [(recv.at[k - 1], ks[k], {axis: lax.rem(q + 4 - k, 4)}) for k in (1, 3, 2)]


def sum_four(dst, own, recv, lead):
    total = math.prod(lead)

    @pl.loop(0, total)
    def _(i):
        at = (i,) if len(lead) == 1 else (i // lead[1], lax.rem(i, lead[1]))
        acc = own[at].astype(F32)
        for k in range(3):
            acc += recv[(k,) + at].astype(F32)
        dst[at] = acc.astype(dst.dtype)


def col_job(w, src, r1, t, r2, s, e, z, y, lsem):
    if e == 0:
        own, piece1, ax1, q1 = src.at[:, 0, :, y], lambda p: src.at[:, 0, :, p], "y", y
        piece2, ax2, q2 = lambda p: t.at[p], "z", z
    else:
        own, piece1, ax1, q1 = src.at[z, 1], lambda p: src.at[p, 1], "z", z
        piece2, ax2, q2 = lambda p: t.at[:, p], "y", y
    first = pltpu.make_async_copy(own, t, lsem)
    first.start()
    waits = others(w, q1, ax1, piece1, r1)
    yield
    first.wait()
    for a in waits:
        w.got(*a)
    sum_four(t, t, r1, (4, 4))
    waits = others(w, q2, ax2, piece2, r2)
    yield
    for a in waits:
        w.got(*a)
    sum_four(s.at[e], piece2(q2), r2, (4,))


def row_job(w, src, r1, t, r2, s, e, z, y, lsem, here=None):
    n = s.shape[-1] // 2
    rows = s.shape[0]
    cols = pl.ds(e * n, n)
    if len(src.shape) == 5:
        at = lambda *q: src.at[(e,) + q]
    else:
        at = lambda *q: src.at[q + (slice(None), cols)]
    if e == 0:
        piece1, ax1, q1, ax2, q2 = lambda p: at(slice(None), p), "y", y, "z", z
    else:
        piece1, ax1, q1, ax2, q2 = lambda p: at(p, slice(None)), "z", z, "y", y
    own = piece1(q1)
    first = pltpu.make_async_copy(own, t, lsem)
    first.start()
    waits = others(w, q1, ax1, piece1, r1) if here is None else []
    yield
    first.wait()
    for a in waits:
        w.got(*a)
    sum_four(t, t, r1, (4,))
    waits = others(w, q2, ax2, lambda p: t.at[p], r2)
    yield
    for a in waits:
        w.got(*a)

    @pl.loop(0, rows // 16)
    def _(i):
        at = pl.ds(pl.multiple_of(i * 16, 16), 16)
        acc = t[q2, at].astype(F32)
        for k in range(3):
            acc += r2[k, at].astype(F32)
        s[at, cols] = acc.astype(BF)


def hand_out(w, s, f, c, x):
    r = 2 * x + c
    ks = [w.new() for _ in range(7)]
    for k, (rr, to) in zip(ks, tp_peers(c, x)):
        w.put(s.at[lax.rem(rr, 2), rr // 2], f.at[r], k, to)
    f[r] = s[c, x]
    yield
    for i, k in enumerate(ks):
        rr = lax.rem(r + 7 - i, 8)
        w.got(f.at[rr], k, {"x": rr // 2, "core": lax.rem(rr, 2)})


def m3_kernel(lens, gains_in, wq_in, wk_in, wv_in, gate_in, up_in, da, dh_in, x_in, h_in, cos_in, sin_in, n1g, wqkv_in,
              wout_in, qp_in, kv_in, o_in, lse_in, s2, g_gate, g_up, g_down, r1_down,
              *rest):
    outs, rest = rest[:10], rest[10:]
    vals, rest = rest[:10], rest[10:]
    ins, rest = rest[:17], rest[17:]
    backward_body(lens, (gains_in, wq_in, wk_in, wv_in, gate_in, up_in, dh_in, x_in, h_in, cos_in, sin_in, wqkv_in,
                         wout_in, qp_in, kv_in, o_in, lse_in), ins, da, n1g, s2, g_gate, g_up, g_down, r1_down,
                  outs, vals, *rest)


def backward_body(lens, ins_from, ins, da, n1g, s2, g_gate, g_up, g_down, r1_down, outs, vals,
              f_gate, f_up, f_q, f_kv, f_out,
              dav, n1v, s2v, do4, delta, acc, kvt, dqt, dkv_s, dkv_r, dqkv, p4, core_r, hop, fin, hop2, fin2,
              d_q, d_kv, d_out,
              ra0, ra1, rb0, rb1, rc, rd0, rd1, re0, re1, rf0, rf1,
              ta0, ta1, tb0, tb1, tc0, tc1, td0, td1, te0, te1, tf0, tf1,
              qa0, qa1, qb0, qb1, qc0, qc1, qd0, qd1, qe0, qe1, qf0, qf1,
              s_gate, s_up, s_q, s_kv, s_down, s_out, ssem, rsem, lsem, isem, osem):
    gains, wq, wk, wv, w_gate, w_up, dh, x_ref, h, cos, sin, wqkv, wout, qp, kv, o, lse = ins
    out, gt, gain_out, q_out, k_out, v_out, wo_out, gate_out, up_out, down_out = vals
    z, c, x, y = (lax.axis_index(a) for a in ALL)
    peers = [to for _, to in tp_peers(c, x)]
    for axis, q in (("y", y), ("z", z)):
        peers += [{axis: lax.rem(q + k, 4)} for k in (1, 2, 3)]
    first = (12, 15, 13, 14, 16, 9, 10)
    order = first + tuple(i for i in range(17) if i not in first)
    loaded = fetch([(ins_from[i], ins[i]) for i in order], isem)
    saved = []

    def give(i):
        cp = pltpu.make_async_copy(vals[i], outs[i], osem.at[i])
        cp.start()
        saved.append(cp)

    entry(peers, (z != x, {"z": x, "x": z}))
    w = Mail(ssem, rsem)
    ag = gather8(w, da, dav)
    pump([ag])
    loads = [pltpu.make_async_copy(a, b, lsem.at[i]) for i, (a, b) in enumerate(
        ((da, dav.at[c, x]), (s2, s2v), (n1g, n1v), (r1_down, rc)))]
    for cp in loads:
        cp.start()
    jobs_down = [
        row_job(w, g_down, rc.at[0], tc0, qc0, s_down, 0, z, y, lsem.at[7], loads[3]),
        row_job(w, g_down, rc.at[1], tc1, qc1, s_down, 1, z, y, lsem.at[8], loads[3]),
    ]
    jobs = [
        col_job(w, g_gate, ra0, ta0, qa0, s_gate, 0, z, y, lsem.at[4]),
        col_job(w, g_gate, ra1, ta1, qa1, s_gate, 1, z, y, lsem.at[5]),
        col_job(w, g_up, rb0, tb0, qb0, s_up, 0, z, y, lsem.at[6]),
        col_job(w, g_up, rb1, tb1, qb1, s_up, 1, z, y, lsem.at[9]),
    ]
    pump(jobs_down)
    pump(jobs)
    pump([ag])
    loads[0].wait()
    pump([ag])
    pump([ag])
    pump([ag])
    pump([ag])
    loads[1].wait()
    loads[3].wait()
    tail2 = ring_tail(w, s2v, hop2, fin2)
    pump([tail2])
    pump([ag])

    for cp in loaded:
        cp.wait()
    ow = wout[...].reshape(256, 2048)
    for g in range(2):
        dv = dott(dav[g].reshape(512, 2048), ow).astype(BF).astype(F32)
        ov = o[g].astype(F32)
        for t in range(2):
            v = dv[:, 128 * t: 128 * t + 128]
            pr = v * ov[:, 128 * t: 128 * t + 128]
            low = lanes(v.shape) < 64
            for b, head in enumerate((pltpu.roll(v, 64, 1), v)):
                rows = pl.ds(128 * (2 * t + b), 128)
                do4[g, :, rows, :] = jnp.where(low, 0.0, head).astype(BF).reshape(4, 128, 128)
                total = jnp.sum(jnp.where(low == (b == 0), pr, 0.0), axis=1, keepdims=True)
                total = jnp.broadcast_to(total, (512, 128)).T
                for j in range(4):
                    delta[g, pl.ds(j, 1), rows] = total[0:1, 128 * j: 128 * j + 128]

    ot = o[...].reshape(1024, 256).T

    @pl.loop(0, 8)
    def _(i):
        cols = pl.ds(pl.multiple_of(256 * i, 256), 256)
        d_out[:, :, :, cols] = dot(ot, dav[:, :, :, cols].reshape(1024, 256)).astype(BF).reshape(4, 4, 16, 256)

    jobs_out = [
        row_job(w, d_out, rd0, td0, qd0, s_out, 0, z, y, lsem.at[10]),
        row_job(w, d_out, rd1, td1, qd1, s_out, 1, z, y, lsem.at[11]),
    ]
    pump(jobs_out)

    g0, g1 = 1 - c, c
    waits = {}
    for no, g in enumerate((g0, g1)):
        kvt[...] = kv[g].reshape(2048, 128).T
        acc[...] = jnp.zeros_like(acc)
        for j in range(4):
            qj, doj = qp[g, j], do4[g, j]
            lse_row, delta_row = lse[g, pl.ds(j, 1), :], delta[g, pl.ds(j, 1), :]
            col = lanes((1, 512))
            place = (4 * j + y) * 128 + lax.rem(col, 128)
            c1, c2 = lens[g, 0], lens[g, 0] + lens[g, 1]
            start = jnp.where(place >= c2, c2, jnp.where(place >= c1, c1, 0))
            dqt[...] = jnp.zeros_like(dqt)

            @pl.loop(0, j + 1)
            def _(b):
                keys = kv[g, b].reshape(512, 128)
                at = 512 * b + lax.broadcasted_iota(jnp.int32, (512, 512), 0)
                ok = (at >= start) & (at <= place)
                pt = jnp.where(ok, jnp.exp(dott(keys, qj) - lse_row), 0.0)
                ds = (pt * (dott(keys, doj) - delta_row)).astype(BF)
                acc[b] += dot(ds, qj) + dot(pt.astype(BF), doj)
                dqt[...] += dot(kvt[:, pl.ds(pl.multiple_of(512 * b, 512), 512)], ds)

            dq = dqt[...].T
            rows = pl.ds(128 * j, 128)
            cs, sn = cos[g, rows, :], sin[g, rows, :]
            for t in range(2):
                v = pair_heads(dq[256 * t: 256 * t + 128], dq[256 * t + 128: 256 * t + 256], True) * (HD ** -0.5)
                dqkv[g, rows, 128 * t: 128 * t + 128] = (v * cs - swap_halves(v) * sn).astype(BF)
            if no == 0 and j == 2:
                pump([tail2])
            if no == 1 and j == 2:
                pump(jobs_out)
        dkv_s[no] = acc[...].astype(BF).reshape(4, 4, 128, 128)
        waits[no] = others(w, y, "y", lambda p, no=no: dkv_s.at[no, :, p], dkv_r.at[no])
        if no == 0:
            pump(jobs_down)
            pump(jobs)
    pump(jobs)
    ends = [hand_out(w, s_gate, f_gate, c, x), hand_out(w, s_up, f_up, c, x)]
    pump(ends)
    pump([tail2])
    loads[2].wait()
    dv = dqkv[:, :, 0:256].reshape(1024, 256)

    @pl.loop(0, 8)
    def _(i):
        cols = pl.ds(pl.multiple_of(256 * i, 256), 256)
        d_q[i // 2, i % 2] = dot(n1v[:, :, :, cols].reshape(1024, 256).T, dv).astype(BF).reshape(4, 4, 16, 256)

    jobs_q = [
        col_job(w, d_q, re0, te0, qe0, s_q, 0, z, y, lsem.at[12]),
        col_job(w, d_q, re1, te1, qe1, s_q, 1, z, y, lsem.at[13]),
    ]
    pump(jobs_q)

    state = {}
    for no, g in enumerate((g0, g1)):
        for a in waits[no]:
            w.got(*a)
        for j in range(4):
            rows = pl.ds(128 * j, 128)
            v = dkv_s[no, j, y].astype(F32)
            for k in range(3):
                v += dkv_r[no, k, j].astype(F32)
            turned = v * cos[g, rows, :] - swap_halves(v) * sin[g, rows, :]
            dqkv[g, rows, 256:384] = jnp.where(lanes(v.shape) < 64, turned, v).astype(BF)

        @pl.loop(0, 8)
        def _(i):
            wt = wqkv[i // 2, i % 2].reshape(256, 384)
            p4[g, :, :, pl.ds(pl.multiple_of(256 * i, 256), 256)] = dott(dqkv[g], wt).astype(BF).reshape(4, 128, 256)

        if no == 0:
            scatter8_core(w, p4, core_r, state)
    rs = scatter8_ring(w, p4, core_r, hop, fin, state)
    pump([rs])
    pump([rs])
    dv = dqkv[:, :, 256:384].reshape(1024, 128)

    @pl.loop(0, 8)
    def _(i):
        cols = pl.ds(pl.multiple_of(256 * i, 256), 256)
        d_kv[i // 2, i % 2] = dot(n1v[:, :, :, cols].reshape(1024, 256).T, dv).astype(BF).reshape(4, 4, 16, 128)

    jobs_kv = [
        col_job(w, d_kv, rf0, tf0, qf0, s_kv, 0, z, y, lsem.at[14]),
        col_job(w, d_kv, rf1, tf1, qf1, s_kv, 1, z, y, lsem.at[15]),
    ]
    pump(jobs_kv)

    @pl.loop(0, 8)
    def _(i):
        rows = pl.ds(pl.multiple_of(i * 16, 16), 16)
        v = h[rows, :] + s2v[x, rows, :].astype(F32) + fin2[0, rows, :].astype(F32) + fin2[1, rows, :].astype(F32)
        out[rows, :] = v.astype(BF)

    give(0)

    pump([rs])
    pump(jobs_out)
    pump(jobs_q)
    pump(jobs_kv)
    more = [transpose_zx(w, s_out, lambda zz: f_out, z, x, lsem.at[17])]
    pump(more)
    pump(jobs_q)
    pump(jobs_kv)
    more += [hand_out(w, s_q, f_q, c, x), hand_out(w, s_kv, f_kv, c, x)]
    pump(more[1:])
    pump(jobs_down)
    down_out[...] = s_down[0:44, :].astype(F32)
    give(9)
    pump(ends)
    gain1, gain2 = gains[0], gains[1]
    total = jnp.zeros((16, 128), F32)
    for f, wt, res in ((f_gate, w_gate, gate_out), (f_up, w_up, up_out)):
        for t in range(44):
            tile = None
            for r, move in collect_moves(t):
                piece = take_lanes(lambda a: f[r, :, 128 * a: 128 * a + 128].astype(F32), [move])
                tile = piece if tile is None else tile + piece
            cols = slice(128 * t, 128 * t + 128)
            total += tile * wt[:, cols].astype(F32)
            res[:, cols] = tile * gain2
    give(7)
    give(8)
    gain_out[1] = jnp.broadcast_to(jnp.sum(total, axis=1, keepdims=True), (16, 128))
    pump([rs])

    @pl.loop(0, 8)
    def _(i):
        rows = pl.ds(pl.multiple_of(i * 16, 16), 16)
        e = p4[c, x, rows, :].astype(F32) + core_r[3, rows, :].astype(F32)
        e = e + fin[0, rows, :].astype(F32) + fin[1, rows, :].astype(F32)
        v = x_ref[rows, :].astype(F32)
        r = lax.rsqrt(jnp.mean(v * v, axis=1, keepdims=True) + EPS)
        gt[rows, :] = dh[rows, :] + r * e - v * (r * r * r * jnp.mean(e * v, axis=1, keepdims=True))

    give(1)
    pump(more)
    wo_out[...] = f_out[...].astype(F32)
    total = jnp.zeros((16, 128), F32)
    for r in range(8):
        for t in range(2):
            cols = slice(256 * r + 128 * t, 256 * r + 128 * t + 128)
            tile = f_q[r, :, 128 * t: 128 * t + 128].astype(F32)
            total += tile * wq[:, cols].astype(F32)
            q_out[:, cols] = tile * gain1
    heads = [f_kv[2 * a].astype(F32) + f_kv[2 * a + 1].astype(F32) for a in range(4)]
    for t in range(2):
        cols = slice(128 * t, 128 * t + 128)
        for res, wt, lower in ((k_out, wk, True), (v_out, wv, False)):
            tile = pair_heads(heads[2 * t], heads[2 * t + 1], lower)
            total += tile * wt[:, cols].astype(F32)
            res[:, cols] = tile * gain1
    gain_out[0] = jnp.broadcast_to(jnp.sum(total, axis=1, keepdims=True), (16, 128))
    for i in (2, 3, 4, 5, 6):
        give(i)
    w.drain()
    for cp in saved:
        cp.wait()


def backward_attention(
        lens, gains, wq, wk, wv, w_gate, w_up, da, dh, x, h, cos, sin, n1g, wqkv, wout, qp, kv, o, lse,
        s2, g_gate, g_up, g_down, r1_down, cid):
    sds = jax.ShapeDtypeStruct
    hb = pl.BlockSpec(memory_space=ANY)
    outs = [sds((128, 2048), BF)] + [sds(a, F32) for a in (
        (128, 2048), (2, 16, 128), (16, 2048), (16, 256), (16, 256), (16, 2048), (16, 5632), (16, 5632), (44, 2048))]
    b = lambda *s: VMEM(s, BF)
    ns = (768, 768, 256, 128)
    r1 = [b(3, 4, 4, 16, 768)] * 4 + [b(2, 3, 4, 48, 1024)] + [b(3, 4, 16, 1024)] * 2
    r1 += [b(3, 4, 4, 16, 256)] * 2 + [b(3, 4, 4, 16, 128)] * 2
    t1 = [b(4, 4, 16, 768)] * 4 + [b(4, 48, 1024)] * 2 + [b(4, 16, 1024)] * 2
    t1 += [b(4, 4, 16, 256)] * 2 + [b(4, 4, 16, 128)] * 2
    r2 = [b(3, 4, 16, 768)] * 4 + [b(3, 48, 1024)] * 2 + [b(3, 16, 1024)] * 2
    r2 += [b(3, 4, 16, 256)] * 2 + [b(3, 4, 16, 128)] * 2
    return pl.pallas_call(
        m3_kernel,
        out_shape=outs,
        in_specs=[pl.BlockSpec(memory_space=pltpu.SMEM)] + [hb] * 24,
        out_specs=[hb] * 10,
        scratch_shapes=[VMEM(a.shape, a.dtype) for a in outs] + [VMEM(a.shape, a.dtype) for a in (
            gains, wq, wk, wv, w_gate, w_up, dh, x, h, cos, sin, wqkv, wout, qp, kv, o, lse)] + [
            b(8, 16, 768), b(8, 16, 768), b(8, 16, 256), b(8, 16, 128), b(16, 2048),
            b(2, 4, 128, 2048), b(2, 4, 128, 2048), b(4, 128, 2048), b(2, 4, 512, 128), VMEM((2, 4, 512), F32),
            VMEM((4, 512, 128), F32), b(128, 2048), VMEM((128, 512), F32), b(2, 4, 4, 128, 128),
            b(2, 3, 4, 128, 128), b(2, 512, 384), b(2, 4, 128, 2048), b(4, 128, 2048), b(2, 64, 2048),
            b(2, 128, 2048), b(2, 64, 2048), b(2, 128, 2048),
            b(4, 2, 4, 4, 16, 256), b(4, 2, 4, 4, 16, 128), b(4, 4, 16, 2048),
        ] + r1 + t1 + r2 + [
            b(2, 4, 16, 768), b(2, 4, 16, 768), b(2, 4, 16, 256), b(2, 4, 16, 128), b(48, 2048), b(16, 2048),
            pltpu.SemaphoreType.DMA((150,)), pltpu.SemaphoreType.DMA((150,)), pltpu.SemaphoreType.DMA((18,)),
            pltpu.SemaphoreType.DMA((17,)), pltpu.SemaphoreType.DMA((10,)),
        ],
        compiler_params=comm_params(cid, 63),
        name="backward_attention",
    )(lens, gains, wq, wk, wv, w_gate, w_up, da, dh, x, h, cos, sin, n1g, wqkv, wout, qp, kv, o, lse, s2, g_gate, g_up, g_down, r1_down)


def copy_kernel(n, *refs):
    ins, outs, held, isem, osem = refs[:n], refs[n:2 * n], refs[2 * n:3 * n], refs[-2], refs[-1]
    loads = fetch(list(zip(ins, held)), isem)
    stores = [pltpu.make_async_copy(held[i], outs[i], osem.at[i]) for i in range(n)]
    for i in range(n):
        loads[i].wait()
        stores[i].start()
    for cp in stores:
        cp.wait()


def copied(arrays):
    hb = pl.BlockSpec(memory_space=ANY)
    return pl.pallas_call(
        functools.partial(copy_kernel, len(arrays)),
        out_shape=[jax.ShapeDtypeStruct(a.shape, a.dtype) for a in arrays],
        in_specs=[hb] * len(arrays),
        out_specs=[hb] * len(arrays),
        scratch_shapes=[VMEM(a.shape, a.dtype) for a in arrays] + [pltpu.SemaphoreType.DMA((len(arrays),))] * 2,
        name="results",
    )(*arrays)


def local(tokens, lengths, attn_gain, w_query, w_key, w_value, w_out, mlp_gain, w_gate, w_up, w_down, cotangent):
    lens = lax.all_gather(lengths, "core", axis=0, tiled=True)
    inputs = tokens.astype(F32)
    n1 = (inputs * lax.rsqrt(jnp.mean(inputs * inputs, axis=1, keepdims=True) + EPS)).astype(BF)
    gains = jnp.broadcast_to(jnp.stack([attn_gain, mlp_gain]).astype(F32)[..., None], (2, 16, 128))
    h, n1g, qp, kv, o, lse, wqkv, wout, cos, sin, dh, da, s2, g_gate, g_up, g_down, r1_down = forward_layer(
        lens, gains, tokens, n1, cotangent, w_query, w_key, w_value, w_out, w_gate, w_up, w_down, 1)
    col = (4, 2, 4, 4, 16, 768)
    output, grad_tokens, gain, g_q, g_k, g_v, g_o, g_gate, g_up, g_down = backward_attention(
        lens, gains, w_query, w_key, w_value, w_gate, w_up, da, dh, tokens, h, cos, sin, n1g, wqkv, wout,
        qp, kv, o, lse, s2, g_gate.reshape(col), g_up.reshape(col), g_down, r1_down, 2)
    output, grad_tokens, g_q, g_k, g_v, g_o, g_gate, g_up, g_down = copied(
        (output, grad_tokens, g_q, g_k, g_v, g_o, g_gate, g_up, g_down))
    return (output, grad_tokens, gain[0, :, 0], g_q, g_k, g_v, g_o, gain[1, :, 0], g_gate, g_up, g_down)


def solution(mesh):
    fine = Mesh(mesh.devices.reshape(4, 2, 4, 4), ALL)
    rows, flat = P(ALL, None), P(ALL)
    in_specs = (rows, P(("z", "core"), None), flat, rows, rows, rows, rows, flat, rows, rows, rows, rows)
    out_specs = (rows, rows, flat, rows, rows, rows, rows, flat, rows, rows, rows)
    return jax.shard_map(local, mesh=fine, in_specs=in_specs, out_specs=out_specs, check_vma=False)
```

```python
import functools
import math

import jax
import jax.numpy as jnp
from jax import lax
from jax.experimental import pallas as pl
from jax.experimental.pallas import tpu as pltpu
from jax.sharding import Mesh
from jax.sharding import PartitionSpec as P

HEADS = 32
KV_HEADS = 4
HD = 64
EPS = 1e-05
THETA = 10000.0
NEG = -1e30
BF = jnp.bfloat16
F32 = jnp.float32
ANY = pl.ANY
VMEM = pltpu.VMEM
TP = ("x", "core")
DP = ("z", "y")
ALL = ("z", "core", "x", "y")


def tdot(a, b):
    return lax.dot_general(a, b, (((0,), (0,)), ((), ())), preferred_element_type=F32)


def dott(a, b):
    return lax.dot_general(a, b, (((1,), (1,)), ((), ())), preferred_element_type=F32)


def dot(a, b):
    return jnp.dot(a, b, preferred_element_type=F32)


class Wire:
    def __init__(self, ssem, rsem):
        self.ssem, self.rsem, self.sent = ssem, rsem, []

    def put(self, src, dst, k, to):
        cp = pltpu.make_async_remote_copy(
            src_ref=src, dst_ref=dst, send_sem=self.ssem.at[k], recv_sem=self.rsem.at[k],
            device_id=to, device_id_type=pl.DeviceIdType.MESH)
        cp.start()
        self.sent.append(cp)
        return cp

    def settle(self, copies):
        for cp in copies:
            cp.wait_send()
        done = {id(cp) for cp in copies}
        self.sent = [cp for cp in self.sent if id(cp) not in done]

    def got(self, dst, k, to):
        pltpu.make_async_remote_copy(
            src_ref=dst, dst_ref=dst, send_sem=self.ssem.at[k], recv_sem=self.rsem.at[k],
            device_id=to, device_id_type=pl.DeviceIdType.MESH).wait_recv()

    def drain(self):
        for cp in self.sent:
            cp.wait_send()


def greet(peers):
    barrier = pltpu.get_barrier_semaphore()
    for to in peers:
        pl.semaphore_signal(barrier, inc=1, device_id=to, device_id_type=pl.DeviceIdType.MESH)
    pl.semaphore_wait(barrier, len(peers))


def cx_ring():
    c, x = lax.axis_index("core"), lax.axis_index("x")
    right, left, opp = lax.rem(x + 1, 4), lax.rem(x + 3, 4), lax.rem(x + 2, 4)
    return c, x, right, left, opp, {"x": right}, {"x": left}, {"core": 1 - c}


def comm_params(cid, mb=None):
    kw = {} if mb is None else {"vmem_limit_bytes": mb << 20}
    return pltpu.CompilerParams(collective_id=cid, has_side_effects=True, **kw)


class Mail(Wire):
    def __init__(self, ssem, rsem):
        super().__init__(ssem, rsem)
        self.used = 0

    def new(self):
        self.used += 1
        return self.used - 1


def around(q):
    return lax.rem(q + 1, 4), lax.rem(q + 3, 4), lax.rem(q + 2, 4)


def ring(w, s, axis, q):
    right, left, opp = around(q)
    to_r, to_l = {axis: right}, {axis: left}
    k = [w.new() for _ in range(4)]
    w.put(s(q, None), s(q, None), k[0], to_r)
    w.put(s(q, None), s(q, None), k[1], to_l)
    yield
    w.got(s(left, None), k[0], to_l)
    w.put(s(left, 0), s(left, 0), k[2], to_r)
    w.got(s(right, None), k[1], to_r)
    w.put(s(right, 1), s(right, 1), k[3], to_l)
    yield
    w.got(s(opp, 0), k[2], to_l)
    w.got(s(opp, 1), k[3], to_r)


def col_flows(w, W, z, y):
    cut = lambda h: slice(None) if h is None else pl.ds(2 * h, 2)

    def first():
        yield from ring(w, lambda p, h: W.at[z, 0, cut(h), p], "y", y)
        yield from ring(w, lambda p, h: W.at[p, 0, cut(h)], "z", z)

    def second():
        yield from ring(w, lambda p, h: W.at[p, 1, cut(h), y], "z", z)
        yield from ring(w, lambda p, h: W.at[:, 1, cut(h), p], "y", y)

    return [first(), second()]


def row_flows(w, W, z, y):
    n = W.shape[-1] // 4
    cut = lambda b, h: pl.ds(2 * n * b, 2 * n) if h is None else pl.ds(2 * n * b + n * h, n)

    def first():
        yield from ring(w, lambda p, h: W.at[z, p, :, cut(0, h)], "y", y)
        yield from ring(w, lambda p, h: W.at[p, :, :, cut(0, h)], "z", z)

    def second():
        yield from ring(w, lambda p, h: W.at[p, y, :, cut(1, h)], "z", z)
        yield from ring(w, lambda p, h: W.at[:, p, :, cut(1, h)], "y", y)

    return [first(), second()]


def straight(w, stages):
    for s, axis, q in stages:
        ks = {}
        for k in (1, 3, 2):
            ks[k] = w.new()
            w.put(s(q), s(q), ks[k], {axis: lax.rem(q + k, 4)})
        yield
        for k in (1, 3, 2):
            frm = lax.rem(q + 4 - k, 4)
            w.got(s(frm), ks[k], {axis: frm})


def col_straight(w, W, z, y):
    return [straight(w, [(lambda p: W.at[z, 0, :, p], "y", y), (lambda p: W.at[p, 0], "z", z)]),
            straight(w, [(lambda p: W.at[p, 1, :, y], "z", z), (lambda p: W.at[:, 1, :, p], "y", y)])]


def row_straight(w, W, z, y):
    n = W.shape[-1] // 2
    a, b = pl.ds(0, n), pl.ds(n, n)
    return [straight(w, [(lambda p: W.at[z, p, :, a], "y", y), (lambda p: W.at[p, :, :, a], "z", z)]),
            straight(w, [(lambda p: W.at[p, y, :, b], "z", z), (lambda p: W.at[:, p, :, b], "y", y)])]


def pump(flows):
    for f in flows:
        next(f, None)


def gather8(w, src, dst):
    c, x, right, left, opp, to_r, to_l, to_c = cx_ring()
    rows = dst.shape[2]
    lo, hi = pl.ds(0, rows // 2), pl.ds(rows // 2, rows // 2)
    k = [w.new() for _ in range(10)]
    out = []
    out += [w.put(src.at[lo], dst.at[c, x, lo], k[0], to_r)]
    out += [w.put(src.at[hi], dst.at[c, x, hi], k[1], to_l)]
    out += [w.put(src.at[hi], dst.at[c, x, hi], k[2], to_r)]
    out += [w.put(src.at[lo], dst.at[c, x, lo], k[3], to_l)]
    out += [w.put(src, dst.at[c, x], k[4], to_c)]
    yield
    w.got(dst.at[c, left, lo], k[0], to_l)
    out += [w.put(dst.at[c, left, lo], dst.at[c, left, lo], k[5], to_r)]
    w.got(dst.at[c, right, hi], k[1], to_r)
    out += [w.put(dst.at[c, right, hi], dst.at[c, right, hi], k[6], to_l)]
    yield
    w.got(dst.at[1 - c, x], k[4], to_c)
    yield
    w.got(dst.at[c, left, hi], k[2], to_l)
    out += [w.put(dst.at[c, left], dst.at[c, left], k[7], to_c)]
    w.got(dst.at[c, right, lo], k[3], to_r)
    out += [w.put(dst.at[c, right], dst.at[c, right], k[8], to_c)]
    yield
    w.got(dst.at[1 - c, left], k[7], to_c)
    w.got(dst.at[1 - c, right], k[8], to_c)
    yield
    w.got(dst.at[c, opp, lo], k[5], to_l)
    w.got(dst.at[c, opp, hi], k[6], to_r)
    out += [w.put(dst.at[c, opp], dst.at[c, opp], k[9], to_c)]
    yield
    w.got(dst.at[1 - c, opp], k[9], to_c)
    w.settle(out)


def add_to(dst, other, r0, rows, step=16):
    @pl.loop(0, rows // step)
    def _(i):
        a = pl.ds(pl.multiple_of(r0 + i * step, step), step)
        b = pl.ds(pl.multiple_of(i * step, step), step)
        dst[a, :] = (dst[a, :].astype(F32) + other[b, :].astype(F32)).astype(dst.dtype)


def scatter8_core(w, p, core_r, state, only=None):
    c, x, right, left, opp, to_r, to_l, to_c = cx_ring()
    if not state:
        state["k"], state["out"] = [w.new() for _ in range(4)], []
    for i, xx in enumerate((opp, right, left, x)):
        if only is None or only == i:
            state["out"].append(w.put(p.at[1 - c, xx], core_r.at[i], state["k"][i], to_c))


def scatter8_ring(w, p, core_r, hop, fin, state):
    c, x, right, left, opp, to_r, to_l, to_c = cx_ring()
    rows = p.shape[2]
    half = rows // 2
    lo, hi = pl.ds(0, half), pl.ds(half, half)
    kc, out = state["k"], state["out"]
    k = [w.new() for _ in range(6)]
    w.got(core_r.at[0], kc[0], to_c)
    add_to(p.at[c, opp], core_r.at[0], 0, rows)
    out += [w.put(p.at[c, opp, lo], hop.at[0], k[0], to_r)]
    out += [w.put(p.at[c, opp, hi], hop.at[1], k[1], to_l)]
    yield
    w.got(core_r.at[1], kc[1], to_c)
    add_to(p.at[c, right], core_r.at[1], 0, rows)
    out += [w.put(p.at[c, right, hi], fin.at[0, hi], k[2], to_r)]
    w.got(core_r.at[2], kc[2], to_c)
    add_to(p.at[c, left], core_r.at[2], 0, rows)
    out += [w.put(p.at[c, left, lo], fin.at[1, lo], k[3], to_l)]
    yield
    w.got(hop.at[0], k[0], to_l)
    add_to(p.at[c, right], hop.at[0], 0, half)
    out += [w.put(p.at[c, right, lo], fin.at[0, lo], k[4], to_r)]
    w.got(hop.at[1], k[1], to_r)
    add_to(p.at[c, left], hop.at[1], half, half)
    out += [w.put(p.at[c, left, hi], fin.at[1, hi], k[5], to_l)]
    yield
    w.got(core_r.at[3], kc[3], to_c)
    w.got(fin.at[0, hi], k[2], to_l)
    w.got(fin.at[1, lo], k[3], to_r)
    w.got(fin.at[0, lo], k[4], to_l)
    w.got(fin.at[1, hi], k[5], to_r)
    w.settle(out)


def lanes(shape):
    return lax.broadcasted_iota(jnp.int32, shape, len(shape) - 1)


def take_lanes(load, moves):
    out = None
    for src, lo, hi in moves:
        a, shift = (src - lo) // 128, (src - lo) % 128
        split = 128 - shift
        turned = lambda t: pltpu.roll(load(t), (128 - shift) % 128, 1) if shift else load(t)
        if hi <= split:
            piece = turned(a)
        elif lo >= split:
            piece = turned(a + 1)
        else:
            piece = jnp.where(lanes((16, 128)) < split, turned(a), turned(a + 1))
        at = lanes(piece.shape)
        out = jnp.where((at >= lo) & (at < hi), piece, jnp.zeros_like(piece) if out is None else out)
    return out


def fetch(pairs, sems):
    copies = [pltpu.make_async_copy(src, dst, sems.at[i]) for i, (src, dst) in enumerate(pairs)]
    for cp in copies:
        cp.start()
    return copies


def unit_place(z, c, x, y):
    return ((z * 2 + c) * 4 + x) * 4 + y


def spread_moves(r, t):
    out = []
    for s in range(16):
        d0 = 48 * s
        lo, hi = max(d0, 128 * t), min(d0 + 44, 128 * t + 128)
        if lo < hi:
            unit = unit_place(s // 4, r % 2, r // 2, s % 4)
            out.append((44 * unit + lo - d0, lo - 128 * t, hi - 128 * t))
    return out


def collect_moves(t):
    out = []
    for unit in range(128):
        d0 = 44 * unit
        lo, hi = max(d0, 128 * t), min(d0 + 44, 128 * t + 128)
        if lo < hi:
            z, c, x, y = unit // 32, unit // 16 % 2, unit // 4 % 4, unit % 4
            out.append((2 * x + c, (48 * (4 * z + y) + lo - d0, lo - 128 * t, hi - 128 * t)))
    return out


def swap_halves(u):
    first = lax.rem(lanes(u.shape), 64) < 32
    return jnp.where(first, pltpu.roll(u, 96, u.ndim - 1), pltpu.roll(u, 32, u.ndim - 1))


def entry(peers, extra=None):
    barrier = pltpu.get_barrier_semaphore()
    for to in peers:
        pl.semaphore_signal(barrier, inc=1, device_id=to, device_id_type=pl.DeviceIdType.MESH)
    if extra is None:
        pl.semaphore_wait(barrier, len(peers))
        return
    more, to = extra

    @pl.when(more)
    def _():
        pl.semaphore_signal(barrier, inc=1, device_id=to, device_id_type=pl.DeviceIdType.MESH)
        pl.semaphore_wait(barrier, len(peers) + 1)

    @pl.when(jnp.logical_not(more))
    def _():
        pl.semaphore_wait(barrier, len(peers))


def tp_peers(c, x):
    r = 2 * x + c
    out = []
    for k in range(1, 8):
        rr = lax.rem(r + k, 8)
        out.append((rr, {"x": rr // 2, "core": lax.rem(rr, 2)}))
    return out


def spread(w, src, W, z, c, x, y, local_sem):
    ks = [w.new() for _ in range(7)]
    for k, (rr, to) in zip(ks, tp_peers(c, x)):
        w.put(src.at[rr], W.at[z, c, x, y], k, to)
    own = pltpu.make_async_copy(src.at[2 * x + c], W.at[z, c, x, y], local_sem)
    own.start()
    yield
    r = 2 * x + c
    for i, k in enumerate(ks):
        rr = lax.rem(r + 7 - i, 8)
        w.got(W.at[z, lax.rem(rr, 2), rr // 2, y], k, {"x": rr // 2, "core": lax.rem(rr, 2)})
    own.wait()


def transpose_zx(w, src, dst_of, z, x, local_sem):
    k = w.new()
    to = {"z": x, "x": z}

    def far():
        return pltpu.make_async_remote_copy(
            src_ref=src, dst_ref=dst_of(x), send_sem=w.ssem.at[k], recv_sem=w.rsem.at[k],
            device_id=to, device_id_type=pl.DeviceIdType.MESH)

    def near():
        return pltpu.make_async_copy(src, dst_of(x), local_sem)

    @pl.when(z != x)
    def _():
        far().start()

    @pl.when(z == x)
    def _():
        near().start()

    yield

    @pl.when(z != x)
    def _():
        far().wait_send()
        w.got(dst_of(z), k, to)

    @pl.when(z == x)
    def _():
        near().wait()


def attend(q, keys, j, y, c1, c2):
    m, n = q.shape[0], keys.shape[0]
    s = dott(q, keys)
    row = lax.broadcasted_iota(jnp.int32, (m, 1), 0)
    place = (4 * j + y) * 128 + lax.rem(row, 128)
    start = jnp.where(place >= c2, c2, jnp.where(place >= c1, c1, 0))
    at = lax.broadcasted_iota(jnp.int32, (m, n), 1)
    s = jnp.where((at >= start) & (at <= place), s, NEG)
    top = jnp.max(s, axis=1, keepdims=True)
    e = jnp.exp(s - top)
    total = jnp.sum(e, axis=1, keepdims=True)
    return dot(e.astype(BF), keys) / total, top + jnp.log(total)


def pair_heads(first, second, lower):
    low = lanes(first.shape) < 64
    if lower:
        return jnp.where(low, first, pltpu.roll(second, 64, 1))
    return jnp.where(low, pltpu.roll(first, 64, 1), second)


def forward_kernel(lens, gains_in, x_in, n1_in, cot_in, wq_in, wk_in, wv_in, out_s, gate_in, up_in, down_in,
                   h_out, n1_out, qp_out, kv_out, o_out, lse_out, wqkv_out, wout_out, cos_out, sin_out,
                   dh_out, da_out, s2, g_gate, g_up, g_down, r1_down,
                   cos, sin, h, qp, kv, o, lse, wqkv, wout, n1, cv, wg, wu, wd, p, core_r, hop, fin,
                   dact, a_all, dg_all, du_all, core2, d_down, qkv_s, gate_s, up_s,
                   gains, x_ref, cot, wq, wk, wv, w_gate, w_up, w_down, ssem, rsem, lsem, osem, isem):
    z, c, x, y = (lax.axis_index(a) for a in ALL)
    peers = [to for _, to in tp_peers(c, x)]
    for axis, q in (("y", y), ("z", z)):
        peers += [{axis: lax.rem(q + k, 4)} for k in (1, 2, 3)]
    w = Mail(ssem, rsem)
    loads = fetch(((gains_in, gains), (wq_in, wq), (wk_in, wk), (wv_in, wv), (n1_in, n1.at[c, x]), (down_in, w_down),
                   (gate_in, w_gate), (up_in, w_up), (cot_in, cot), (x_in, x_ref)), isem)
    saved = []

    def save(src, dst):
        cp = pltpu.make_async_copy(src, dst, osem.at[len(saved)])
        cp.start()
        saved.append(cp)
        return cp

    for cp in loads[:4]:
        cp.wait()
    gain1, gain2 = gains[0], gains[1]
    for r in range(8):
        for t in range(2):
            at = 256 * r + 128 * t
            qkv_s[r, :, 128 * t: 128 * t + 128] = (wq[:, at: at + 128].astype(F32) * gain1).astype(BF)
        t, odd = r // 4, r // 2 % 2
        kt, vt = wk[:, 128 * t: 128 * t + 128].astype(F32), wv[:, 128 * t: 128 * t + 128].astype(F32)
        kt, vt = (pltpu.roll(kt, 64, 1), vt) if odd else (kt, pltpu.roll(vt, 64, 1))
        qkv_s[r, :, 256:384] = (jnp.where(lanes(kt.shape) < 64, kt, vt) * gain1).astype(BF)
    entry(peers, (z != x, {"z": x, "x": z}))

    sp_qkv = spread(w, qkv_s, wqkv, z, c, x, y, lsem.at[0])
    pump([sp_qkv])
    loads[4].wait()
    ag_n1 = gather8(w, n1.at[c, x], n1)
    pump([ag_n1])
    for cp in loads[5:]:
        cp.wait()
    wd[z, y] = jnp.concatenate([w_down[...], jnp.zeros((4, 2048), BF)], axis=0)
    pump([sp_qkv])
    fl_qkv = col_straight(w, wqkv, z, y)
    pump(fl_qkv)
    for src, dst in ((w_gate, gate_s), (w_up, up_s)):
        for r in range(8):
            for t in range(6):
                load = lambda a: src[:, 128 * a: 128 * a + 128].astype(F32)
                dst[r, :, 128 * t: 128 * t + 128] = (take_lanes(load, spread_moves(r, t)) * gain2).astype(BF)
    pump([ag_n1])
    pump([ag_n1])
    pump(fl_qkv)
    spreads = [spread(w, gate_s, wg, z, c, x, y, lsem.at[2]), spread(w, up_s, wu, z, c, x, y, lsem.at[3])]
    pump(spreads)
    tr_out = transpose_zx(w, out_s, lambda zz: wout.at[zz, y], z, x, lsem.at[1])
    pump([tr_out])
    fl_down = row_flows(w, wd, z, y)
    pump(fl_down)

    for g in range(2):
        lane = lanes((128, 128))
        freq = jnp.exp(lax.rem(lane, 32).astype(F32) * (-2.0 * math.log(THETA) / HD))
        c1, c2 = lens[g, 0], lens[g, 0] + lens[g, 1]

        @pl.loop(0, 4)
        def _(j):
            place = (4 * j + y) * 128 + lax.broadcasted_iota(jnp.int32, (128, 128), 0)
            start = jnp.where(place >= c2, c2, jnp.where(place >= c1, c1, 0))
            angle = (place - start).astype(F32) * freq
            rows = pl.ds(pl.multiple_of(128 * j, 128), 128)
            cos[g, rows, :] = jnp.cos(angle)
            turned = jnp.sin(angle)
            sin[g, rows, :] = jnp.where(lax.rem(lane, 64) < 32, -turned, turned)

    pump([ag_n1])
    pump([tr_out])
    fl_out = row_straight(w, wout, z, y)
    pump(fl_out)
    pump(spreads)
    fl_gu = col_flows(w, wg, z, y) + col_flows(w, wu, z, y)
    pump(fl_gu)
    fl_mlp = fl_down + fl_gu
    pump([ag_n1])
    pump([ag_n1])
    pump(fl_qkv)
    pump([ag_n1])
    weights = wqkv[...].reshape(2048, 384)

    def project(g, keys_too):
        u = dot(n1[g].reshape(512, 2048), weights)
        cs, sn = cos[g], sin[g]
        if keys_too:
            v = u[:, 256:384]
            turned = jnp.where(lanes(v.shape) < 64, v * cs + swap_halves(v) * sn, v)
            kv[g, :, y] = turned.astype(BF).reshape(4, 128, 128)
        for t in range(2):
            v = u[:, 128 * t: 128 * t + 128]
            v = (v * cs + swap_halves(v) * sn) * (HD ** -0.5)
            low = lanes(v.shape) < 64
            for b, head in enumerate((v, pltpu.roll(v, 64, 1))):
                rows = pl.ds(128 * (2 * t + b), 128)
                qp[g, :, rows, :] = jnp.where(low, head, 0.0).astype(BF).reshape(4, 128, 128)

    g0, g1 = 1 - c, c
    to_c = {"core": 1 - c}
    pump(fl_mlp)
    project(g0, True)
    fl_kv = [straight(w, [(lambda pp: kv.at[g0, :, pp], "y", y)])]
    pump(fl_kv)
    pump(fl_out)
    ag_cot = gather8(w, cot, cv)
    pump([ag_cot])
    project(g1, False)
    keep_n1 = save(n1, n1_out)
    save(wqkv, wqkv_out)
    save(cos, cos_out)
    save(sin, sin_out)
    keep_cot = save(cot, cv.at[c, x])
    pump(fl_mlp[0::2])
    pump(fl_kv)
    k_kv = w.new()
    w.put(kv.at[g0], kv.at[g0], k_kv, to_c)
    pump(fl_mlp[1::2])

    state = {}
    for turn_no, g in enumerate((g0, g1)):
        if turn_no == 1:
            w.got(kv.at[g], k_kv, to_c)
            save(kv, kv_out)
            save(qp, qp_out)
            save(wout, wout_out)
        for j in range(4):
            n = 512 * (j + 1)
            keys = kv[g, 0:j + 1].reshape(n, 128)
            for t in range(2):
                part = qp[g, j, 256 * t: 256 * t + 256]
                res, total = attend(part, keys, j, y, lens[g, 0], lens[g, 0] + lens[g, 1])
                both = pair_heads(res[:128], res[128:], False)
                o[g, pl.ds(128 * j, 128), 128 * t: 128 * t + 128] = both.astype(BF)
                lse[g, pl.ds(j, 1), 256 * t: 256 * t + 256] = jnp.broadcast_to(total, (256, 128)).T[0:1, :]
            if j == 2:
                pump([ag_cot])
        pump(fl_out)
        out_w = wout[...].reshape(256, 2048)

        @pl.loop(0, 4)
        def _(i):
            p[g, i] = dot(o[g, pl.ds(pl.multiple_of(128 * i, 128), 128), :], out_w).astype(BF)

        if turn_no == 0:
            keep_n1.wait()
            scatter8_core(w, p, core_r, state)
    rs = scatter8_ring(w, p, core_r, hop, fin, state)
    pump([rs])
    pump([rs])
    save(o, o_out)
    save(lse, lse_out)
    pump([ag_cot])
    pump([ag_cot])
    pump([ag_cot])
    pump([rs])
    pump([ag_cot])
    pump(fl_mlp[0::2])
    pump(fl_mlp[1::2])
    pump([rs])

    @pl.loop(0, 8)
    def _(i):
        rows = pl.ds(pl.multiple_of(i * 16, 16), 16)
        v = x_ref[rows, :].astype(F32) + p[c, x, rows, :].astype(F32) + core_r[3, rows, :].astype(F32)
        v = v + fin[0, rows, :].astype(F32) + fin[1, rows, :].astype(F32)
        h[rows, :] = v
        n1[c, x, rows, :] = (v * lax.rsqrt(jnp.mean(v * v, axis=1, keepdims=True) + EPS)).astype(BF)

    keep_h = save(h, h_out)
    n2v = n1
    ag = gather8(w, n2v.at[c, x], n2v)
    pump([ag])
    pump(fl_down)
    keep_cot.wait()
    down = wd[...].reshape(768, 2048)

    @pl.loop(0, 2)
    def _(g):
        for t in range(2):
            v = dott(cv[g, 2 * t: 2 * t + 2].reshape(256, 2048), down)
            dact[g, 2 * t: 2 * t + 2] = v.astype(BF).reshape(2, 128, 768)

    pump([ag])
    pump([ag])
    pump(fl_gu)
    cc, xx, right, left, opp, to_r, to_l, to_c = cx_ring()
    st3, st2 = {}, {}

    def block(b, number):
        @pl.loop(0, 3)
        def _(i):
            cols = pl.ds(pl.multiple_of(256 * i, 256), 256)
            nv = n2v[:, b].reshape(256, 2048)
            gp = dot(nv, wg[:, :, :, :, :, cols].reshape(2048, 256))
            u = dot(nv, wu[:, :, :, :, :, cols].reshape(2048, 256))
            sig = jax.nn.sigmoid(gp)
            act = gp * sig
            d = dact[:, b, :, cols].reshape(256, 256).astype(F32)
            a_all[:, b, :, cols] = (act * u).astype(BF).reshape(2, 128, 256)
            dg_all[:, b, :, cols] = (d * u * sig * (1.0 + gp * (1.0 - sig))).astype(BF).reshape(2, 128, 256)
            du_all[:, b, :, cols] = (d * act).astype(BF).reshape(2, 128, 256)

        @pl.loop(0, 8)
        def _(i):
            part = dott(dg_all[:, b].reshape(256, 768), wg[i // 2, i % 2].reshape(256, 768))
            part += dott(du_all[:, b].reshape(256, 768), wu[i // 2, i % 2].reshape(256, 768))
            p[:, b, :, pl.ds(pl.multiple_of(256 * i, 256), 256)] = part.astype(BF).reshape(2, 128, 256)

        scatter8_core(w, p, core_r, st3, number)

    block(x, 3)
    pump([ag])
    pump([ag])
    block(left, 2)
    pump([ag])
    pump([ag])
    block(opp, 0)
    rs3 = scatter8_ring(w, p, core_r, hop, fin, st3)
    pump([rs3])
    block(right, 1)
    pump([rs3])
    at = a_all[...].reshape(1024, 768).T

    @pl.loop(0, 8)
    def _(i):
        cols = pl.ds(pl.multiple_of(256 * i, 256), 256)
        d_down[:, :, :, cols] = dot(at, cv[:, :, :, cols].reshape(1024, 256)).astype(BF).reshape(4, 4, 48, 256)

    first, second = pl.ds(0, 1024), pl.ds(1024, 1024)
    landed = others(w, y, "y", lambda pp: d_down.at[:, pp, :, first], r1_down.at[0])
    landed += others(w, z, "z", lambda pp: d_down.at[pp, :, :, second], r1_down.at[1])
    save(d_down, g_down)

    p2 = cv

    def out_part(g):
        @pl.loop(0, 8)
        def _(i):
            cols = pl.ds(pl.multiple_of(256 * i, 256), 256)
            part = dot(a_all[g].reshape(512, 768), wd[:, :, :, cols].reshape(768, 256))
            p2[g, :, :, cols] = part.astype(BF).reshape(4, 128, 256)

    pump([rs3])
    out_part(g0)
    scatter8_core(w, p2, core2, st2)
    out_part(g1)

    dg, du = dg_all[...].reshape(1024, 768), du_all[...].reshape(1024, 768)

    def stage(i, slot, k):
        return pltpu.make_async_copy(
            dact.at[slot, pl.ds(2 * k, 2)], (g_gate, g_up)[k].at[i], lsem.at[4 + 2 * slot + k])

    @pl.loop(0, 4)
    def _(i):
        for slot in range(2):
            cols = pl.ds(pl.multiple_of(512 * i + 256 * slot, 256), 256)
            t = n2v[:, :, :, cols].reshape(1024, 256).T

            @pl.when(i > 0)
            def _():
                stage(2 * i + slot - 2, slot, 0).wait()
                stage(2 * i + slot - 2, slot, 1).wait()

            dact[slot, 0:2] = dot(t, dg).astype(BF).reshape(2, 128, 768)
            dact[slot, 2:4] = dot(t, du).astype(BF).reshape(2, 128, 768)
            stage(2 * i + slot, slot, 0).start()
            stage(2 * i + slot, slot, 1).start()

    for i, b in enumerate((opp, right, left, x)):
        w.got(core2.at[i], st2["k"][i], to_c)
        add_to(p2.at[c, b], core2.at[i], 0, 128)
    save(p2.at[c], s2)
    pump([rs3])
    keep_h.wait()

    @pl.loop(0, 8)
    def _(i):
        rows = pl.ds(pl.multiple_of(i * 16, 16), 16)
        e = p[c, x, rows, :].astype(F32) + core_r[3, rows, :].astype(F32)
        e = e + fin[0, rows, :].astype(F32) + fin[1, rows, :].astype(F32)
        v = h[rows, :]
        r = lax.rsqrt(jnp.mean(v * v, axis=1, keepdims=True) + EPS)
        out = cot[rows, :].astype(F32) + r * e - v * (r * r * r * jnp.mean(e * v, axis=1, keepdims=True))
        h[rows, :] = out
        n1[c, x, rows, :] = out.astype(BF)

    save(h, dh_out)
    save(n1.at[c, x], da_out)
    w.drain()
    for slot in range(2):
        stage(6 + slot, slot, 0).wait()
        stage(6 + slot, slot, 1).wait()
    for a in landed:
        w.got(*a)
    for cp in saved:
        if all(cp is not a for a in (keep_n1, keep_h, keep_cot)):
            cp.wait()


def forward_layer(lens, gains, tokens, n1, cot, wq, wk, wv, out_s, w_gate, w_up, w_down, cid):
    sds = jax.ShapeDtypeStruct
    hb = pl.BlockSpec(memory_space=ANY)
    col, big = (4, 2, 4, 4, 16, 768), (2, 4, 128, 2048)
    row, half, table = (128, 2048), (2, 4, 128, 768), ((2, 512, 128), F32)
    mid = [((2, 4, 512, 128), BF), ((2, 4, 4, 128, 128), BF), ((2, 512, 256), BF), ((2, 4, 512), F32),
           ((4, 2, 4, 4, 16, 384), BF), ((4, 4, 16, 2048), BF)]
    outs = [(row, F32), (big, BF)] + mid + [table, table] + [
        (row, F32), (row, BF), ((4, 128, 2048), BF), ((8, 2, 128, 768), BF), ((8, 2, 128, 768), BF),
        ((4, 4, 48, 2048), BF), ((2, 3, 4, 48, 1024), BF)]
    scratch = [table, table, (row, F32)] + mid + [
        (big, BF), (big, BF), (col, BF), (col, BF), ((4, 4, 48, 2048), BF),
        (big, BF), ((4, 128, 2048), BF), ((2, 64, 2048), BF), ((2, 128, 2048), BF),
        (half, BF), (half, BF), (half, BF), (half, BF), ((4, 128, 2048), BF), ((4, 4, 48, 2048), BF),
        ((8, 16, 384), BF), ((8, 16, 768), BF), ((8, 16, 768), BF),
        ((2, 16, 128), F32), (row, BF), (row, BF), ((16, 2048), BF), ((16, 256), BF), ((16, 256), BF),
        ((16, 5632), BF), ((16, 5632), BF), ((44, 2048), BF)]
    return pl.pallas_call(
        forward_kernel,
        out_shape=[sds(*a) for a in outs],
        in_specs=[pl.BlockSpec(memory_space=pltpu.SMEM)] + [hb] * 11,
        out_specs=[hb] * len(outs),
        scratch_shapes=[VMEM(*a) for a in scratch] + [
            pltpu.SemaphoreType.DMA((170,)), pltpu.SemaphoreType.DMA((170,)), pltpu.SemaphoreType.DMA((8,)),
            pltpu.SemaphoreType.DMA((18,)), pltpu.SemaphoreType.DMA((10,)),
        ],
        compiler_params=comm_params(cid, 63),
        name="forward_layer",
    )(lens, gains, tokens, n1, cot, wq, wk, wv, out_s, w_gate, w_up, w_down)


def ring_tail(w, s, hop, fin):
    c, x, right, left, opp, to_r, to_l, to_c = cx_ring()
    half = s.shape[1] // 2
    lo, hi = pl.ds(0, half), pl.ds(half, half)
    k = [w.new() for _ in range(6)]
    w.put(s.at[opp, lo], hop.at[0], k[0], to_r)
    w.put(s.at[opp, hi], hop.at[1], k[1], to_l)
    w.put(s.at[right, hi], fin.at[0, hi], k[2], to_r)
    w.put(s.at[left, lo], fin.at[1, lo], k[3], to_l)
    yield
    w.got(hop.at[0], k[0], to_l)
    add_to(s.at[right], hop.at[0], 0, half)
    w.put(s.at[right, lo], fin.at[0, lo], k[4], to_r)
    w.got(hop.at[1], k[1], to_r)
    add_to(s.at[left], hop.at[1], half, half)
    w.put(s.at[left, hi], fin.at[1, hi], k[5], to_l)
    yield
    w.got(fin.at[0, hi], k[2], to_l)
    w.got(fin.at[1, lo], k[3], to_r)
    w.got(fin.at[0, lo], k[4], to_l)
    w.got(fin.at[1, hi], k[5], to_r)


def others(w, q, axis, piece, recv):
    ks = {}
    for k in (1, 3, 2):
        to = lax.rem(q + k, 4)
        ks[k] = w.new()
        w.put(piece(to), recv.at[k - 1], ks[k], {axis: to})
    return [(recv.at[k - 1], ks[k], {axis: lax.rem(q + 4 - k, 4)}) for k in (1, 3, 2)]


def sum_four(dst, own, recv, lead):
    total = math.prod(lead)

    @pl.loop(0, total)
    def _(i):
        at = (i,) if len(lead) == 1 else (i // lead[1], lax.rem(i, lead[1]))
        acc = own[at].astype(F32)
        for k in range(3):
            acc += recv[(k,) + at].astype(F32)
        dst[at] = acc.astype(dst.dtype)


def col_job(w, src, r1, t, r2, s, e, z, y, lsem):
    if e == 0:
        own, piece1, ax1, q1 = src.at[:, 0, :, y], lambda p: src.at[:, 0, :, p], "y", y
        piece2, ax2, q2 = lambda p: t.at[p], "z", z
    else:
        own, piece1, ax1, q1 = src.at[z, 1], lambda p: src.at[p, 1], "z", z
        piece2, ax2, q2 = lambda p: t.at[:, p], "y", y
    first = pltpu.make_async_copy(own, t, lsem)
    first.start()
    waits = others(w, q1, ax1, piece1, r1)
    yield
    first.wait()
    for a in waits:
        w.got(*a)
    sum_four(t, t, r1, (4, 4))
    waits = others(w, q2, ax2, piece2, r2)
    yield
    for a in waits:
        w.got(*a)
    sum_four(s.at[e], piece2(q2), r2, (4,))


def row_job(w, src, r1, t, r2, s, e, z, y, lsem, here=None):
    n = s.shape[-1] // 2
    rows = s.shape[0]
    cols = pl.ds(e * n, n)
    if len(src.shape) == 5:
        at = lambda *q: src.at[(e,) + q]
    else:
        at = lambda *q: src.at[q + (slice(None), cols)]
    if e == 0:
        piece1, ax1, q1, ax2, q2 = lambda p: at(slice(None), p), "y", y, "z", z
    else:
        piece1, ax1, q1, ax2, q2 = lambda p: at(p, slice(None)), "z", z, "y", y
    own = piece1(q1)
    first = pltpu.make_async_copy(own, t, lsem)
    first.start()
    waits = others(w, q1, ax1, piece1, r1) if here is None else []
    yield
    first.wait()
    for a in waits:
        w.got(*a)
    sum_four(t, t, r1, (4,))
    waits = others(w, q2, ax2, lambda p: t.at[p], r2)
    yield
    for a in waits:
        w.got(*a)

    @pl.loop(0, rows // 16)
    def _(i):
        at = pl.ds(pl.multiple_of(i * 16, 16), 16)
        acc = t[q2, at].astype(F32)
        for k in range(3):
            acc += r2[k, at].astype(F32)
        s[at, cols] = acc.astype(BF)


def hand_out(w, s, f, c, x):
    r = 2 * x + c
    ks = [w.new() for _ in range(7)]
    for k, (rr, to) in zip(ks, tp_peers(c, x)):
        w.put(s.at[lax.rem(rr, 2), rr // 2], f.at[r], k, to)
    f[r] = s[c, x]
    yield
    for i, k in enumerate(ks):
        rr = lax.rem(r + 7 - i, 8)
        w.got(f.at[rr], k, {"x": rr // 2, "core": lax.rem(rr, 2)})


def m3_kernel(lens, gains_in, wq_in, wk_in, wv_in, gate_in, up_in, da, dh_in, x_in, h_in, cos_in, sin_in, n1g, wqkv_in,
              wout_in, qp_in, kv_in, o_in, lse_in, s2, g_gate, g_up, g_down, r1_down,
              *rest):
    outs, rest = rest[:10], rest[10:]
    vals, rest = rest[:10], rest[10:]
    ins, rest = rest[:17], rest[17:]
    backward_body(lens, (gains_in, wq_in, wk_in, wv_in, gate_in, up_in, dh_in, x_in, h_in, cos_in, sin_in, wqkv_in,
                         wout_in, qp_in, kv_in, o_in, lse_in), ins, da, n1g, s2, g_gate, g_up, g_down, r1_down,
                  outs, vals, *rest)


def backward_body(lens, ins_from, ins, da, n1g, s2, g_gate, g_up, g_down, r1_down, outs, vals,
              f_gate, f_up, f_q, f_kv, f_out,
              dav, n1v, s2v, do4, delta, acc, kvt, dqt, dkv_s, dkv_r, dqkv, p4, core_r, hop, fin, hop2, fin2,
              d_q, d_kv, d_out,
              ra0, ra1, rb0, rb1, rc, rd0, rd1, re0, re1, rf0, rf1,
              ta0, ta1, tb0, tb1, tc0, tc1, td0, td1, te0, te1, tf0, tf1,
              qa0, qa1, qb0, qb1, qc0, qc1, qd0, qd1, qe0, qe1, qf0, qf1,
              s_gate, s_up, s_q, s_kv, s_down, s_out, ssem, rsem, lsem, isem, osem):
    gains, wq, wk, wv, w_gate, w_up, dh, x_ref, h, cos, sin, wqkv, wout, qp, kv, o, lse = ins
    out, gt, gain_out, q_out, k_out, v_out, wo_out, gate_out, up_out, down_out = vals
    z, c, x, y = (lax.axis_index(a) for a in ALL)
    peers = [to for _, to in tp_peers(c, x)]
    for axis, q in (("y", y), ("z", z)):
        peers += [{axis: lax.rem(q + k, 4)} for k in (1, 2, 3)]
    first = (12, 15, 13, 14, 16, 9, 10)
    order = first + tuple(i for i in range(17) if i not in first)
    loaded = fetch([(ins_from[i], ins[i]) for i in order], isem)
    saved = []

    def give(i):
        cp = pltpu.make_async_copy(vals[i], outs[i], osem.at[i])
        cp.start()
        saved.append(cp)

    entry(peers, (z != x, {"z": x, "x": z}))
    w = Mail(ssem, rsem)
    ag = gather8(w, da, dav)
    pump([ag])
    loads = [pltpu.make_async_copy(a, b, lsem.at[i]) for i, (a, b) in enumerate(
        ((da, dav.at[c, x]), (s2, s2v), (n1g, n1v), (r1_down, rc)))]
    for cp in loads:
        cp.start()
    jobs_down = [
        row_job(w, g_down, rc.at[0], tc0, qc0, s_down, 0, z, y, lsem.at[7], loads[3]),
        row_job(w, g_down, rc.at[1], tc1, qc1, s_down, 1, z, y, lsem.at[8], loads[3]),
    ]
    jobs = [
        col_job(w, g_gate, ra0, ta0, qa0, s_gate, 0, z, y, lsem.at[4]),
        col_job(w, g_gate, ra1, ta1, qa1, s_gate, 1, z, y, lsem.at[5]),
        col_job(w, g_up, rb0, tb0, qb0, s_up, 0, z, y, lsem.at[6]),
        col_job(w, g_up, rb1, tb1, qb1, s_up, 1, z, y, lsem.at[9]),
    ]
    pump(jobs_down)
    pump(jobs)
    pump([ag])
    loads[0].wait()
    pump([ag])
    pump([ag])
    pump([ag])
    pump([ag])
    loads[1].wait()
    loads[3].wait()
    tail2 = ring_tail(w, s2v, hop2, fin2)
    pump([tail2])
    pump([ag])

    for cp in loaded:
        cp.wait()
    ow = wout[...].reshape(256, 2048)
    for g in range(2):
        dv = dott(dav[g].reshape(512, 2048), ow).astype(BF).astype(F32)
        ov = o[g].astype(F32)
        for t in range(2):
            v = dv[:, 128 * t: 128 * t + 128]
            pr = v * ov[:, 128 * t: 128 * t + 128]
            low = lanes(v.shape) < 64
            for b, head in enumerate((pltpu.roll(v, 64, 1), v)):
                rows = pl.ds(128 * (2 * t + b), 128)
                do4[g, :, rows, :] = jnp.where(low, 0.0, head).astype(BF).reshape(4, 128, 128)
                total = jnp.sum(jnp.where(low == (b == 0), pr, 0.0), axis=1, keepdims=True)
                total = jnp.broadcast_to(total, (512, 128)).T
                for j in range(4):
                    delta[g, pl.ds(j, 1), rows] = total[0:1, 128 * j: 128 * j + 128]

    g0, g1 = 1 - c, c
    waits = {}
    for no, g in enumerate((g0, g1)):
        kvt[...] = kv[g].reshape(2048, 128).T
        acc[...] = jnp.zeros_like(acc)
        for j in range(4):
            qj, doj = qp[g, j], do4[g, j]
            lse_row, delta_row = lse[g, pl.ds(j, 1), :], delta[g, pl.ds(j, 1), :]
            col = lanes((1, 512))
            place = (4 * j + y) * 128 + lax.rem(col, 128)
            c1, c2 = lens[g, 0], lens[g, 0] + lens[g, 1]
            start = jnp.where(place >= c2, c2, jnp.where(place >= c1, c1, 0))
            dqt[...] = jnp.zeros_like(dqt)

            @pl.loop(0, j + 1)
            def _(b):
                keys = kv[g, b].reshape(512, 128)
                at = 512 * b + lax.broadcasted_iota(jnp.int32, (512, 512), 0)
                ok = (at >= start) & (at <= place)
                pt = jnp.where(ok, jnp.exp(dott(keys, qj) - lse_row), 0.0)
                ds = (pt * (dott(keys, doj) - delta_row)).astype(BF)
                acc[b] += dot(ds, qj) + dot(pt.astype(BF), doj)
                dqt[...] += dot(kvt[:, pl.ds(pl.multiple_of(512 * b, 512), 512)], ds)

            dq = dqt[...].T
            rows = pl.ds(128 * j, 128)
            cs, sn = cos[g, rows, :], sin[g, rows, :]
            for t in range(2):
                v = pair_heads(dq[256 * t: 256 * t + 128], dq[256 * t + 128: 256 * t + 256], True) * (HD ** -0.5)
                dqkv[g, rows, 128 * t: 128 * t + 128] = (v * cs - swap_halves(v) * sn).astype(BF)
            if no == 0 and j == 2:
                pump([tail2])
        dkv_s[no] = acc[...].astype(BF).reshape(4, 4, 128, 128)
        waits[no] = others(w, y, "y", lambda p, no=no: dkv_s.at[no, :, p], dkv_r.at[no])
        if no == 0:
            pump(jobs_down)
            pump(jobs)
    pump(jobs)
    ends = [hand_out(w, s_gate, f_gate, c, x), hand_out(w, s_up, f_up, c, x)]
    pump(ends)
    pump([tail2])
    loads[2].wait()
    dv = dqkv[:, :, 0:256].reshape(1024, 256)

    @pl.loop(0, 8)
    def _(i):
        cols = pl.ds(pl.multiple_of(256 * i, 256), 256)
        d_q[i // 2, i % 2] = dot(n1v[:, :, :, cols].reshape(1024, 256).T, dv).astype(BF).reshape(4, 4, 16, 256)

    jobs_q = [
        col_job(w, d_q, re0, te0, qe0, s_q, 0, z, y, lsem.at[12]),
        col_job(w, d_q, re1, te1, qe1, s_q, 1, z, y, lsem.at[13]),
    ]
    pump(jobs_q)
    ot = o[...].reshape(1024, 256).T

    @pl.loop(0, 8)
    def _(i):
        cols = pl.ds(pl.multiple_of(256 * i, 256), 256)
        d_out[:, :, :, cols] = dot(ot, dav[:, :, :, cols].reshape(1024, 256)).astype(BF).reshape(4, 4, 16, 256)

    jobs_out = [
        row_job(w, d_out, rd0, td0, qd0, s_out, 0, z, y, lsem.at[10]),
        row_job(w, d_out, rd1, td1, qd1, s_out, 1, z, y, lsem.at[11]),
    ]
    pump(jobs_out)

    state = {}
    for no, g in enumerate((g0, g1)):
        for a in waits[no]:
            w.got(*a)
        for j in range(4):
            rows = pl.ds(128 * j, 128)
            v = dkv_s[no, j, y].astype(F32)
            for k in range(3):
                v += dkv_r[no, k, j].astype(F32)
            turned = v * cos[g, rows, :] - swap_halves(v) * sin[g, rows, :]
            dqkv[g, rows, 256:384] = jnp.where(lanes(v.shape) < 64, turned, v).astype(BF)

        @pl.loop(0, 8)
        def _(i):
            wt = wqkv[i // 2, i % 2].reshape(256, 384)
            p4[g, :, :, pl.ds(pl.multiple_of(256 * i, 256), 256)] = dott(dqkv[g], wt).astype(BF).reshape(4, 128, 256)

        if no == 0:
            scatter8_core(w, p4, core_r, state)
    rs = scatter8_ring(w, p4, core_r, hop, fin, state)
    pump([rs])
    pump([rs])
    dv = dqkv[:, :, 256:384].reshape(1024, 128)

    @pl.loop(0, 8)
    def _(i):
        cols = pl.ds(pl.multiple_of(256 * i, 256), 256)
        d_kv[i // 2, i % 2] = dot(n1v[:, :, :, cols].reshape(1024, 256).T, dv).astype(BF).reshape(4, 4, 16, 128)

    jobs_kv = [
        col_job(w, d_kv, rf0, tf0, qf0, s_kv, 0, z, y, lsem.at[14]),
        col_job(w, d_kv, rf1, tf1, qf1, s_kv, 1, z, y, lsem.at[15]),
    ]
    pump(jobs_kv)

    @pl.loop(0, 8)
    def _(i):
        rows = pl.ds(pl.multiple_of(i * 16, 16), 16)
        v = h[rows, :] + s2v[x, rows, :].astype(F32) + fin2[0, rows, :].astype(F32) + fin2[1, rows, :].astype(F32)
        out[rows, :] = v.astype(BF)

    give(0)

    pump([rs])
    pump(jobs_out)
    pump(jobs_q)
    pump(jobs_kv)
    pump(jobs_out)
    more = [transpose_zx(w, s_out, lambda zz: f_out, z, x, lsem.at[17])]
    pump(more)
    pump(jobs_q)
    pump(jobs_kv)
    more += [hand_out(w, s_q, f_q, c, x), hand_out(w, s_kv, f_kv, c, x)]
    pump(more[1:])
    pump(jobs_down)
    down_out[...] = s_down[0:44, :].astype(F32)
    give(9)
    pump(ends)
    gain1, gain2 = gains[0], gains[1]
    total = jnp.zeros((16, 128), F32)
    for f, wt, res in ((f_gate, w_gate, gate_out), (f_up, w_up, up_out)):
        for t in range(44):
            tile = None
            for r, move in collect_moves(t):
                piece = take_lanes(lambda a: f[r, :, 128 * a: 128 * a + 128].astype(F32), [move])
                tile = piece if tile is None else tile + piece
            cols = slice(128 * t, 128 * t + 128)
            total += tile * wt[:, cols].astype(F32)
            res[:, cols] = tile * gain2
    give(7)
    give(8)
    gain_out[1] = jnp.broadcast_to(jnp.sum(total, axis=1, keepdims=True), (16, 128))
    pump([rs])

    @pl.loop(0, 8)
    def _(i):
        rows = pl.ds(pl.multiple_of(i * 16, 16), 16)
        e = p4[c, x, rows, :].astype(F32) + core_r[3, rows, :].astype(F32)
        e = e + fin[0, rows, :].astype(F32) + fin[1, rows, :].astype(F32)
        v = x_ref[rows, :].astype(F32)
        r = lax.rsqrt(jnp.mean(v * v, axis=1, keepdims=True) + EPS)
        gt[rows, :] = dh[rows, :] + r * e - v * (r * r * r * jnp.mean(e * v, axis=1, keepdims=True))

    give(1)
    pump(more)
    wo_out[...] = f_out[...].astype(F32)
    total = jnp.zeros((16, 128), F32)
    for r in range(8):
        for t in range(2):
            cols = slice(256 * r + 128 * t, 256 * r + 128 * t + 128)
            tile = f_q[r, :, 128 * t: 128 * t + 128].astype(F32)
            total += tile * wq[:, cols].astype(F32)
            q_out[:, cols] = tile * gain1
    heads = [f_kv[2 * a].astype(F32) + f_kv[2 * a + 1].astype(F32) for a in range(4)]
    for t in range(2):
        cols = slice(128 * t, 128 * t + 128)
        for res, wt, lower in ((k_out, wk, True), (v_out, wv, False)):
            tile = pair_heads(heads[2 * t], heads[2 * t + 1], lower)
            total += tile * wt[:, cols].astype(F32)
            res[:, cols] = tile * gain1
    gain_out[0] = jnp.broadcast_to(jnp.sum(total, axis=1, keepdims=True), (16, 128))
    for i in (2, 3, 4, 5, 6):
        give(i)
    w.drain()
    for cp in saved:
        cp.wait()


def backward_attention(
        lens, gains, wq, wk, wv, w_gate, w_up, da, dh, x, h, cos, sin, n1g, wqkv, wout, qp, kv, o, lse,
        s2, g_gate, g_up, g_down, r1_down, cid):
    sds = jax.ShapeDtypeStruct
    hb = pl.BlockSpec(memory_space=ANY)
    outs = [sds((128, 2048), BF)] + [sds(a, F32) for a in (
        (128, 2048), (2, 16, 128), (16, 2048), (16, 256), (16, 256), (16, 2048), (16, 5632), (16, 5632), (44, 2048))]
    b = lambda *s: VMEM(s, BF)
    ns = (768, 768, 256, 128)
    r1 = [b(3, 4, 4, 16, 768)] * 4 + [b(2, 3, 4, 48, 1024)] + [b(3, 4, 16, 1024)] * 2
    r1 += [b(3, 4, 4, 16, 256)] * 2 + [b(3, 4, 4, 16, 128)] * 2
    t1 = [b(4, 4, 16, 768)] * 4 + [b(4, 48, 1024)] * 2 + [b(4, 16, 1024)] * 2
    t1 += [b(4, 4, 16, 256)] * 2 + [b(4, 4, 16, 128)] * 2
    r2 = [b(3, 4, 16, 768)] * 4 + [b(3, 48, 1024)] * 2 + [b(3, 16, 1024)] * 2
    r2 += [b(3, 4, 16, 256)] * 2 + [b(3, 4, 16, 128)] * 2
    return pl.pallas_call(
        m3_kernel,
        out_shape=outs,
        in_specs=[pl.BlockSpec(memory_space=pltpu.SMEM)] + [hb] * 24,
        out_specs=[hb] * 10,
        scratch_shapes=[VMEM(a.shape, a.dtype) for a in outs] + [VMEM(a.shape, a.dtype) for a in (
            gains, wq, wk, wv, w_gate, w_up, dh, x, h, cos, sin, wqkv, wout, qp, kv, o, lse)] + [
            b(8, 16, 768), b(8, 16, 768), b(8, 16, 256), b(8, 16, 128), b(16, 2048),
            b(2, 4, 128, 2048), b(2, 4, 128, 2048), b(4, 128, 2048), b(2, 4, 512, 128), VMEM((2, 4, 512), F32),
            VMEM((4, 512, 128), F32), b(128, 2048), VMEM((128, 512), F32), b(2, 4, 4, 128, 128),
            b(2, 3, 4, 128, 128), b(2, 512, 384), b(2, 4, 128, 2048), b(4, 128, 2048), b(2, 64, 2048),
            b(2, 128, 2048), b(2, 64, 2048), b(2, 128, 2048),
            b(4, 2, 4, 4, 16, 256), b(4, 2, 4, 4, 16, 128), b(4, 4, 16, 2048),
        ] + r1 + t1 + r2 + [
            b(2, 4, 16, 768), b(2, 4, 16, 768), b(2, 4, 16, 256), b(2, 4, 16, 128), b(48, 2048), b(16, 2048),
            pltpu.SemaphoreType.DMA((150,)), pltpu.SemaphoreType.DMA((150,)), pltpu.SemaphoreType.DMA((18,)),
            pltpu.SemaphoreType.DMA((17,)), pltpu.SemaphoreType.DMA((10,)),
        ],
        compiler_params=comm_params(cid, 63),
        name="backward_attention",
    )(lens, gains, wq, wk, wv, w_gate, w_up, da, dh, x, h, cos, sin, n1g, wqkv, wout, qp, kv, o, lse, s2, g_gate, g_up, g_down, r1_down)


def copy_kernel(n, *refs):
    ins, outs, held, isem, osem = refs[:n], refs[n:2 * n], refs[2 * n:3 * n], refs[-2], refs[-1]
    loads = fetch(list(zip(ins, held)), isem)
    stores = [pltpu.make_async_copy(held[i], outs[i], osem.at[i]) for i in range(n)]
    for i in range(n):
        loads[i].wait()
        stores[i].start()
    for cp in stores:
        cp.wait()


def copied(arrays):
    hb = pl.BlockSpec(memory_space=ANY)
    return pl.pallas_call(
        functools.partial(copy_kernel, len(arrays)),
        out_shape=[jax.ShapeDtypeStruct(a.shape, a.dtype) for a in arrays],
        in_specs=[hb] * len(arrays),
        out_specs=[hb] * len(arrays),
        scratch_shapes=[VMEM(a.shape, a.dtype) for a in arrays] + [pltpu.SemaphoreType.DMA((len(arrays),))] * 2,
        name="results",
    )(*arrays)


def local(tokens, lengths, attn_gain, w_query, w_key, w_value, w_out, mlp_gain, w_gate, w_up, w_down, cotangent):
    lens = lax.all_gather(lengths, "core", axis=0, tiled=True)
    inputs = tokens.astype(F32)
    n1 = (inputs * lax.rsqrt(jnp.mean(inputs * inputs, axis=1, keepdims=True) + EPS)).astype(BF)
    gains = jnp.broadcast_to(jnp.stack([attn_gain, mlp_gain]).astype(F32)[..., None], (2, 16, 128))
    h, n1g, qp, kv, o, lse, wqkv, wout, cos, sin, dh, da, s2, g_gate, g_up, g_down, r1_down = forward_layer(
        lens, gains, tokens, n1, cotangent, w_query, w_key, w_value, w_out, w_gate, w_up, w_down, 1)
    col = (4, 2, 4, 4, 16, 768)
    output, grad_tokens, gain, g_q, g_k, g_v, g_o, g_gate, g_up, g_down = backward_attention(
        lens, gains, w_query, w_key, w_value, w_gate, w_up, da, dh, tokens, h, cos, sin, n1g, wqkv, wout,
        qp, kv, o, lse, s2, g_gate.reshape(col), g_up.reshape(col), g_down, r1_down, 2)
    output, grad_tokens, g_q, g_k, g_v, g_o, g_gate, g_up, g_down = copied(
        (output, grad_tokens, g_q, g_k, g_v, g_o, g_gate, g_up, g_down))
    return (output, grad_tokens, gain[0, :, 0], g_q, g_k, g_v, g_o, gain[1, :, 0], g_gate, g_up, g_down)


def solution(mesh):
    fine = Mesh(mesh.devices.reshape(4, 2, 4, 4), ALL)
    rows, flat = P(ALL, None), P(ALL)
    in_specs = (rows, P(("z", "core"), None), flat, rows, rows, rows, rows, flat, rows, rows, rows, rows)
    out_specs = (rows, rows, flat, rows, rows, rows, rows, flat, rows, rows, rows)
    return jax.shard_map(local, mesh=fine, in_specs=in_specs, out_specs=out_specs, check_vma=False)
```
